32 devices in a mesh: dp: 8 (over z, y), seq: 4 (over x, core).
Axes of the slice: x: 2, y: 2, z: 4, core: 2. Of those that a mesh axis runs over, the one named last changes fastest.
Arguments:
- block_input: bfloat16 [16384, 768], P(('dp', 'seq')), may hold values from -6 to 6
- teacher: bfloat16 [16384, 768], P(('dp', 'seq')), may hold values from -6 to 6
- prev_logits: float32 [16384, 12], P(('dp', 'seq')), may hold values from -3 to 3
- valid_mask: int32 [16384], P(('dp', 'seq')), may hold values from 0 to 1, as said below
- segments: int32 [16384], P(('dp', 'seq')), may hold values from 0 to 256, as said below
- routes: int32 [16384, 2], P(('dp', 'seq')), may hold values from 0 to 11, all different within a row; in each aligned block of 512 rows (0 to 511, 512 to 1023, ...) at most 160 rows name the same one
- input_proj: bfloat16 [768, 2304], P(('dp', 'seq')), may hold values from -0.21875 to 0.21875
- output_proj: bfloat16 [768, 768], P(('dp', 'seq')), may hold values from -0.875 to 0.875
- attention_gain: bfloat16 [768], P(('dp', 'seq')), may hold values from 0.5 to 1.5
- mixture_gain: bfloat16 [768], P(('dp', 'seq')), may hold values from 0.5 to 1.5
- router: bfloat16 [768, 12], P(('dp', 'seq')), may hold values from -0.15625 to 0.15625
- const_mix: bfloat16 [768, 4], P(('dp', 'seq')), may hold values from -0.21875 to 0.21875
- const_vectors: bfloat16 [2, 768], P(None, ('dp', 'seq')), may hold values from -5 to 5
- expert_gate: bfloat16 [8, 768, 2048], P('seq', 'dp'), may hold values from -0.21875 to 0.21875
- expert_up: bfloat16 [8, 768, 2048], P('seq', 'dp'), may hold values from -0.21875 to 0.21875
- expert_down: bfloat16 [8, 2048, 768], P('seq', 'dp'), may hold values from -0.25 to 0.25
Outputs:
- block_output: bfloat16 [16384, 768], P(('dp', 'seq'))
- mean_loss: float32 [], replicated
- grad_input: float32 [16384, 768], P(('dp', 'seq'))
- grad_input_proj: float32 [768, 2304], P(('dp', 'seq'))
- grad_output_proj: float32 [768, 768], P(('dp', 'seq'))
- grad_attention_gain: float32 [768], P(('dp', 'seq'))
- grad_mixture_gain: float32 [768], P(('dp', 'seq'))
- grad_router: float32 [768, 12], P(('dp', 'seq'))
- grad_const_mix: float32 [768, 4], P(('dp', 'seq'))
- grad_const_vectors: float32 [2, 768], P(None, ('dp', 'seq'))
- grad_expert_gate: float32 [8, 768, 2048], P('seq', 'dp')
- grad_expert_up: float32 [8, 768, 2048], P('seq', 'dp')
- grad_expert_down: float32 [8, 2048, 768], P('seq', 'dp')
The draws below stay inside these ranges and needn't reach their ends.
Inputs may be any that keep to these rules, and one draw needn't show every extreme that they name: `valid_mask`: each sequence of 2048 tokens is valid on a leading run of more than 1536 tokens and pad after it. `segments`: never falling within a sequence, starting at 0; one document of each sequence begins within its first 256 tokens and runs to the end of its valid tokens; trailing pad, where there is any, has the number 512 // 2 and every valid token a smaller one. A token's two routes differ; among the 512 rows of one device no expert is chosen by more than 160 rows.
All inputs are finite; a program needn't handle non-finite values.
Results may differ from the reference program's by a relative error of at most 0.0088.
Values may be sent and summed in bfloat16 or wider, within the bound.
No kernel may reach another device: no remote copies, remote signals or barrier semaphores. Data moves between devices by JAX's collectives and lax.ppermute only.
A program may use at most 192 MiB of HBM per device.

```python
import math
import jax
import jax.numpy as jnp
import numpy as np
from jax import lax

D = 768
HEADS = 12
HEAD = 64
FF = 2048
EXPERTS = 8
ROUTES = 12
TOP = 2
TOK_DEV = 512
CAP = 160
SEQ_LEN = 2048
TOKENS = 16384
N_DP = 8
DEVICES = 32


def doc_layout(key):
    key_pad, key_start, key_cuts = jax.random.split(key, 3)
    seq_ids = jnp.arange(N_DP, dtype=jnp.int32)[:, None]
    pad_length = (N_DP - 1 - seq_ids) * (2 * TOK_DEV // 3) // max(N_DP - 1, 1) + jax.random.randint(key_pad, (N_DP, 1), 0, TOK_DEV // 8 + 1)
    doc_start = jax.random.randint(key_start, (N_DP, 1), 1, TOK_DEV // 2)
    positions = jnp.arange(SEQ_LEN, dtype=jnp.int32)[None, :]
    valid_end = SEQ_LEN - pad_length
    cuts = (jax.random.randint(key_cuts, (N_DP, SEQ_LEN), 0, 16) == 0) & (positions > 0) & (positions < doc_start)
    new_doc = cuts | (positions == doc_start)
    running = jnp.cumsum(new_doc.astype(jnp.int32), 1).astype(jnp.int32)
    segment_ids = jnp.where(positions >= valid_end, TOK_DEV // 2, running).astype(jnp.int32)
    valid_ids = (positions < valid_end).astype(jnp.int32)
    return (segment_ids.reshape(-1), valid_ids.reshape(-1))


def draw_segments(key, part):
    return doc_layout(key)[0]


def draw_valid_mask(key, part):
    return doc_layout(key)[1]


def level_of(stream_key, extent, cuts, least, high):
    factor_of = 1.0
    for position, shards_of in cuts:
        steps = jax.random.uniform(jax.random.fold_in(jax.random.fold_in(stream_key, 6), position), (shards_of,), jnp.float32, least / len(cuts), high / len(cuts))
        factor_of = factor_of * jnp.repeat(jnp.exp(steps), extent[position] // shards_of).reshape((-1,) + (1,) * (len(extent) - 1 - position))
    return factor_of


def routed_block(own_key, own, number, rows, count, top, limit, slope):
    order = jax.random.permutation(own_key, count)
    crowded, ordinary = load_shares(count, rows * top, limit, slope, True), load_shares(count, rows * top, limit, slope, False)
    places = jnp.arange(count)

    def named(tallies, offset_by):
        used = int((tallies > 0).sum())
        fixed = max(1, used // 4)
        moved = fixed + (places - fixed + offset_by * (used - fixed)) % max(1, count - fixed)
        return jnp.zeros((count,), jnp.int32).at[order[jnp.where(places < fixed, places, moved)]].set(jnp.asarray(tallies, jnp.int32))

    tallies = jnp.where(number % 4 == 0, named(crowded, number // 4), named(ordinary, number - number // 4 - 1))
    mixed = jax.random.permutation(jax.random.fold_in(own, 3), count)
    donor, taker = mixed[0:count // 2 * 2:2], mixed[1:count // 2 * 2:2]
    room = jnp.minimum(tallies[donor] - 1, limit - tallies[taker]) // 2
    room = jnp.where((donor == order[0]) | (taker == order[0]) | (tallies[taker] == 0), 0, jnp.maximum(room, 0))
    moved = jax.random.randint(jax.random.fold_in(own, 4), (count // 2,), 0, 1 << 20) % (room + 1)
    tallies = tallies.at[donor].add(-moved).at[taker].add(moved)
    labels = jnp.searchsorted(jnp.cumsum(tallies), jnp.arange(rows * top), side="right").astype(jnp.int32)
    table = labels.reshape(top, rows).T
    table = table[jax.random.permutation(jax.random.fold_in(own, 1), rows)]
    offset_by = jax.random.randint(jax.random.fold_in(own, 2), (rows, 1), 0, top)
    return jnp.take_along_axis(table, (jnp.arange(top)[None, :] + offset_by) % top, axis=1)


def load_shares(number_of, total, limit, lean, full):
    loads = [(1 << 20) // math.isqrt(grade ** lean) + 1 for grade in range(1, number_of + 1)]
    largest = limit if full else min(limit, max(-(-total // number_of), total * loads[0] // sum(loads)))
    least = 1 if total - largest >= number_of - 1 else 0
    given, spare = [largest] + [least] * (number_of - 1), total - largest - least * (number_of - 1)
    while spare > 0:
        movable = [i for i in range(1, number_of) if given[i] < largest] or [i for i in range(1, number_of) if given[i] < limit]
        pool, left = sum([loads[i] for i in movable]), spare
        for i in movable:
            extra = min(limit - given[i], max(1, left * loads[i] // pool), spare)
            given[i] = given[i] + extra
            spare = spare - extra
    return np.array(given)


def scatter_about(rng, dims, width, bound, cuts=(), kind=jnp.bfloat16):
    loudness = level_of(rng, dims, cuts, -0.22, 0.18) if cuts else 1.0
    values = jax.random.normal(rng, dims, jnp.float32) * width * loudness
    return jnp.minimum(jnp.maximum(values, -bound), bound).astype(kind)


def setup_inputs(seed: int = 0) -> dict:
    streams_of = jax.random.split(jax.random.key(seed), 17)
    block_input = scatter_about(streams_of[0], (TOKENS, D), 1.0, 6.0, ((0, 32),))
    teacher = scatter_about(streams_of[1], (TOKENS, D), 1.0, 6.0, ((0, 32),))
    prev_logits = scatter_about(streams_of[2], (TOKENS, ROUTES), 0.5, 3.0, ((0, 32),), jnp.float32)
    valid_mask = draw_valid_mask(jax.random.fold_in(streams_of[16], 71), 0)
    segments = draw_segments(jax.random.fold_in(streams_of[16], 71), 0)
    routes_keys = jax.random.split(jax.random.fold_in(streams_of[5], 1), TOKENS // TOK_DEV)
    routes_turns = jax.random.permutation(jax.random.fold_in(streams_of[5], 3), TOKENS // TOK_DEV)
    routes = jax.vmap(lambda own, number: routed_block(jax.random.fold_in(streams_of[5], 2), own, number, TOK_DEV, ROUTES, TOP, CAP, 1))(routes_keys, routes_turns).reshape((TOKENS, TOP))
    input_proj = scatter_about(streams_of[6], (D, 3 * D), D ** -0.5, 0.21875, ((0, 32),))
    output_proj = scatter_about(streams_of[7], (D, D), (D // 16) ** -0.5, 0.875, ((0, 32),))
    attention_gain = jnp.clip(1.0 + 0.1 * jax.random.normal(streams_of[8], (D,), jnp.float32), 0.5, 1.5).astype(jnp.bfloat16)
    mixture_gain = jnp.clip(1.0 + 0.1 * jax.random.normal(streams_of[9], (D,), jnp.float32), 0.5, 1.5).astype(jnp.bfloat16)
    router = scatter_about(streams_of[10], (D, ROUTES), (2 * D) ** -0.5, 0.15625, ((0, 32),))
    const_mix = scatter_about(streams_of[11], (D, 4), D ** -0.5, 0.21875, ((0, 32),))
    const_vectors = scatter_about(streams_of[12], (2, D), 1.0, 5.0, ((1, 32),))
    expert_gate = scatter_about(streams_of[13], (EXPERTS, D, FF), D ** -0.5, 0.21875, ((0, 4), (1, 8)))
    expert_up = scatter_about(streams_of[14], (EXPERTS, D, FF), D ** -0.5, 0.21875, ((0, 4), (1, 8)))
    expert_down = scatter_about(streams_of[15], (EXPERTS, FF, D), (FF // 4) ** -0.5, 0.25, ((0, 4), (1, 8)))
    return {"block_input": block_input, "teacher": teacher, "prev_logits": prev_logits, "valid_mask": valid_mask, "segments": segments, "routes": routes, "input_proj": input_proj, "output_proj": output_proj, "attention_gain": attention_gain, "mixture_gain": mixture_gain, "router": router, "const_mix": const_mix, "const_vectors": const_vectors, "expert_gate": expert_gate, "expert_up": expert_up, "expert_down": expert_down}


exact = lax.Precision.HIGHEST
epsilon = 1e-06
masked_out = -1e+30

@jax.custom_vjp
def low(v):
    return lax.optimization_barrier(v.astype(jnp.bfloat16)).astype(jnp.float32)

@jax.custom_vjp
def low_back(v):
    return v

def low_keep(v):
    return (low(v), None)

def low_pass(kept, grad):
    return (grad,)

def back_keep(v):
    return (v, None)

def back_low(kept, grad):
    return (low(grad),)
low.defvjp(low_keep, low_pass)
low_back.defvjp(back_keep, back_low)

def rms_unit(values):
    return values * lax.rsqrt(lax.optimization_barrier(jnp.mean(values * values, -1, keepdims=True)) + epsilon)

def attend(packed):
    query, keyed, values, seq_segments = packed
    length = query.shape[0]
    raw_scores = low_back(jnp.einsum('qhd,khd->hqk', query, keyed, precision=exact) * HEAD ** (-0.5))
    positions = jnp.arange(length)
    allowed = (seq_segments[None, :] == seq_segments[:, None]) & (positions[None, :] <= positions[:, None])
    scores = jnp.where(allowed[None], raw_scores, masked_out)
    row_max = lax.optimization_barrier(jnp.max(scores, -1, keepdims=True))
    expo = jnp.exp(scores - row_max)
    weights = expo / lax.optimization_barrier(jnp.sum(expo, -1, keepdims=True))
    return jnp.einsum('hqk,khd->qhd', low(weights), values, precision=exact)

def reference(block_input, teacher, prev_logits, valid_mask, segments, routes, input_proj, output_proj, attention_gain, mixture_gain, router, const_mix, const_vectors, expert_gate, expert_up, expert_down):
    params = tuple((item.astype(jnp.float32) for item in (block_input, input_proj, output_proj, attention_gain, mixture_gain, router, const_mix, const_vectors, expert_gate, expert_up, expert_down)))
    target = teacher.astype(jnp.float32)
    valid_f = valid_mask.astype(jnp.float32)
    valid_count = jnp.sum(valid_f)
    max_rows = CAP * DEVICES
    flat_routes = routes.reshape(-1).astype(jnp.int32)
    onehot_e = (flat_routes[:, None] == jnp.arange(EXPERTS, dtype=jnp.int32)[None, :]).astype(jnp.int32)
    slot_rank = lax.optimization_barrier(jnp.sum((jnp.cumsum(onehot_e, 0) - onehot_e) * onehot_e, -1))
    slot_dest = jnp.where(flat_routes < EXPERTS, flat_routes * max_rows + slot_rank, EXPERTS * max_rows).astype(jnp.int32)
    slot_table = jnp.full((EXPERTS * max_rows + 1,), 2 * TOKENS, jnp.int32).at[slot_dest].set(jnp.arange(2 * TOKENS, dtype=jnp.int32))
    slot_table = slot_table[:EXPERTS * max_rows].reshape(EXPERTS, max_rows)

    def objective(inputs, proj_in, proj_out, gain_first, gain_second, router_w, mix_w, vectors, gate_w, up_w, down_w):
        unit_first = rms_unit(inputs)
        normed_first = low(unit_first * gain_first)
        projected = low(low_back(jnp.dot(normed_first, proj_in, precision=exact)))
        query = projected[:, :D].reshape(N_DP, SEQ_LEN, HEADS, HEAD)
        keyed = projected[:, D:2 * D].reshape(N_DP, SEQ_LEN, HEADS, HEAD)
        values = projected[:, 2 * D:].reshape(N_DP, SEQ_LEN, HEADS, HEAD)
        seq_segments = segments.reshape(N_DP, SEQ_LEN)
        attended = lax.map(jax.checkpoint(attend), (query, keyed, values, seq_segments)).reshape(TOKENS, D)
        attended = low(low_back(attended))
        residual_mid = inputs + low_back(jnp.dot(attended, proj_out, precision=exact))
        normed = rms_unit(residual_mid) * gain_second
        logits = jnp.dot(normed, router_w, precision=exact) + prev_logits
        route_probs = jax.nn.softmax(logits, -1)
        picked = jnp.take_along_axis(route_probs, routes, 1)
        gate_weights = picked / lax.optimization_barrier(jnp.sum(picked, -1, keepdims=True))
        onehot = (routes[:, :, None] == jnp.arange(ROUTES, dtype=jnp.int32)[None, None, :]).astype(jnp.float32)
        weights_all = lax.optimization_barrier(jnp.sum(gate_weights[:, :, None] * onehot, 1))
        mix_weights = jax.nn.softmax(jnp.dot(normed, mix_w, precision=exact).reshape(TOKENS, 2, 2), -1)
        const_out = mix_weights[..., 0:1] * normed[:, None, :] + mix_weights[..., 1:2] * vectors[None]
        local_terms = weights_all[:, EXPERTS + 1:EXPERTS + 2] * normed + lax.optimization_barrier(jnp.sum(weights_all[:, EXPERTS + 2:EXPERTS + 4, None] * const_out, 1))
        normed_pad = jnp.concatenate([normed, jnp.zeros((1, D), jnp.float32)], 0)
        gates_pad = jnp.concatenate([gate_weights.reshape(-1), jnp.zeros((1,), jnp.float32)], 0)

        def one_expert(packed):
            first_w, second_w, third_w, slot_ids = packed
            row_input = low(low_back(normed_pad[slot_ids // 2]))
            gate_part = low_back(jnp.dot(row_input, first_w, precision=exact))
            up_part = low_back(jnp.dot(row_input, second_w, precision=exact))
            hidden = low(jax.nn.silu(gate_part) * up_part)
            result = low(low_back(jnp.dot(hidden, third_w, precision=exact)))
            return result * gates_pad[slot_ids][:, None]
        contrib = lax.map(jax.checkpoint(one_expert), (gate_w, up_w, down_w, slot_table))
        expert_sum = jnp.zeros((TOKENS + 1, D), jnp.float32).at[(slot_table // 2).reshape(-1)].add(contrib.reshape(-1, D))[:TOKENS]
        full_output = residual_mid + local_terms + expert_sum
        differ = full_output - target
        total = TOKENS / valid_count * 0.5 * jnp.sum(valid_f[:, None] * differ * differ)
        return (total, full_output)
    total, pullback, full_output = jax.vjp(objective, *params, has_aux=True)
    gradients = pullback(jnp.ones_like(total))
    mean_loss = total / (TOKENS * D)
    return (full_output.astype(jnp.bfloat16), mean_loss, gradients[0], gradients[1], gradients[2], gradients[3], gradients[4], gradients[5], gradients[6], gradients[7], gradients[8], gradients[9], gradients[10])
```

```python
import jax
import jax.numpy as jnp
import numpy as np
from jax import lax
from jax.sharding import Mesh, PartitionSpec as P

HEAD = 64
EXPERTS = 8
ROUTES = 12
CAP = 160

ALL = ("do", "di", "seq")
PLANE = ("di", "seq")

exact = lax.Precision.HIGHEST
epsilon = 1e-06
masked_out = -1e30
bf16 = jnp.bfloat16
f32 = jnp.float32


def rms_scale(values):
    return lax.rsqrt(jnp.mean(values * values, -1, keepdims=True) + epsilon)


def dot_rows(left, right, precision=None):
    return lax.dot_general(
        left,
        right,
        (((0,), (0,)), ((), ())),
        preferred_element_type=jnp.float32,
        precision=precision,
    )


def dot_last(left, right, precision=None):
    return lax.dot_general(
        left,
        right,
        (((1,), (1,)), ((), ())),
        preferred_element_type=jnp.float32,
        precision=precision,
    )


def exchange(blocks, axes):
    return lax.all_to_all(blocks, axes, split_axis=0, concat_axis=0, tiled=True)


def to_all(block, count):
    return exchange(jnp.broadcast_to(block[None], (count,) + block.shape), ALL)


def gather_seq(block, size):
    held = block[None]
    step = size // 2
    while step:
        pairs = [(i, i ^ step) for i in range(size)]
        held = jnp.concatenate([held, lax.ppermute(held, "seq", pairs)], 0)
        step //= 2
    order = [0]
    step = size // 2
    while step:
        order = order + [k ^ step for k in order]
        step //= 2
    return held, order


def body(
    block_input,
    teacher,
    prev_logits,
    valid_mask,
    segments,
    routes,
    input_proj,
    output_proj,
    attention_gain,
    mixture_gain,
    router,
    const_mix,
    const_vectors,
    expert_gate,
    expert_up,
    expert_down,
):
    n_out, n_in, n_seq = (lax.axis_size(a) for a in ALL)
    n_all = n_out * n_in * n_seq
    tokens_here, features = block_input.shape
    rows_here = input_proj.shape[0]
    wide = features // n_seq
    seq_id = lax.axis_index("seq")

    def expert_weight(shard):
        mine = exchange(shard, "di")
        whole = lax.all_gather(mine, "do", axis=0, tiled=False)
        return whole.reshape(-1, shard.shape[2])

    gate_full = expert_weight(expert_gate)
    up_full = expert_weight(expert_up)
    down_full = expert_weight(expert_down)

    own_cols = (
        input_proj.reshape(rows_here, 3, n_seq, wide)
        .transpose(2, 0, 1, 3)
        .reshape(n_seq, rows_here, 3 * wide)
    )
    count_here = jnp.sum(valid_mask)
    count_cols = jnp.stack([count_here // 32, count_here % 32]).astype(bf16)
    small = jnp.concatenate(
        [
            attention_gain[:, None],
            mixture_gain[:, None],
            router,
            const_mix,
            const_vectors.T,
            jnp.broadcast_to(count_cols[None], (rows_here, 2)),
        ],
        1,
    )
    pad = -(3 * wide + small.shape[1]) % 128
    packed = jnp.concatenate(
        [
            own_cols,
            jnp.broadcast_to(small[None], (n_seq,) + small.shape),
            jnp.zeros((n_seq, rows_here, pad), bf16),
        ],
        2,
    )
    packed = jnp.broadcast_to(packed[None], (n_out * n_in,) + packed.shape).reshape(
        n_all, rows_here, -1
    )
    got = exchange(packed, ALL)
    counts = got[:, 0, 3 * wide + 20 : 3 * wide + 22].astype(f32)
    valid_count = jnp.sum(counts[:, 0]) * 32.0 + jnp.sum(counts[:, 1])
    got = got.reshape(features, -1)
    own_in = got[:, : 3 * wide]
    small_all = got[:, 3 * wide : 3 * wide + 20].astype(f32)
    gain_first = small_all[:, 0]
    gain_mid = small_all[:, 1]
    router_f = small_all[:, 2:14]
    mix_f = small_all[:, 14:18]
    vectors_f = small_all[:, 18:20].T
    full_out = to_all(output_proj, n_all).reshape(features, features)

    seg_row = jnp.pad(segments.astype(bf16), (0, features * 2 - tokens_here)).reshape(2, features)
    with_seg = jnp.concatenate(
        [block_input, jnp.pad(seg_row, ((0, 14), (0, 0)))], 0
    )
    held, order = gather_seq(with_seg, n_seq)
    where = [order.index(j) for j in range(n_seq)]
    chosen = jnp.array(where, jnp.int32)[jnp.arange(n_seq) ^ seq_id]
    held = held[chosen]
    seq_inputs = held[:, :tokens_here].reshape(-1, features).astype(f32)
    seq_segments = (
        held[:, tokens_here : tokens_here + 2]
        .reshape(n_seq, 2 * features)[:, :tokens_here]
        .reshape(-1)
    )

    inputs_f = block_input.astype(f32)
    scale_seq = rms_scale(seq_inputs)
    unit_seq = seq_inputs * scale_seq
    normed_first = (unit_seq * gain_first).astype(bf16)
    projected = jnp.dot(normed_first, own_in, preferred_element_type=f32).astype(bf16)
    length = n_seq * tokens_here
    heads_here = wide // HEAD
    query_three, key_three, value_three = (
        projected[:, k * wide : (k + 1) * wide].reshape(length, heads_here, HEAD) for k in range(3)
    )
    block_rows = min(512, length)
    block_count = length // block_rows
    scaling = HEAD ** (-0.5)
    key_positions = jnp.arange(length)

    def block_scores(block_id):
        first_row = block_id * block_rows
        query_block = lax.dynamic_slice_in_dim(query_three, first_row, block_rows, 0)
        segment_block = lax.dynamic_slice_in_dim(seq_segments, first_row, block_rows, 0)
        scores = (
            jnp.einsum("qhd,khd->hqk", query_block, key_three, preferred_element_type=jnp.float32)
            * scaling
        )
        allowed = (seq_segments[None, :] == segment_block[:, None]) & (
            key_positions[None, :] <= first_row + jnp.arange(block_rows)[:, None]
        )
        return (query_block, jnp.where(allowed[None], scores, masked_out))

    def forward_block(block_id):
        query_block, scores = block_scores(block_id)
        row_max = jnp.max(scores, -1, keepdims=True)
        expo = jnp.exp(scores - row_max)
        row_total = jnp.sum(expo, -1, keepdims=True)
        weights = (expo / row_total).astype(jnp.bfloat16)
        attended = jnp.einsum(
            "hqk,khd->qhd", weights, value_three, preferred_element_type=jnp.float32
        )
        return (attended.astype(jnp.bfloat16), (row_max + jnp.log(row_total))[..., 0])

    attended_blocks, log_totals = lax.map(forward_block, jnp.arange(block_count))
    attended_heads = attended_blocks.reshape(n_seq, tokens_here, wide)
    attended_tok = exchange(attended_heads, "seq").transpose(1, 0, 2).reshape(tokens_here, features)

    residual_mid = inputs_f + jnp.dot(attended_tok, full_out, preferred_element_type=jnp.float32)
    scale_second = rms_scale(residual_mid)
    unit_second = residual_mid * scale_second
    normed = unit_second * gain_mid
    route_probs = jax.nn.softmax(jnp.dot(normed, router_f, precision=exact) + prev_logits, -1)
    onehot = (routes[:, :, None] == jnp.arange(ROUTES, dtype=jnp.int32)[None, None, :]).astype(
        jnp.float32
    )
    picked = jnp.sum(onehot * route_probs[:, None, :], -1)
    picked_sum = jnp.sum(picked, -1, keepdims=True)
    gate_weights = picked / picked_sum
    weights_all = jnp.sum(gate_weights[:, :, None] * onehot, 1)
    mix_weights = jax.nn.softmax(
        jnp.dot(normed, mix_f, precision=exact).reshape(tokens_here, 2, 2), -1
    )
    const_out = mix_weights[..., 0:1] * normed[:, None, :] + mix_weights[..., 1:2] * vectors_f[None]
    copy_weight = weights_all[:, EXPERTS + 1 : EXPERTS + 2]
    const_weight = weights_all[:, EXPERTS + 2 : EXPERTS + 4]
    local_terms = copy_weight * normed + jnp.sum(const_weight[:, :, None] * const_out, 1)

    flat_routes = routes.reshape(-1)
    onehot_e = (flat_routes[:, None] == jnp.arange(EXPERTS, dtype=jnp.int32)[None, :]).astype(
        jnp.int32
    )
    slot_rank = jnp.sum((jnp.cumsum(onehot_e, 0) - onehot_e) * onehot_e, -1)
    host = (flat_routes % n_in) * n_seq + flat_routes // n_in
    slot_dest = jnp.where(flat_routes < EXPERTS, host * CAP + slot_rank, EXPERTS * CAP)
    slots = jnp.arange(EXPERTS * CAP, dtype=jnp.int32)
    place = (slot_dest.reshape(tokens_here, 2)[:, :, None] == slots).astype(bf16)

    def dispatch(rows_zero, rows_one):
        return (
            dot_rows(place[:, 0], rows_zero) + dot_rows(place[:, 1], rows_one)
        ).astype(bf16).reshape(EXPERTS, CAP, features)

    def collect(rows, route):
        return jnp.dot(place[:, route], rows, preferred_element_type=f32)

    normed_low = normed.astype(bf16)
    recv_rows = exchange(dispatch(normed_low, normed_low), PLANE).reshape(-1, features)
    gate_part = jnp.dot(recv_rows, gate_full, preferred_element_type=f32)
    up_part = jnp.dot(recv_rows, up_full, preferred_element_type=f32)
    hidden = (jax.nn.silu(gate_part) * up_part).astype(bf16)
    result_rows = jnp.dot(hidden, down_full, preferred_element_type=f32).astype(bf16)
    back_rows = exchange(result_rows.reshape(EXPERTS, CAP, features), PLANE).reshape(-1, features)
    expert_terms = jnp.stack([collect(back_rows, 0), collect(back_rows, 1)], 1)
    full_output = residual_mid + local_terms + jnp.sum(gate_weights[:, :, None] * expert_terms, 1)
    valid_f = valid_mask.astype(jnp.float32)
    differ = full_output - teacher.astype(jnp.float32)
    squared = jnp.sum(valid_f[:, None] * differ * differ)
    grad_full = valid_f[:, None] * differ * (tokens_here * n_all / valid_count)
    gated = (gate_weights[:, :, None] * grad_full[:, None, :]).astype(bf16)
    grad_recv = exchange(dispatch(gated[:, 0], gated[:, 1]), PLANE).reshape(-1, features)

    def expert_grad(partial):
        low = partial.astype(bf16)
        part = lax.psum_scatter(low, "do", scatter_dimension=0, tiled=True)
        part = part.reshape(n_in, -1, partial.shape[1])
        return exchange(part, "di").astype(f32)

    grad_expert_down = expert_grad(dot_rows(hidden, grad_recv))
    sigmoid_gate = jax.nn.sigmoid(gate_part)
    silu_gate = gate_part * sigmoid_gate
    grad_hidden = dot_last(grad_recv, down_full)
    grad_gate_part = (
        grad_hidden * up_part * sigmoid_gate * (1.0 + gate_part * (1.0 - sigmoid_gate))
    ).astype(bf16)
    grad_up_part = (grad_hidden * silu_gate).astype(bf16)
    grad_rows = (dot_last(grad_gate_part, gate_full) + dot_last(grad_up_part, up_full)).astype(bf16)
    grad_back = exchange(grad_rows.reshape(EXPERTS, CAP, features), PLANE).reshape(-1, features)
    grad_expert_gate = expert_grad(dot_rows(recv_rows, grad_gate_part))
    grad_expert_up = expert_grad(dot_rows(recv_rows, grad_up_part))

    expert_dot = jnp.sum(grad_full[:, None, :] * expert_terms, -1)
    copy_dot = jnp.sum(grad_full * normed, -1)
    const_dot = jnp.sum(grad_full[:, None, :] * const_out, -1)
    grad_gates = (
        expert_dot
        + onehot[:, :, EXPERTS + 1] * copy_dot[:, None]
        + jnp.sum(onehot[:, :, EXPERTS + 2 : EXPERTS + 4] * const_dot[:, None, :], -1)
    )
    grad_picked = (grad_gates - jnp.sum(gate_weights * grad_gates, -1, keepdims=True)) / picked_sum
    grad_probs = jnp.sum(grad_picked[:, :, None] * onehot, 1)
    grad_logits = route_probs * (grad_probs - jnp.sum(route_probs * grad_probs, -1, keepdims=True))
    grad_router = dot_rows(normed, grad_logits, exact)
    grad_const = const_weight[:, :, None] * grad_full[:, None, :]
    grad_mix = jnp.stack(
        [jnp.sum(grad_const * normed[:, None, :], -1), jnp.sum(grad_const * vectors_f[None], -1)],
        -1,
    )
    grad_z = (
        mix_weights * (grad_mix - jnp.sum(mix_weights * grad_mix, -1, keepdims=True))
    ).reshape(tokens_here, 4)
    grad_const_mix = dot_rows(normed, grad_z, exact)
    grad_const_vectors = jnp.sum(mix_weights[..., 1:2] * grad_const, 0)
    grad_normed = copy_weight * grad_full + dot_last(grad_logits, router_f, exact)
    grad_normed = (
        grad_normed
        + jnp.sum(mix_weights[..., 0:1] * grad_const, 1)
        + dot_last(grad_z, mix_f, exact)
    )
    grad_normed = grad_normed + collect(grad_back, 0) + collect(grad_back, 1)
    grad_mixture_gain = jnp.sum(grad_normed * unit_second, 0)
    grad_hat = grad_normed * gain_mid
    grad_mid = grad_full + scale_second * (
        grad_hat - unit_second * jnp.mean(grad_hat * unit_second, -1, keepdims=True)
    )
    grad_branch = grad_mid.astype(bf16)
    grad_output_proj = dot_rows(attended_tok, grad_branch).astype(bf16)
    grad_output_proj = exchange(grad_output_proj.reshape(n_all, rows_here, features), ALL)
    grad_output_proj = jnp.sum(grad_output_proj.astype(f32), 0)
    grad_attended = dot_last(grad_branch, full_out).astype(bf16)
    grad_attended = grad_attended.reshape(tokens_here, n_seq, wide).transpose(1, 0, 2)
    grad_three = exchange(grad_attended, "seq").reshape(length, heads_here, HEAD)

    def backward_block(carry, block_id):
        grad_key, grad_value = carry
        first_row = block_id * block_rows
        query_block, scores = block_scores(block_id)
        probs_block = jnp.exp(scores - log_totals[block_id][..., None])
        grad_block = lax.dynamic_slice_in_dim(grad_three, first_row, block_rows, 0)
        grad_value = grad_value + jnp.einsum(
            "hqk,qhd->khd",
            probs_block.astype(jnp.bfloat16),
            grad_block,
            preferred_element_type=jnp.float32,
        )
        grad_prob = jnp.einsum(
            "qhd,khd->hqk", grad_block, value_three, preferred_element_type=jnp.float32
        )
        inner = jnp.sum(probs_block * grad_prob, -1, keepdims=True)
        grad_scores = (probs_block * (grad_prob - inner)).astype(jnp.bfloat16)
        grad_query = (
            jnp.einsum("hqk,khd->qhd", grad_scores, key_three, preferred_element_type=jnp.float32)
            * scaling
        )
        grad_key = (
            grad_key
            + jnp.einsum(
                "hqk,qhd->khd", grad_scores, query_block, preferred_element_type=jnp.float32
            )
            * scaling
        )
        return ((grad_key, grad_value), grad_query.astype(jnp.bfloat16))

    zeros_heads = jnp.zeros((length, heads_here, HEAD), jnp.float32)
    (grad_key, grad_value), grad_queries = lax.scan(
        backward_block, (zeros_heads, zeros_heads), jnp.arange(block_count)
    )
    grad_projected = jnp.concatenate(
        [
            grad_queries.reshape(length, wide),
            grad_key.astype(bf16).reshape(length, wide),
            grad_value.astype(bf16).reshape(length, wide),
        ],
        1,
    )
    grad_input_proj = dot_rows(normed_first, grad_projected).astype(bf16)
    grad_input_proj = exchange(grad_input_proj.reshape(n_all, rows_here, 3 * wide), ALL)
    grad_input_proj = (
        jnp.sum(
            grad_input_proj.reshape(n_out * n_in, n_seq, rows_here, 3, wide).astype(f32), 0
        )
        .transpose(1, 2, 0, 3)
        .reshape(rows_here, 3 * features)
    )
    partial_first = dot_last(grad_projected, own_in)
    grad_attention_gain = jnp.sum(partial_first * unit_seq, 0)

    held = partial_first.reshape(n_seq, tokens_here, features)[
        jnp.arange(n_seq) ^ seq_id
    ]
    step = 1
    index = list(range(n_seq))
    while step < n_seq:
        pairs = [(i, i ^ step) for i in range(n_seq)]
        keep = [k for k, t in enumerate(index) if not t & step]
        give = [index.index(index[k] ^ step) for k in keep]
        sent = held[np.array(give)].astype(bf16)
        held = held[np.array(keep)] + lax.ppermute(sent, "seq", pairs).astype(f32)
        index = [index[k] for k in keep]
        step *= 2
    grad_normed_first = held[0]

    scale_first = rms_scale(inputs_f)
    unit_first = inputs_f * scale_first
    grad_hat_first = grad_normed_first * gain_first
    grad_input = grad_mid + scale_first * (
        grad_hat_first - unit_first * jnp.mean(grad_hat_first * unit_first, -1, keepdims=True)
    )
    small_grads = jnp.concatenate(
        [
            grad_attention_gain[:, None],
            grad_mixture_gain[:, None],
            grad_router,
            grad_const_mix,
            grad_const_vectors.T,
            jnp.broadcast_to(squared, (features, 1)),
        ],
        1,
    )
    small_grads = jnp.sum(exchange(small_grads.reshape(n_all, rows_here, 21), ALL), 0)
    mean_loss = small_grads[0, 20] / (2.0 * features * valid_count)
    return (
        full_output.astype(bf16),
        mean_loss,
        grad_input,
        grad_input_proj,
        grad_output_proj,
        small_grads[:, 0],
        small_grads[:, 1],
        small_grads[:, 2:14],
        small_grads[:, 14:18],
        small_grads[:, 18:20].T,
        grad_expert_gate,
        grad_expert_up,
        grad_expert_down,
    )


def solution(mesh):
    n_seq = mesh.shape["seq"]
    n_in = EXPERTS // n_seq
    cut = Mesh(mesh.devices.reshape(-1, n_in, n_seq), ALL)
    rows = P(ALL, None)
    line = P(ALL)
    cols = P(None, ALL)
    expert = P("seq", ("do", "di"), None)
    return jax.shard_map(
        body,
        mesh=cut,
        in_specs=(rows, rows, rows, line, line, rows, rows, rows, line, line, rows, rows, cols)
        + (expert,) * 3,
        out_specs=(rows, P(), rows, rows, rows, line, line, rows, rows, cols) + (expert,) * 3,
        check_vma=False,
    )
```

```python
import jax
import jax.numpy as jnp
import numpy as np
from jax import lax
from jax.experimental import pallas as pl
from jax.experimental.pallas import tpu as pltpu
from jax.sharding import Mesh, PartitionSpec as P

HEAD = 64
EXPERTS = 8
ROUTES = 12
CAP = 160
BLK = 256

ALL = ("do", "di", "seq")
PLANE = ("di", "seq")

exact = lax.Precision.HIGHEST
epsilon = 1e-06
masked_out = -1e30
bf16 = jnp.bfloat16
f32 = jnp.float32


def rms_scale(values):
    return lax.rsqrt(jnp.mean(values * values, -1, keepdims=True) + epsilon)


def dot_rows(left, right, precision=None):
    return lax.dot_general(
        left,
        right,
        (((0,), (0,)), ((), ())),
        preferred_element_type=jnp.float32,
        precision=precision,
    )


def dot_last(left, right, precision=None):
    return lax.dot_general(
        left,
        right,
        (((1,), (1,)), ((), ())),
        preferred_element_type=jnp.float32,
        precision=precision,
    )


def nt(a,b): return lax.dot_general(a,b,(((1,),(1,)),((),())),preferred_element_type=f32)
def nn(a,b): return jnp.dot(a,b,preferred_element_type=f32)
def tn(a,b): return lax.dot_general(a,b,(((0,),(0,)),((),())),preferred_element_type=f32)

def fwd_kernel(tbl, held, gain, win, winT, start, normed, att, oT, lse, qn, kn, vn, qT, kT, kbuf, vbuf):
    i=pl.program_id(0)
    wide=win.shape[1]//3
    heads=wide//HEAD
    per=held.shape[1]//BLK
    t=tbl[i//per]
    off=pl.multiple_of((i%per)*BLK,BLK)
    x=held[t,pl.ds(off,BLK),:].astype(f32)
    scale=lax.rsqrt(jnp.mean(x*x,-1,keepdims=True)+epsilon)
    nb=(x*scale*gain[...]).astype(bf16)
    normed[...]=nb
    proj=nn(nb,win[...]).astype(bf16)
    projT=nt(winT[...],nb).astype(bf16)
    qs=projT[:wide]*bf16(HEAD ** -0.5)
    qT[...]=qs
    kT[...]=projT[wide:2*wide]
    vbuf[i]=projT[2*wide:]
    for h in range(heads):
        qn[h]=proj[:,h*HEAD:(h+1)*HEAD]*bf16(HEAD ** -0.5)
        kh=proj[:,wide+h*HEAD:wide+(h+1)*HEAD]
        kn[h]=kh
        kbuf[i,h]=kh
        vn[h]=proj[:,2*wide+h*HEAD:2*wide+(h+1)*HEAD]
    rows=lax.broadcasted_iota(jnp.int32,(BLK,BLK),0)
    cols=lax.broadcasted_iota(jnp.int32,(BLK,BLK),1)
    first=start[...]
    def tile(j,h,mask):
        s=nn(kbuf[j,h],qs[h*HEAD:(h+1)*HEAD])
        return jnp.where(mask,s,masked_out)
    mask=(rows+i*BLK>=first)&(rows<=cols)
    state=[]
    for h in range(heads):
        s=tile(i,h,mask)
        m=jnp.max(s,0,keepdims=True)
        e=jnp.exp(s-m)
        l=jnp.sum(e,0,keepdims=True)
        o=nn(vbuf[i,h*HEAD:(h+1)*HEAD],e.astype(bf16))
        state.append((m,l,o))
    def step(j,state):
        mask=rows+j*BLK>=first
        new=[]
        for h in range(heads):
            m,l,o=state[h]
            s=tile(j,h,mask)
            n=jnp.maximum(m,jnp.max(s,0,keepdims=True))
            a=jnp.exp(m-n)
            e=jnp.exp(s-n)
            l=l*a+jnp.sum(e,0,keepdims=True)
            o=o*a+nn(vbuf[j,h*HEAD:(h+1)*HEAD],e.astype(bf16))
            new.append((n,l,o))
        return tuple(new)
    state=lax.fori_loop(0,i,step,tuple(state))
    for h in range(heads):
        m,l,o=state[h]
        o=o/l
        oT[h*HEAD:(h+1)*HEAD]=o
        lse[h:h+1]=m+jnp.log(l)
    lse[heads:]=jnp.zeros((lse.shape[0]-heads,BLK),f32)
    att[...]=oT[...].T.astype(bf16)

def attend_forward(tbl, held, gain, win, winT, start):
    feat=held.shape[2]
    length=start.shape[1]; wide=win.shape[1]//3; heads=wide//HEAD; nb=length//BLK
    full=lambda shape: pl.BlockSpec(shape,lambda i,*_:(0,)*len(shape))
    tokb=pl.BlockSpec((wide,BLK),lambda i,*_:(0,i))
    headb=pl.BlockSpec((heads,BLK,HEAD),lambda i,*_:(0,i,0))
    S=jax.ShapeDtypeStruct
    return pl.pallas_call(fwd_kernel,
      grid_spec=pltpu.PrefetchScalarGridSpec(num_scalar_prefetch=1,grid=(nb,),
        in_specs=[full(held.shape),full(gain.shape),full(win.shape),full(winT.shape),pl.BlockSpec((1,BLK),lambda i,*_:(0,i))],
        out_specs=[pl.BlockSpec((BLK,feat),lambda i,*_:(i,0)),pl.BlockSpec((BLK,wide),lambda i,*_:(i,0)),tokb,pl.BlockSpec((8,BLK),lambda i,*_:(0,i)),headb,headb,headb,tokb,tokb],
        scratch_shapes=[pltpu.VMEM((nb,heads,BLK,HEAD),bf16),pltpu.VMEM((nb,wide,BLK),bf16)]),
      out_shape=[S((length,feat),bf16),S((length,wide),bf16),S((wide,length),f32),S((8,length),f32),S((heads,length,HEAD),bf16),S((heads,length,HEAD),bf16),S((heads,length,HEAD),bf16),S((wide,length),bf16),S((wide,length),bf16)],
      compiler_params=pltpu.CompilerParams(vmem_limit_bytes=48<<20),
      name="attend_forward")(tbl,held,gain,win,winT,start)

def bwd_kernel(go, oT, lse, qn, kn, vn, qT, kT, start, gq, gk, gv, gT, dq, delta):
    j=pl.program_id(0)
    nb=pl.num_programs(0)
    heads=kn.shape[0]
    rows=lax.broadcasted_iota(jnp.int32,(BLK,BLK),0)
    cols=lax.broadcasted_iota(jnp.int32,(BLK,BLK),1)
    @pl.when(j==0)
    def _():
        dq[...]=jnp.zeros_like(dq)
        for b in range(gT.shape[0]):
            g=go[b*BLK:(b+1)*BLK,:].astype(f32).T
            gT[b]=g.astype(bf16)
            prod=g*oT[:,b*BLK:(b+1)*BLK]
            for h in range(heads):
                delta[b,h:h+1]=jnp.sum(prod[h*HEAD:(h+1)*HEAD],0,keepdims=True)
    def tile(i,accs,mask):
        new=[]
        at=pl.multiple_of(i*BLK,BLK)
        ds_=pl.ds(at,BLK)
        if mask is None:
            mask=rows+j*BLK>=start[:,ds_]
        else:
            mask=mask&(rows+j*BLK>=start[:,ds_])
        gblk=go[ds_,:]
        for h in range(heads):
            dk,dv=accs[h]
            hs=slice(h*HEAD,(h+1)*HEAD)
            s=nn(kn[h],qT[hs,ds_])
            p=jnp.exp(jnp.where(mask,s,masked_out)-lse[h:h+1,ds_])
            g=gblk[:,hs]
            dv=dv+nn(p.astype(bf16),g)
            dp=nn(vn[h],gT[i,hs])
            d=(p*(dp-delta[i,h:h+1])).astype(bf16)
            dk=dk+nn(d,qn[h,ds_])
            dq[i,hs]+=nn(kT[hs],d)
            new.append((dk,dv))
        return tuple(new)
    zero=jnp.zeros((BLK,HEAD),f32)
    accs=tile(j,tuple((zero,zero) for _ in range(heads)),rows<=cols)
    accs=lax.fori_loop(j+1,nb,lambda i,a:tile(i,a,None),accs)
    gk[...]=jnp.concatenate([a[0] for a in accs],1).astype(bf16)
    gv[...]=jnp.concatenate([a[1] for a in accs],1).astype(bf16)
    gq[...]=(dq[j]*HEAD ** -0.5).T.astype(bf16)

def attend_backward(go,oT,lse,qn,kn,vn,qT,kT,start):
    length,wide=go.shape; heads=wide//HEAD; nb=length//BLK
    full=lambda a: pl.BlockSpec(a.shape,lambda i,*_:(0,)*a.ndim)
    headb=pl.BlockSpec((heads,BLK,HEAD),lambda i,*_:(0,i,0))
    tokb=pl.BlockSpec((wide,BLK),lambda i,*_:(0,i))
    rowb=pl.BlockSpec((BLK,wide),lambda i,*_:(i,0))
    S=jax.ShapeDtypeStruct
    return pl.pallas_call(bwd_kernel,grid=(nb,),
      in_specs=[full(go),full(oT),full(lse),full(qn),headb,headb,full(qT),tokb,full(start)],
      out_specs=[rowb]*3,
      out_shape=[S((length,wide),bf16)]*3,
      scratch_shapes=[pltpu.VMEM((nb,wide,BLK),bf16),pltpu.VMEM((nb,wide,BLK),f32),pltpu.VMEM((nb,8,BLK),f32)],
      compiler_params=pltpu.CompilerParams(vmem_limit_bytes=48<<20),
      name="attend_backward")(go,oT,lse,qn,kn,vn,qT,kT,start)


def exchange(blocks, axes):
    return lax.all_to_all(blocks, axes, split_axis=0, concat_axis=0, tiled=True)


def to_all(block, count):
    return exchange(jnp.broadcast_to(block[None], (count,) + block.shape), ALL)


def gather_seq(block, size):
    held = block[None]
    step = size // 2
    while step:
        pairs = [(i, i ^ step) for i in range(size)]
        held = jnp.concatenate([held, lax.ppermute(held, "seq", pairs)], 0)
        step //= 2
    order = [0]
    step = size // 2
    while step:
        order = order + [k ^ step for k in order]
        step //= 2
    return held, order


def body(
    block_input,
    teacher,
    prev_logits,
    valid_mask,
    segments,
    routes,
    input_proj,
    output_proj,
    attention_gain,
    mixture_gain,
    router,
    const_mix,
    const_vectors,
    expert_gate,
    expert_up,
    expert_down,
):
    n_out, n_in, n_seq = (lax.axis_size(a) for a in ALL)
    n_all = n_out * n_in * n_seq
    tokens_here, features = block_input.shape
    rows_here = input_proj.shape[0]
    wide = features // n_seq
    seq_id = lax.axis_index("seq")

    def expert_weight(shard):
        mine = exchange(shard, "di")
        whole = lax.all_gather(mine, "do", axis=0, tiled=False)
        return whole.reshape(-1, shard.shape[2])

    gate_full = expert_weight(expert_gate)
    up_full = expert_weight(expert_up)
    down_full = expert_weight(expert_down)

    own_cols = (
        input_proj.reshape(rows_here, 3, n_seq, wide)
        .transpose(2, 0, 1, 3)
        .reshape(n_seq, rows_here, 3 * wide)
    )
    count_here = jnp.sum(valid_mask)
    count_cols = jnp.stack([count_here // 32, count_here % 32]).astype(bf16)
    small = jnp.concatenate(
        [
            attention_gain[:, None],
            mixture_gain[:, None],
            router,
            const_mix,
            const_vectors.T,
            jnp.broadcast_to(count_cols[None], (rows_here, 2)),
        ],
        1,
    )
    pad = -(3 * wide + small.shape[1]) % 128
    packed = jnp.concatenate(
        [
            own_cols,
            jnp.broadcast_to(small[None], (n_seq,) + small.shape),
            jnp.zeros((n_seq, rows_here, pad), bf16),
        ],
        2,
    )
    packed = jnp.broadcast_to(packed[None], (n_out * n_in,) + packed.shape).reshape(
        n_all, rows_here, -1
    )
    got = exchange(packed, ALL)
    counts = got[:, 0, 3 * wide + 20 : 3 * wide + 22].astype(f32)
    valid_count = jnp.sum(counts[:, 0]) * 32.0 + jnp.sum(counts[:, 1])
    got = got.reshape(features, -1)
    own_in = got[:, : 3 * wide]
    small_all = got[:, 3 * wide : 3 * wide + 20].astype(f32)
    gain_first = small_all[:, 0]
    gain_mid = small_all[:, 1]
    router_f = small_all[:, 2:14]
    mix_f = small_all[:, 14:18]
    vectors_f = small_all[:, 18:20].T
    full_out = to_all(output_proj, n_all).reshape(features, features)

    seg_row = jnp.pad(segments.astype(bf16), (0, features * 2 - tokens_here)).reshape(2, features)
    with_seg = jnp.concatenate(
        [block_input, jnp.pad(seg_row, ((0, 14), (0, 0)))], 0
    )
    held, order = gather_seq(with_seg, n_seq)
    where = [order.index(j) for j in range(n_seq)]
    chosen = jnp.array(where, jnp.int32)[jnp.arange(n_seq) ^ seq_id]
    length = n_seq * tokens_here
    seq_segments = (
        held[:, tokens_here : tokens_here + 2]
        .reshape(n_seq, 2 * features)[:, :tokens_here][chosen]
        .reshape(1, -1)
    )
    positions = jnp.arange(length, dtype=jnp.int32)[None]
    fresh = seq_segments != jnp.pad(seq_segments[:, :-1], ((0, 0), (1, 0)), constant_values=-1)
    start = lax.cummax(jnp.where(fresh, positions, 0), axis=1)

    inputs_f = block_input.astype(f32)
    normed_first, attended, attended_t, log_totals, *heads_saved = attend_forward(
        chosen, held, gain_first[None], own_in, own_in.T, start
    )
    attended_heads = attended.reshape(n_seq, tokens_here, wide)
    attended_tok = exchange(attended_heads, "seq").transpose(1, 0, 2).reshape(tokens_here, features)

    residual_mid = inputs_f + jnp.dot(attended_tok, full_out, preferred_element_type=jnp.float32)
    scale_second = rms_scale(residual_mid)
    unit_second = residual_mid * scale_second
    normed = unit_second * gain_mid
    route_probs = jax.nn.softmax(jnp.dot(normed, router_f, precision=exact) + prev_logits, -1)
    onehot = (routes[:, :, None] == jnp.arange(ROUTES, dtype=jnp.int32)[None, None, :]).astype(
        jnp.float32
    )
    picked = jnp.sum(onehot * route_probs[:, None, :], -1)
    picked_sum = jnp.sum(picked, -1, keepdims=True)
    gate_weights = picked / picked_sum
    weights_all = jnp.sum(gate_weights[:, :, None] * onehot, 1)
    mix_weights = jax.nn.softmax(
        jnp.dot(normed, mix_f, precision=exact).reshape(tokens_here, 2, 2), -1
    )
    const_out = mix_weights[..., 0:1] * normed[:, None, :] + mix_weights[..., 1:2] * vectors_f[None]
    copy_weight = weights_all[:, EXPERTS + 1 : EXPERTS + 2]
    const_weight = weights_all[:, EXPERTS + 2 : EXPERTS + 4]
    local_terms = copy_weight * normed + jnp.sum(const_weight[:, :, None] * const_out, 1)

    flat_routes = routes.reshape(-1)
    onehot_e = (flat_routes[:, None] == jnp.arange(EXPERTS, dtype=jnp.int32)[None, :]).astype(
        jnp.int32
    )
    slot_rank = jnp.sum((jnp.cumsum(onehot_e, 0) - onehot_e) * onehot_e, -1)
    host = (flat_routes % n_in) * n_seq + flat_routes // n_in
    slot_dest = jnp.where(flat_routes < EXPERTS, host * CAP + slot_rank, EXPERTS * CAP)
    slots = jnp.arange(EXPERTS * CAP, dtype=jnp.int32)
    place = (slot_dest.reshape(tokens_here, 2)[:, :, None] == slots).astype(bf16)

    def dispatch(rows_zero, rows_one):
        return (
            dot_rows(place[:, 0], rows_zero) + dot_rows(place[:, 1], rows_one)
        ).astype(bf16).reshape(EXPERTS, CAP, features)

    def collect(rows, route):
        return jnp.dot(place[:, route], rows, preferred_element_type=f32)

    normed_low = normed.astype(bf16)
    recv_rows = exchange(dispatch(normed_low, normed_low), PLANE).reshape(-1, features)
    gate_part = jnp.dot(recv_rows, gate_full, preferred_element_type=f32)
    up_part = jnp.dot(recv_rows, up_full, preferred_element_type=f32)
    hidden = (jax.nn.silu(gate_part) * up_part).astype(bf16)
    result_rows = jnp.dot(hidden, down_full, preferred_element_type=f32).astype(bf16)
    back_rows = exchange(result_rows.reshape(EXPERTS, CAP, features), PLANE).reshape(-1, features)
    expert_terms = jnp.stack([collect(back_rows, 0), collect(back_rows, 1)], 1)
    full_output = residual_mid + local_terms + jnp.sum(gate_weights[:, :, None] * expert_terms, 1)
    valid_f = valid_mask.astype(jnp.float32)
    differ = full_output - teacher.astype(jnp.float32)
    squared = jnp.sum(valid_f[:, None] * differ * differ)
    grad_full = valid_f[:, None] * differ * (tokens_here * n_all / valid_count)
    gated = (gate_weights[:, :, None] * grad_full[:, None, :]).astype(bf16)
    grad_recv = exchange(dispatch(gated[:, 0], gated[:, 1]), PLANE).reshape(-1, features)

    def expert_grad(partial):
        low = partial.astype(bf16)
        part = lax.psum_scatter(low, "do", scatter_dimension=0, tiled=True)
        part = part.reshape(n_in, -1, partial.shape[1])
        return exchange(part, "di").astype(f32)

    grad_expert_down = expert_grad(dot_rows(hidden, grad_recv))
    sigmoid_gate = jax.nn.sigmoid(gate_part)
    silu_gate = gate_part * sigmoid_gate
    grad_hidden = dot_last(grad_recv, down_full)
    grad_gate_part = (
        grad_hidden * up_part * sigmoid_gate * (1.0 + gate_part * (1.0 - sigmoid_gate))
    ).astype(bf16)
    grad_up_part = (grad_hidden * silu_gate).astype(bf16)
    grad_rows = (dot_last(grad_gate_part, gate_full) + dot_last(grad_up_part, up_full)).astype(bf16)
    grad_back = exchange(grad_rows.reshape(EXPERTS, CAP, features), PLANE).reshape(-1, features)
    grad_expert_gate = expert_grad(dot_rows(recv_rows, grad_gate_part))
    grad_expert_up = expert_grad(dot_rows(recv_rows, grad_up_part))

    expert_dot = jnp.sum(grad_full[:, None, :] * expert_terms, -1)
    copy_dot = jnp.sum(grad_full * normed, -1)
    const_dot = jnp.sum(grad_full[:, None, :] * const_out, -1)
    grad_gates = (
        expert_dot
        + onehot[:, :, EXPERTS + 1] * copy_dot[:, None]
        + jnp.sum(onehot[:, :, EXPERTS + 2 : EXPERTS + 4] * const_dot[:, None, :], -1)
    )
    grad_picked = (grad_gates - jnp.sum(gate_weights * grad_gates, -1, keepdims=True)) / picked_sum
    grad_probs = jnp.sum(grad_picked[:, :, None] * onehot, 1)
    grad_logits = route_probs * (grad_probs - jnp.sum(route_probs * grad_probs, -1, keepdims=True))
    grad_router = dot_rows(normed, grad_logits, exact)
    grad_const = const_weight[:, :, None] * grad_full[:, None, :]
    grad_mix = jnp.stack(
        [jnp.sum(grad_const * normed[:, None, :], -1), jnp.sum(grad_const * vectors_f[None], -1)],
        -1,
    )
    grad_z = (
        mix_weights * (grad_mix - jnp.sum(mix_weights * grad_mix, -1, keepdims=True))
    ).reshape(tokens_here, 4)
    grad_const_mix = dot_rows(normed, grad_z, exact)
    grad_const_vectors = jnp.sum(mix_weights[..., 1:2] * grad_const, 0)
    grad_normed = copy_weight * grad_full + dot_last(grad_logits, router_f, exact)
    grad_normed = (
        grad_normed
        + jnp.sum(mix_weights[..., 0:1] * grad_const, 1)
        + dot_last(grad_z, mix_f, exact)
    )
    grad_normed = grad_normed + collect(grad_back, 0) + collect(grad_back, 1)
    grad_mixture_gain = jnp.sum(grad_normed * unit_second, 0)
    grad_hat = grad_normed * gain_mid
    grad_mid = grad_full + scale_second * (
        grad_hat - unit_second * jnp.mean(grad_hat * unit_second, -1, keepdims=True)
    )
    grad_branch = grad_mid.astype(bf16)
    grad_output_proj = dot_rows(attended_tok, grad_branch).astype(bf16)
    grad_output_proj = exchange(grad_output_proj.reshape(n_all, rows_here, features), ALL)
    grad_output_proj = jnp.sum(grad_output_proj.astype(f32), 0)
    grad_attended = dot_last(grad_branch, full_out).astype(bf16)
    grad_attended = grad_attended.reshape(tokens_here, n_seq, wide).transpose(1, 0, 2)
    grad_heads = exchange(grad_attended, "seq").reshape(length, wide)

    grad_projected = jnp.concatenate(
        attend_backward(grad_heads, attended_t, log_totals, *heads_saved, start), 1
    )
    grad_input_proj = dot_rows(normed_first, grad_projected).astype(bf16)
    grad_input_proj = exchange(grad_input_proj.reshape(n_all, rows_here, 3 * wide), ALL)
    grad_input_proj = (
        jnp.sum(
            grad_input_proj.reshape(n_out * n_in, n_seq, rows_here, 3, wide).astype(f32), 0
        )
        .transpose(1, 2, 0, 3)
        .reshape(rows_here, 3 * features)
    )
    partial_first = dot_last(grad_projected, own_in)
    seq_inputs = held[chosen, :tokens_here].reshape(-1, features).astype(f32)
    unit_seq = seq_inputs * rms_scale(seq_inputs)
    grad_attention_gain = jnp.sum(partial_first * unit_seq, 0)

    held = partial_first.reshape(n_seq, tokens_here, features)[
        jnp.arange(n_seq) ^ seq_id
    ]
    step = 1
    index = list(range(n_seq))
    while step < n_seq:
        pairs = [(i, i ^ step) for i in range(n_seq)]
        keep = [k for k, t in enumerate(index) if not t & step]
        give = [index.index(index[k] ^ step) for k in keep]
        sent = held[np.array(give)].astype(bf16)
        held = held[np.array(keep)] + lax.ppermute(sent, "seq", pairs).astype(f32)
        index = [index[k] for k in keep]
        step *= 2
    grad_normed_first = held[0]

    scale_first = rms_scale(inputs_f)
    unit_first = inputs_f * scale_first
    grad_hat_first = grad_normed_first * gain_first
    grad_input = grad_mid + scale_first * (
        grad_hat_first - unit_first * jnp.mean(grad_hat_first * unit_first, -1, keepdims=True)
    )
    small_grads = jnp.concatenate(
        [
            grad_attention_gain[:, None],
            grad_mixture_gain[:, None],
            grad_router,
            grad_const_mix,
            grad_const_vectors.T,
            jnp.broadcast_to(squared, (features, 1)),
        ],
        1,
    )
    small_grads = jnp.sum(exchange(small_grads.reshape(n_all, rows_here, 21), ALL), 0)
    mean_loss = small_grads[0, 20] / (2.0 * features * valid_count)
    return (
        full_output.astype(bf16),
        mean_loss,
        grad_input,
        grad_input_proj,
        grad_output_proj,
        small_grads[:, 0],
        small_grads[:, 1],
        small_grads[:, 2:14],
        small_grads[:, 14:18],
        small_grads[:, 18:20].T,
        grad_expert_gate,
        grad_expert_up,
        grad_expert_down,
    )


def solution(mesh):
    n_seq = mesh.shape["seq"]
    n_in = EXPERTS // n_seq
    cut = Mesh(mesh.devices.reshape(-1, n_in, n_seq), ALL)
    rows = P(ALL, None)
    line = P(ALL)
    cols = P(None, ALL)
    expert = P("seq", ("do", "di"), None)
    return jax.shard_map(
        body,
        mesh=cut,
        in_specs=(rows, rows, rows, line, line, rows, rows, rows, line, line, rows, rows, cols)
        + (expert,) * 3,
        out_specs=(rows, P(), rows, rows, rows, line, line, rows, rows, cols) + (expert,) * 3,
        check_vma=False,
    )
```

```python
import jax
import jax.numpy as jnp
import numpy as np
from jax import lax
from jax.experimental import pallas as pl
from jax.experimental.pallas import tpu as pltpu
from jax.sharding import Mesh, PartitionSpec as P

HEAD = 64
EXPERTS = 8
ROUTES = 12
CAP = 160
BLK = 512

OUTER = ("a", "b")
SEQ = ("sx", "sc")
ALL = OUTER + ("d",) + SEQ
PLANE = ("d",) + SEQ
ROWS = ("b", "d", "sx")

exact = lax.Precision.HIGHEST
epsilon = 1e-06
masked_out = -1e30
bf16 = jnp.bfloat16
f32 = jnp.float32


def rms_scale(values):
    return lax.rsqrt(jnp.mean(values * values, -1, keepdims=True) + epsilon)


def dot_rows(left, right, precision=None):
    return lax.dot_general(
        left,
        right,
        (((0,), (0,)), ((), ())),
        preferred_element_type=jnp.float32,
        precision=precision,
    )


def dot_last(left, right, precision=None):
    return lax.dot_general(
        left,
        right,
        (((1,), (1,)), ((), ())),
        preferred_element_type=jnp.float32,
        precision=precision,
    )


def nt(a,b): return lax.dot_general(a,b,(((1,),(1,)),((),())),preferred_element_type=f32)
def nn(a,b): return jnp.dot(a,b,preferred_element_type=f32)
def tn(a,b): return lax.dot_general(a,b,(((0,),(0,)),((),())),preferred_element_type=f32)

def fwd_kernel(tbl, held, gain, win, winT, start, normed, att, oT, lse, qn, kn, vn, qT, kT, kbuf, vbuf):
    i=pl.program_id(0)
    wide=win.shape[1]//3
    heads=wide//HEAD
    per=held.shape[1]//BLK
    t=tbl[i//per]
    off=pl.multiple_of((i%per)*BLK,BLK)
    x=held[t,pl.ds(off,BLK),:].astype(f32)
    scale=lax.rsqrt(jnp.mean(x*x,-1,keepdims=True)+epsilon)
    nb=(x*scale*gain[...]).astype(bf16)
    normed[...]=nb
    proj=nn(nb,win[...]).astype(bf16)
    projT=nt(winT[...],nb).astype(bf16)
    qs=projT[:wide]*bf16(HEAD ** -0.5)
    qT[...]=qs
    kT[...]=projT[wide:2*wide]
    vbuf[i]=projT[2*wide:]
    for h in range(heads):
        qn[h]=proj[:,h*HEAD:(h+1)*HEAD]*bf16(HEAD ** -0.5)
        kh=proj[:,wide+h*HEAD:wide+(h+1)*HEAD]
        kn[h]=kh
        kbuf[i,h]=kh
        vn[h]=proj[:,2*wide+h*HEAD:2*wide+(h+1)*HEAD]
    rows=lax.broadcasted_iota(jnp.int32,(BLK,BLK),0)
    cols=lax.broadcasted_iota(jnp.int32,(BLK,BLK),1)
    first=start[...]
    def tile(j,h,mask):
        s=nn(kbuf[j,h],qs[h*HEAD:(h+1)*HEAD])
        return jnp.where(mask,s,masked_out)
    mask=(rows+i*BLK>=first)&(rows<=cols)
    state=[]
    for h in range(heads):
        s=tile(i,h,mask)
        m=jnp.max(s,0,keepdims=True)
        e=jnp.exp(s-m)
        l=jnp.sum(e,0,keepdims=True)
        o=nn(vbuf[i,h*HEAD:(h+1)*HEAD],e.astype(bf16))
        state.append((m,l,o))
    def step(j,state):
        mask=rows+j*BLK>=first
        new=[]
        for h in range(heads):
            m,l,o=state[h]
            s=tile(j,h,mask)
            n=jnp.maximum(m,jnp.max(s,0,keepdims=True))
            a=jnp.exp(m-n)
            e=jnp.exp(s-n)
            l=l*a+jnp.sum(e,0,keepdims=True)
            o=o*a+nn(vbuf[j,h*HEAD:(h+1)*HEAD],e.astype(bf16))
            new.append((n,l,o))
        return tuple(new)
    state=lax.fori_loop(0,i,step,tuple(state))
    for h in range(heads):
        m,l,o=state[h]
        o=o/l
        oT[h*HEAD:(h+1)*HEAD]=o
        att[0,h*HEAD:(h+1)*HEAD]=o.astype(bf16)
        lse[h:h+1]=m+jnp.log(l)
    lse[heads:]=jnp.zeros((lse.shape[0]-heads,BLK),f32)

def attend_forward(table, held, gain, win, win_t, start, tokens, after):
    feat = held.shape[2]
    length = start.shape[1]
    wide = win.shape[1] // 3
    heads = wide // HEAD
    nb = length // BLK
    per = tokens // BLK
    whole = (None, None)
    heads_out = (sds((heads, length, HEAD), bf16), (heads, BLK, HEAD), by_mid)
    cols_out = (sds((wide, length), bf16), (wide, BLK), by_col)
    return call(
        fwd_kernel,
        "attend_forward",
        26,
        (nb,),
        [
            (table,) + whole,
            (held,) + whole,
            (gain,) + whole,
            (win,) + whole,
            (win_t,) + whole,
            (start, (1, BLK), by_col),
        ],
        [
            (sds((length, feat), bf16), (BLK, feat), by_row),
            (sds((length // tokens, wide, tokens), bf16), (1, wide, BLK), lambda i, *_: (i // per, 0, i % per)),
            (sds((wide, length), f32), (wide, BLK), by_col),
            (sds((8, length), f32), (8, BLK), by_col),
            heads_out,
            heads_out,
            heads_out,
            cols_out,
            cols_out,
        ],
        [pltpu.VMEM((nb, heads, BLK, HEAD), bf16), pltpu.VMEM((nb, wide, BLK), bf16)],
        prefetch=1,
        after=after,
    )


def bwd_kernel(
    table, go, o_t, lse, qn, kn, vn, q_t, k_t, start, held, normed, win, small,
    keep, send, gin, g_nat, dq, delta, gin_acc, gain_acc,
):
    j = pl.program_id(0)
    nb = pl.num_programs(0)
    heads = kn.shape[0]
    wide = q_t.shape[0]
    per = go.shape[2] // BLK
    rows = lax.broadcasted_iota(jnp.int32, (BLK, BLK), 0)
    cols = lax.broadcasted_iota(jnp.int32, (BLK, BLK), 1)

    def chunk(ref, i, lanes):
        return ref[i // per, lanes, pl.ds(pl.multiple_of(i % per * BLK, BLK), BLK)]

    @pl.when(j == 0)
    def _():
        dq[...] = jnp.zeros_like(dq)
        gin_acc[...] = jnp.zeros_like(gin_acc)
        gain_acc[...] = jnp.zeros_like(gain_acc)
        for b in range(g_nat.shape[0]):
            g = chunk(go, b, slice(None)).astype(f32)
            g_nat[b] = g.T.astype(bf16)
            prod = g * o_t[:, b * BLK : (b + 1) * BLK]
            for h in range(heads):
                delta[b, h : h + 1] = jnp.sum(prod[h * HEAD : (h + 1) * HEAD], 0, keepdims=True)

    def tile(i, accs, mask):
        new = []
        here = pl.ds(pl.multiple_of(i * BLK, BLK), BLK)
        inside = rows + j * BLK >= start[:, here]
        mask = inside if mask is None else mask & inside
        g_all = g_nat[i]
        for h in range(heads):
            dk, dv = accs[h]
            hs = slice(h * HEAD, (h + 1) * HEAD)
            s = nn(kn[h], q_t[hs, here])
            p = jnp.exp(jnp.where(mask, s, masked_out) - lse[h : h + 1, here])
            dv = dv + nn(p.astype(bf16), g_all[:, hs])
            dp = nn(vn[h], chunk(go, i, hs))
            d = (p * (dp - delta[i, h : h + 1])).astype(bf16)
            dk = dk + nn(d, qn[h, here])
            dq[i, hs] += nn(k_t[hs], d)
            new.append((dk, dv))
        return tuple(new)

    zero = jnp.zeros((BLK, HEAD), f32)
    accs = tile(j, tuple((zero, zero) for _ in range(heads)), rows <= cols)
    accs = lax.fori_loop(j + 1, nb, lambda i, a: tile(i, a, None), accs)
    gp = jnp.concatenate(
        [(dq[j] * HEAD**-0.5).T] + [a[0] for a in accs] + [a[1] for a in accs], 1
    ).astype(bf16)
    back = nt(gp, win[...])
    x = held[0].astype(f32)
    scale = lax.rsqrt(jnp.mean(x * x, -1, keepdims=True) + epsilon)
    gain_acc[0:1] += jnp.sum(back * (x * scale), 0, keepdims=True)
    gin_acc[...] += tn(normed[...], gp)
    place = table[j // per]
    half = keep.shape[0]
    here = pl.ds(pl.multiple_of(j % per * BLK, BLK), BLK)

    @pl.when(place < half)
    def _():
        keep[place, here, :] = back

    @pl.when(place >= half)
    def _():
        send[place - half, here, :] = back.astype(bf16)

    @pl.when(j == nb - 1)
    def _():
        gain = gain_acc[...].T[:, 0:1]
        high = gain.astype(bf16).astype(f32)
        lane = lax.broadcasted_iota(jnp.int32, small.shape, 1)
        tail = jnp.where(lane == 0, high, small[...].astype(f32))
        tail = jnp.where(lane == 21, gain - high, tail)
        gin[...] = jnp.concatenate([gin_acc[...], tail], 1).astype(bf16)


def attend_backward(
    table, go, o_t, lse, qn, kn, vn, q_t, k_t, start, held, normed, win, small, after
):
    n_seq, wide, tokens = go.shape
    length = n_seq * tokens
    heads = wide // HEAD
    feat = win.shape[0]
    nb = length // BLK
    per = tokens // BLK
    half = n_seq // 2
    whole = (None, None)

    def by_table(i, tbl):
        return (tbl[i // per], i % per, 0)

    return call(
        bwd_kernel,
        "attend_backward",
        38,
        (nb,),
        [
            (table,) + whole,
            (go,) + whole,
            (o_t,) + whole,
            (lse,) + whole,
            (qn,) + whole,
            (kn, (heads, BLK, HEAD), by_mid),
            (vn, (heads, BLK, HEAD), by_mid),
            (q_t,) + whole,
            (k_t, (wide, BLK), by_col),
            (start,) + whole,
            (held, (1, BLK, feat), by_table),
            (normed, (BLK, feat), by_row),
            (win,) + whole,
            (small,) + whole,
        ],
        [
            (sds((half, tokens, feat), f32),) + whole,
            (sds((half, tokens, feat), bf16),) + whole,
            (sds((feat, 3 * wide + small.shape[1]), bf16),) + whole,
        ],
        [
            pltpu.VMEM((nb, BLK, wide), bf16),
            pltpu.VMEM((nb, wide, BLK), f32),
            pltpu.VMEM((nb, 8, BLK), f32),
            pltpu.VMEM((feat, 3 * wide), f32),
            pltpu.VMEM((8, feat), f32),
        ],
        prefetch=1,
        after=after,
    )


def call(kernel, name, cost, grid, ins, outs, scratch=(), prefetch=0, limit=60, after=()):
    def spec(shape, block, index):
        if block is None:
            return pl.BlockSpec(shape, lambda *_: (0,) * len(shape))
        return pl.BlockSpec(block, index)

    n_in, n_out = len(ins), len(outs)

    def ordered(*refs):
        rest = refs[n_in + len(after) :]
        rest[n_out][...] = jnp.zeros_like(rest[n_out])
        kernel(*refs[:n_in], *rest[:n_out], *rest[n_out + 1 :])

    outs = list(outs) + [(sds((1, 1), f32), None, None)]
    return pl.pallas_call(
        ordered,
        grid_spec=pltpu.PrefetchScalarGridSpec(
            num_scalar_prefetch=prefetch,
            grid=grid,
            in_specs=[spec(a.shape, b, i) for a, b, i in ins[prefetch:]]
            + [pl.BlockSpec(memory_space=pl.ANY)] * len(after),
            out_specs=[spec(s.shape, b, i) for s, b, i in outs],
            scratch_shapes=list(scratch),
        ),
        out_shape=[s for s, _, _ in outs],
        compiler_params=pltpu.CompilerParams(vmem_limit_bytes=limit << 20),
        cost_estimate=pl.CostEstimate(
            flops=cost * 1150000000,
            bytes_accessed=sum(v.size * v.dtype.itemsize for v, _, _ in ins[prefetch:] + outs),
            transcendentals=0,
        ),
        name=name,
    )(*[a for a, _, _ in ins], *after)


def sds(shape, dtype):
    return jax.ShapeDtypeStruct(shape, dtype)


def by_row(i, *_):
    return (i, 0)


def by_col(i, *_):
    return (0, i)


def by_first(i, *_):
    return (i, 0, 0)


def by_last(i, *_):
    return (0, 0, i)


def by_mid(i, *_):
    return (0, i, 0)


def exact_dot(a, b, dims=((1,), (0,))):
    return lax.dot_general(a, b, (dims, ((), ())), preferred_element_type=f32, precision=exact)


def dispatch_rows(dest, rows, send):
    hosts, cap, features = send.shape
    group = max(g for g in range(1, hosts + 1) if hosts % g == 0 and g * cap <= 640)

    def one(h, carry):
        slot = lax.broadcasted_iota(jnp.int32, (group * cap, dest.shape[1]), 0) + h * group * cap
        hits = [slot == dest[r : r + 1] for r in range(2)]
        if len(rows) == 1:
            hits = [hits[0] | hits[1]]
        total = None
        for hit, part in zip(hits, rows):
            term = nn(jnp.where(hit, 1.0, 0.0).astype(bf16), part[...])
            total = term if total is None else total + term
        send[pl.ds(h * group, group)] = total.astype(bf16).reshape(group, cap, features)
        return carry

    lax.fori_loop(0, hosts // group, one, 0)


def mid_kernel(att, x, wo, gain, wrm, prev, dest, res, normed, soft, send, low):
    i = pl.program_id(0)
    n_seq, wide, block = att.shape
    acc = x[...].astype(f32)
    for s in range(n_seq):
        acc = acc + tn(att[s], wo[s * wide : (s + 1) * wide])
    res[...] = acc
    scale = lax.rsqrt(jnp.mean(acc * acc, -1, keepdims=True) + epsilon)
    unit = acc * scale * gain[...]
    normed[...] = unit
    low[pl.ds(pl.multiple_of(i * block, block), block), :] = unit.astype(bf16)
    logits = exact_dot(unit, wrm[...]) + prev[...]
    lane = lax.broadcasted_iota(jnp.int32, logits.shape, 1)
    result = jnp.zeros_like(logits)
    for lo, hi in ((0, ROUTES), (ROUTES, ROUTES + 2), (ROUTES + 2, ROUTES + 4)):
        inside = (lane >= lo) & (lane < hi)
        part = jnp.where(inside, logits, masked_out)
        expo = jnp.where(inside, jnp.exp(part - jnp.max(part, -1, keepdims=True)), 0.0)
        result = result + expo / jnp.sum(expo, -1, keepdims=True)
    soft[...] = result

    @pl.when(i == pl.num_programs(0) - 1)
    def _():
        dispatch_rows(dest, (low,), send)


def prepare_kernel(got, win, win_t, gains, wrm, out):
    inner = win.shape[1]
    out[...] = got[:, got.shape[1] - out.shape[1] :]
    turned = got[:, : got.shape[1] - out.shape[1]].astype(f32).T
    win[...] = got[:, :inner]
    win_t[...] = turned[:inner].astype(bf16)
    gains[0:2] = turned[inner : inner + 2]
    gains[2:4] = turned[inner + 18 : inner + 20]
    gains[4:8] = jnp.zeros_like(gains[4:8])
    wrm[...] = got[:, inner + 2 : inner + 18].astype(f32)


def gate_parts(soft, routes):
    lane = lax.broadcasted_iota(jnp.int32, soft.shape, 1)
    hits = [(lane == routes[:, r : r + 1]).astype(f32) for r in range(2)]
    picked = [jnp.sum(h * soft, -1, keepdims=True) for h in hits]
    total = picked[0] + picked[1]
    gates = [p / total for p in picked]
    spread = gates[0] * hits[0] + gates[1] * hits[1]

    def lane_of(values, k):
        return values[:, k : k + 1]

    copy = lane_of(spread, EXPERTS + 1)
    const = [lane_of(spread, EXPERTS + 2 + c) for c in range(2)]
    mix = [[lane_of(soft, ROUTES + 2 * c + k) for k in range(2)] for c in range(2)]
    return lane, hits, total, gates, copy, const, mix


def loss_kernel(
    back, dest_col, dest, routes, soft, normed, res, teacher, valid, vectors, factor,
    out, grad, stats, send, squared, low0, low1,
):
    i = pl.program_id(0)
    block = res.shape[0]
    hosts, cap, features = back.shape
    rows = back[...].reshape(hosts * cap, features)
    slot = lax.broadcasted_iota(jnp.int32, (block, hosts * cap), 1)
    terms = [
        nn(jnp.where(slot == dest_col[:, r : r + 1], 1.0, 0.0).astype(bf16), rows)
        for r in range(2)
    ]
    lane, hits, total, gates, copy, const, mix = gate_parts(soft[...], routes[...])
    vec = [vectors[c : c + 1] for c in range(2)]
    unit = normed[...]
    full = res[...] + (copy + const[0] * mix[0][0] + const[1] * mix[1][0]) * unit
    full = full + (const[0] * mix[0][1]) * vec[0] + (const[1] * mix[1][1]) * vec[1]
    full = full + gates[0] * terms[0] + gates[1] * terms[1]
    out[...] = full.astype(bf16)
    ok = valid[...]
    differ = (full - teacher[...].astype(f32)) * ok
    gf = differ * factor[0, 0]
    grad[...] = gf
    here = pl.ds(pl.multiple_of(i * block, block), block)
    low0[here, :] = (gates[0] * gf).astype(bf16)
    low1[here, :] = (gates[1] * gf).astype(bf16)

    def over(values):
        return jnp.sum(gf * values, -1, keepdims=True)

    parts = [over(terms[0]), over(terms[1]), over(unit), over(vec[0]), over(vec[1])]
    tile = lax.broadcasted_iota(jnp.int32, stats.shape, 1)
    filled = jnp.zeros(stats.shape, f32)
    for k, part in enumerate(parts):
        filled = jnp.where(tile == k, part, filled)
    stats[...] = filled

    @pl.when(i == 0)
    def _():
        squared[...] = jnp.zeros_like(squared)

    squared[...] += jnp.sum(differ * differ, 0, keepdims=True)

    @pl.when(i == pl.num_programs(0) - 1)
    def _():
        dispatch_rows(dest, (low0, low1), send)


def route_kernel(soft, routes, stats, grad, normed, wrm, partial, small, small_vec):
    i = pl.program_id(0)
    probs = soft[...]
    lane, hits, total, gates, copy, const, mix = gate_parts(probs, routes[...])
    s = stats[...]
    dots = [s[:, k : k + 1] for k in range(5)]
    const_dot = [mix[c][0] * dots[2] + mix[c][1] * dots[3 + c] for c in range(2)]
    grad_gates = []
    for r in range(2):
        h = hits[r]
        grad_gates.append(
            dots[r]
            + h[:, EXPERTS + 1 : EXPERTS + 2] * dots[2]
            + h[:, EXPERTS + 2 : EXPERTS + 3] * const_dot[0]
            + h[:, EXPERTS + 3 : EXPERTS + 4] * const_dot[1]
        )
    mean = gates[0] * grad_gates[0] + gates[1] * grad_gates[1]
    grad_probs = sum(hits[r] * ((grad_gates[r] - mean) / total) for r in range(2))
    only = jnp.where(lane < ROUTES, probs, 0.0)
    both = only * (grad_probs - jnp.sum(only * grad_probs, -1, keepdims=True))
    for c in range(2):
        grad_mix = [const[c] * dots[2], const[c] * dots[3 + c]]
        inner = mix[c][0] * grad_mix[0] + mix[c][1] * grad_mix[1]
        for k in range(2):
            both = jnp.where(lane == ROUTES + 2 * c + k, mix[c][k] * (grad_mix[k] - inner), both)
    gf = grad[...]
    unit = normed[...]
    coef = copy + const[0] * mix[0][0] + const[1] * mix[1][0]
    partial[...] = coef * gf + exact_dot(both, wrm[...], ((1,), (1,)))
    spread = jnp.where(lane == 0, const[0] * mix[0][1], 0.0)
    spread = jnp.where(lane == 1, const[1] * mix[1][1], spread)

    @pl.when(i == 0)
    def _():
        small[...] = jnp.zeros_like(small)
        small_vec[...] = jnp.zeros_like(small_vec)

    small[...] += exact_dot(unit, both, ((0,), (0,)))
    small_vec[...] += exact_dot(gf, spread, ((0,), (0,)))


def join_kernel(
    back, dest_col, partial, res, grad, gain, wo, mid, branch, out, gain_grad
):
    i = pl.program_id(0)
    block = res.shape[0]
    hosts, cap, features = back.shape
    rows = back[...].reshape(hosts * cap, features)
    slot = lax.broadcasted_iota(jnp.int32, (block, hosts * cap), 1)
    hit = (slot == dest_col[:, 0:1]) | (slot == dest_col[:, 1:2])
    grad_normed = partial[...] + nn(jnp.where(hit, 1.0, 0.0).astype(bf16), rows)
    r = res[...]
    scale = lax.rsqrt(jnp.mean(r * r, -1, keepdims=True) + epsilon)
    unit = r * scale

    @pl.when(i == 0)
    def _():
        gain_grad[...] = jnp.zeros_like(gain_grad)

    gain_grad[...] += jnp.sum(grad_normed * unit, 0, keepdims=True)
    hat = grad_normed * gain[...]
    total = grad[...] + scale * (hat - unit * jnp.mean(hat * unit, -1, keepdims=True))
    mid[...] = total
    low = total.astype(bf16)
    branch[...] = low
    n_seq, wide, _ = out.shape
    for s in range(n_seq):
        out[s] = nt(wo[s * wide : (s + 1) * wide], low).astype(bf16)


def out_grad_kernel(att, branch, out):
    n_seq, wide, _ = att.shape
    for s in range(n_seq):
        out[s * wide : (s + 1) * wide] = nn(att[s], branch[...]).astype(bf16)


def whole_tile(me, own, other, tile):
    tile[:, pl.ds(me[0], 1)] = own[:, None]
    tile[:, pl.ds(1 - me[0], 1)] = other[:, None]
    return tile[...].reshape(-1, tile.shape[-1])


def split_tile(me, values, tile):
    tile[...] = values.reshape(tile.shape)
    return tile[:, pl.ds(me[0], 1)][:, 0], tile[:, pl.ds(1 - me[0], 1)][:, 0]


def expert_hidden_kernel(me, rows, own, other, gate_part, up_part, hidden, gate, up):
    x = rows[...]
    g = nn(x, whole_tile(me, own[:, 0], other[:, 0], gate))
    u = nn(x, whole_tile(me, own[:, 1], other[:, 1], up))
    gate_part[...] = g
    up_part[...] = u
    hidden[...] = (g / (1.0 + jnp.exp(-g)) * u).astype(bf16)


def expert_result_kernel(me, hidden, own, other, result, down):
    @pl.when(pl.program_id(0) == 0)
    def _():
        whole_tile(me, own[...], other[...], down)

    result[...] = nn(hidden[...], down[...].reshape(-1, down.shape[-1])).astype(bf16)


def down_grad_kernel(me, hidden, grad, own, other, parts):
    own[...], other[...] = split_tile(me, tn(hidden[...], grad[...]).astype(bf16), parts)


def expert_backward_kernel(
    me, rows, grad, gate_part, up_part, own, other, down_own, down_other,
    d_own, d_other, result, gate, up, down, parts, acc,
):
    f = pl.program_id(0)
    gh = nt(grad[...], whole_tile(me, down_own[...], down_other[...], down))
    g = gate_part[...]
    u = up_part[...]
    sig = 1.0 / (1.0 + jnp.exp(-g))
    dg = (gh * u * sig * (1.0 + g * (1.0 - sig))).astype(bf16)
    du = (gh * (g * sig)).astype(bf16)
    for k, d in enumerate((dg, du)):
        d_own[:, k], d_other[:, k] = split_tile(me, tn(rows[...], d).astype(bf16), parts)
    part = nt(dg, whole_tile(me, own[:, 0], other[:, 0], gate))
    part = part + nt(du, whole_tile(me, own[:, 1], other[:, 1], up))

    @pl.when(f == 0)
    def _():
        acc[...] = part

    @pl.when(f > 0)
    def _():
        acc[...] += part

    @pl.when(f == pl.num_programs(0) - 1)
    def _():
        result[...] = acc[...].astype(bf16)


def seq_add_kernel(keep, given, near, far):
    near[...] = keep[0] + given[0].astype(f32)
    far[...] = (keep[1] + given[1].astype(f32)).astype(bf16)


def finish_kernel(near, given, mid, x, gain, out):
    grad = near[...] + given[...].astype(f32)
    values = x[...].astype(f32)
    scale = lax.rsqrt(jnp.mean(values * values, -1, keepdims=True) + epsilon)
    unit = values * scale
    hat = grad * gain[...]
    out[...] = mid[...] + scale * (hat - unit * jnp.mean(hat * unit, -1, keepdims=True))


def exchange(blocks, axes):
    return lax.all_to_all(blocks, axes, split_axis=0, concat_axis=0, tiled=True)


def to_all(block, count):
    return exchange(jnp.broadcast_to(block[None], (count,) + block.shape), ALL)


def gather_seq(block, size):
    held = block[None]
    step = size // 2
    while step:
        pairs = [(i, i ^ step) for i in range(size)]
        held = jnp.concatenate([held, lax.ppermute(held, SEQ, pairs)], 0)
        step //= 2
    order = [0]
    step = size // 2
    while step:
        order = order + [k ^ step for k in order]
        step //= 2
    return held, order


def body(
    block_input,
    teacher,
    prev_logits,
    valid_mask,
    segments,
    routes,
    input_proj,
    output_proj,
    attention_gain,
    mixture_gain,
    router,
    const_mix,
    const_vectors,
    expert_gate,
    expert_up,
    expert_down,
):
    n_out, n_in, n_seq = (lax.axis_size(a) for a in (OUTER, "d", SEQ))
    n_all = n_out * n_in * n_seq
    n_far = lax.axis_size("a")
    tokens_here, features = block_input.shape
    rows_here = input_proj.shape[0]
    wide = features // n_seq
    seq_id = lax.axis_index(SEQ)

    a_id, b_id, d_id, c_id = (lax.axis_index(x) for x in ("a", "b", "d", "sc"))
    me = c_id.reshape(1)
    swap = [(0, 1), (1, 0)]
    cross = [(1, 2), (2, 1)]

    def item(values, index):
        return lax.dynamic_index_in_dim(values, index, 0, keepdims=False)

    def in_order(index, mine, given):
        return jnp.where(index == 0, jnp.stack([mine, given]), jnp.stack([given, mine]))

    place = [(b, d, c) for b in range(2) for d in range(2) for c in range(2)]
    alike = [(4 * b + 2 * d + c, 4 * b + 2 * c + d) for b, d, c in place if d != c]
    unlike = [(4 * b + 2 * d + c, 4 * (1 - b) + 2 * c + d) for b, d, c in place]

    def cross(same, other):
        same = jnp.where(c_id == d_id, same, lax.ppermute(same, ("b", "d", "sc"), alike))
        return in_order(b_id, same, lax.ppermute(other, ("b", "d", "sc"), unlike))

    def far_pair(pair):
        return lax.all_gather(pair, "a", axis=0, tiled=False)

    def both_cores(far, done):
        own = far.reshape((n_out,) + far.shape[2:]) + done[0, 0].astype(bf16)
        return own, lax.ppermute(own, "sc", swap)

    def core_sum(own, other):
        total = own.astype(f32) + lax.ppermute(other, "sc", swap).astype(f32)
        return total.astype(bf16).reshape((n_far, 2) + own.shape[1:])

    def far_sum(part):
        return lax.psum_scatter(part, "a", scatter_dimension=0, tiled=False)

    def to_owner(part):
        return cross(item(part, b_id), item(part, 1 - b_id)).astype(f32)

    slice_rows = expert_gate.shape[1]
    odd_rows = slice_rows % 16 != 0

    def to_order(own, other):
        pair = in_order(c_id, own, other)
        return pair.transpose(2, 1, 0, 3, 4).reshape(2, features, -1)

    def from_order(both, count):
        pair = both.reshape(2, count, 2, -1, both.shape[2]).transpose(2, 1, 0, 3, 4)
        return item(pair, c_id), item(pair, 1 - c_id)

    def gate_and_up(index):
        return jnp.stack([item(expert_gate, index), item(expert_up, index)])

    in_pair = cross(gate_and_up(b_id), gate_and_up(1 - b_id))
    down_pair = cross(item(expert_down, b_id), item(expert_down, 1 - b_id))
    own_cols = input_proj.reshape(rows_here, 3, n_seq, wide)
    own_cols = own_cols.transpose(0, 2, 1, 3).reshape(rows_here, -1)
    count_here = jnp.sum(valid_mask)
    count_cols = jnp.stack([count_here // 32, count_here % 32]).astype(bf16)
    small = jnp.concatenate(
        [
            attention_gain[:, None],
            mixture_gain[:, None],
            router,
            const_mix,
            const_vectors.T,
            jnp.broadcast_to(count_cols[None], (rows_here, 2)),
        ],
        1,
    )
    n_small = small.shape[1]
    small = jnp.pad(small, ((0, 0), (0, -(3 * wide + n_small) % 128)))
    packed = jnp.concatenate(
        [
            own_cols.reshape(rows_here, n_seq, 3 * wide).transpose(1, 0, 2),
            jnp.broadcast_to(small[None], (n_seq,) + small.shape),
        ],
        2,
    )
    n_plane = n_in * n_seq
    piece = features // n_plane
    out_piece = output_proj.reshape(rows_here, n_in, n_seq, piece).transpose(1, 2, 0, 3)
    inner = packed.shape[2]
    packed = jnp.concatenate(
        [jnp.broadcast_to(packed[None], (n_in,) + packed.shape), out_piece], 3
    )
    packed = jnp.pad(packed, ((0, 0),) * 3 + ((0, -packed.shape[3] % 128),))
    packed = jnp.broadcast_to(packed[None], (n_out,) + packed.shape)
    got = exchange(packed.reshape((n_all,) + packed.shape[3:]), ALL)
    counts = got[:, 0, 3 * wide + 20 : 3 * wide + 22].astype(f32)
    valid_count = jnp.sum(counts[:, 0]) * 32.0 + jnp.sum(counts[:, 1])
    got = got.reshape(features, -1)
    own_in, own_in_t, gains, wrm, out_cols, prepared = call(
        prepare_kernel,
        "prepare",
        3,
        (1,),
        [(got, None, None)],
        [
            (sds((features, 3 * wide), bf16), None, None),
            (sds((3 * wide, features), bf16), None, None),
            (sds((8, features), f32), None, None),
            (sds((features, ROUTES + 4), f32), None, None),
            (sds((features, got.shape[1] - inner), bf16), None, None),
        ],
    )
    in_far = far_pair(in_pair)
    down_far = far_pair(down_pair + prepared[0, 0].astype(bf16))
    gain_first, gain_mid, vectors_f = gains[0:1], gains[1:2], gains[2:4]
    out_part = jnp.broadcast_to(out_cols[None], (n_plane,) + out_cols.shape)
    full_out = exchange(out_part, PLANE)[:, :, :piece].transpose(1, 0, 2)
    full_out = full_out.reshape(features, features)

    seg_row = jnp.pad(segments.astype(bf16), (0, features * 2 - tokens_here)).reshape(2, features)
    with_seg = jnp.concatenate(
        [block_input, jnp.pad(seg_row, ((0, 14), (0, 0)))], 0
    )
    held, order = gather_seq(with_seg, n_seq)
    where = [order.index(j) for j in range(n_seq)]
    chosen = jnp.array(where, jnp.int32)[jnp.arange(n_seq) ^ seq_id]
    length = n_seq * tokens_here
    seq_segments = (
        held[:, tokens_here : tokens_here + 2]
        .reshape(n_seq, 2 * features)[:, :tokens_here][chosen]
        .reshape(1, -1)
    )
    positions = jnp.arange(length, dtype=jnp.int32)[None]
    fresh = seq_segments != jnp.pad(seq_segments[:, :-1], ((0, 0), (1, 0)), constant_values=-1)
    start = lax.cummax(jnp.where(fresh, positions, 0), axis=1)

    normed_first, attended, attended_t, log_totals, *heads_saved, forward_done = attend_forward(
        chosen, held, gain_first, own_in, own_in_t, start, tokens_here,
        [],
    )
    attended_tok = exchange(attended, SEQ)

    flat_routes = routes.reshape(-1)
    onehot_e = (flat_routes[:, None] == jnp.arange(EXPERTS, dtype=jnp.int32)[None, :]).astype(
        jnp.int32
    )
    slot_rank = jnp.sum((jnp.cumsum(onehot_e, 0) - onehot_e) * onehot_e, -1)
    host = (flat_routes % 2) * 4 + flat_routes // 2 % 2 * 2 + flat_routes // 4
    slot_dest = jnp.where(flat_routes < EXPERTS, host * CAP + slot_rank, EXPERTS * CAP)
    slot_dest = slot_dest.reshape(tokens_here, 2)
    slot_row = jnp.pad(slot_dest.T, ((0, 6), (0, 0)))

    whole = (None, None)
    rows_block = 128
    steps = (tokens_here // rows_block,)
    wide_block = ((rows_block, features), by_row)
    soft_block = ((rows_block, ROUTES + 4), by_row)
    pair_block = ((rows_block, 2), by_row)
    slots_shape = (EXPERTS, CAP, features)
    tok = sds((tokens_here, features), f32)
    residual_mid, normed, soft, send_rows, mid_done = call(
        mid_kernel,
        "mid",
        10,
        steps,
        [
            (attended_tok, (n_seq, wide, rows_block), by_last),
            (block_input,) + wide_block,
            (full_out,) + whole,
            (gain_mid,) + whole,
            (wrm,) + whole,
            (jnp.pad(prev_logits, ((0, 0), (0, 4))),) + soft_block,
            (slot_row,) + whole,
        ],
        [
            (tok,) + wide_block,
            (tok,) + wide_block,
            (sds((tokens_here, ROUTES + 4), f32),) + soft_block,
            (sds(slots_shape, bf16),) + whole,
        ],
        [pltpu.VMEM((tokens_here, features), bf16)],
    )
    in_parts_w = both_cores(in_far, mid_done)
    if odd_rows:
        in_parts_w = from_order(to_order(*in_parts_w), 4)
    recv_rows = exchange(send_rows, ROWS).reshape(-1, features)
    n_rows = recv_rows.shape[0]
    hid = expert_gate.shape[2]
    tile = 512 if hid % 512 == 0 else hid
    tiles = (hid // tile,)
    pieces, _, piece_rows, _ = in_parts_w[0].shape
    w_part = ((pieces, 2, piece_rows, tile), lambda i, *_: (0, 0, 0, i))
    w_tile = pltpu.VMEM((pieces, 2, piece_rows, tile), bf16)
    h_col = ((n_rows, tile), by_col)
    in_parts = [(w,) + w_part for w in in_parts_w]
    gate_part, up_part, hidden, hidden_done = call(
        expert_hidden_kernel,
        "expert_hidden",
        14,
        tiles,
        [(me,) + whole, (recv_rows,) + whole] + in_parts,
        [
            (sds((n_rows, hid), f32),) + h_col,
            (sds((n_rows, hid), f32),) + h_col,
            (sds((n_rows, hid), bf16),) + h_col,
        ],
        [w_tile] * 2,
        prefetch=1,
    )
    down_parts_w = both_cores(down_far, hidden_done)
    far_pieces, far_rows, _ = down_parts_w[0].shape
    per_tile = tile // (2 * far_rows)
    down_block = ((per_tile, far_rows, features), by_first)
    down_tile = pltpu.VMEM((per_tile, 2, far_rows, features), bf16)
    row_tile = n_rows // 4
    result_rows, _ = call(
        expert_result_kernel,
        "expert_result",
        8,
        (4,),
        [
            (me,) + whole,
            (hidden, (row_tile, hid), by_row),
            (down_parts_w[0],) + whole,
            (down_parts_w[1],) + whole,
        ],
        [(sds((n_rows, features), bf16), (row_tile, features), by_row)],
        [pltpu.VMEM((far_pieces, 2, far_rows, features), bf16)],
        prefetch=1,
    )
    back_rows = exchange(result_rows.reshape(slots_shape), ROWS)
    valid_f = valid_mask.astype(f32)[:, None]
    factor = (tokens_here * n_all / valid_count).reshape(1, 1)
    full_output, grad_full, stats, grad_send, squared, _ = call(
        loss_kernel,
        "loss",
        11,
        steps,
        [
            (back_rows,) + whole,
            (slot_dest,) + pair_block,
            (slot_row,) + whole,
            (routes,) + pair_block,
            (soft,) + soft_block,
            (normed,) + wide_block,
            (residual_mid,) + wide_block,
            (teacher,) + wide_block,
            (valid_f, (rows_block, 1), by_row),
            (vectors_f,) + whole,
            (factor,) + whole,
        ],
        [
            (sds((tokens_here, features), bf16),) + wide_block,
            (tok,) + wide_block,
            (sds((tokens_here, 8), f32), (rows_block, 8), by_row),
            (sds(slots_shape, bf16),) + whole,
            (sds((1, features), f32),) + whole,
        ],
        [pltpu.VMEM((tokens_here, features), bf16)] * 2,
    )
    grad_recv = exchange(grad_send, ROWS).reshape(-1, features)
    *down_grads, _ = call(
        down_grad_kernel,
        "down_grad",
        8,
        tiles,
        [(me,) + whole, (hidden,) + h_col, (grad_recv,) + whole],
        [(sds(down_parts_w[0].shape, bf16),) + down_block] * 2,
        [down_tile],
        prefetch=1,
    )
    down_sum = core_sum(*down_grads)
    part_out = (sds(in_parts_w[0].shape, bf16),) + w_part
    *in_grads, grad_rows, backward_done = call(
        expert_backward_kernel,
        "expert_backward",
        32,
        tiles,
        [
            (me,) + whole,
            (recv_rows,) + whole,
            (grad_recv,) + whole,
            (gate_part,) + h_col,
            (up_part,) + h_col,
        ]
        + in_parts
        + [
            (down_parts_w[0],) + down_block,
            (down_parts_w[1],) + down_block,
        ],
        [part_out] * 2 + [(sds((n_rows, features), bf16),) + whole],
        [w_tile] * 2 + [down_tile, w_tile, pltpu.VMEM((n_rows, features), f32)],
        prefetch=1,
        after=[down_sum],
    )
    grad_back = exchange(grad_rows.reshape(slots_shape), ROWS)
    if odd_rows:
        in_grads = from_order(to_order(*in_grads), n_out)
    partial_normed, small_cols, vector_cols, route_done = call(
        route_kernel,
        "route",
        14,
        steps,
        [
            (soft,) + soft_block,
            (routes,) + pair_block,
            (stats, (rows_block, 8), by_row),
            (grad_full,) + wide_block,
            (normed,) + wide_block,
            (wrm,) + whole,
        ],
        [
            (tok,) + wide_block,
            (sds((features, ROUTES + 4), f32),) + whole,
            (sds((features, ROUTES + 4), f32),) + whole,
        ],
    )
    in_sum = core_sum(*in_grads)

    grad_mid, grad_branch, grad_attended, grad_mixture_gain, _ = call(
        join_kernel,
        "join",
        8,
        steps,
        [
            (grad_back,) + whole,
            (slot_dest,) + pair_block,
            (partial_normed,) + wide_block,
            (residual_mid,) + wide_block,
            (grad_full,) + wide_block,
            (gain_mid,) + whole,
            (full_out,) + whole,
        ],
        [
            (tok,) + wide_block,
            (sds((tokens_here, features), bf16),) + wide_block,
            (sds((n_seq, wide, tokens_here), bf16), (n_seq, wide, rows_block), by_last),
            (sds((1, features), f32),) + whole,
        ],
        after=[in_sum],
    )
    grad_output_proj, _ = call(
        out_grad_kernel,
        "out_grad",
        3,
        (1,),
        [(attended_tok,) + whole, (grad_branch,) + whole],
        [(sds((features, features), bf16),) + whole],
    )
    down_part = far_sum(down_sum)
    grad_heads = exchange(grad_attended, SEQ)

    def to_plane(part):
        part = part.reshape(n_out, n_in * n_seq, rows_here, -1).transpose(1, 0, 2, 3)
        return exchange(part, PLANE)

    out_grad = jnp.sum(to_plane(grad_output_proj).astype(f32), 0).astype(bf16)

    small_grads = jnp.concatenate(
        [
            jnp.zeros((features, 1), f32),
            grad_mixture_gain.T,
            small_cols,
            vector_cols[:, :2],
            jnp.broadcast_to(jnp.sum(squared), (features, 1)),
        ],
        1,
    )
    n_small = small_grads.shape[1]

    def two_parts(values, axis):
        high = values.astype(bf16)
        rest = (values - high.astype(f32)).astype(bf16)
        both = jnp.concatenate([high, rest], axis)
        return both

    small_low = two_parts(small_grads, 1)
    small_low = jnp.pad(small_low, ((0, 0), (0, -(3 * wide + 2 * n_small) % 128)))
    keep, sent, last, attention_done = attend_backward(
        chosen, grad_heads, attended_t, log_totals, *heads_saved, start, held, normed_first,
        own_in, small_low, [grad_output_proj],
    )

    sent = lax.ppermute(sent, SEQ, [(i, i ^ 1) for i in range(n_seq)])
    near, sent, added = call(
        seq_add_kernel,
        "seq_add",
        3,
        (2,),
        [
            (keep, (2, tokens_here // 2, features), by_mid),
            (sent, (2, tokens_here // 2, features), by_mid),
        ],
        [
            (tok, (tokens_here // 2, features), by_row),
            (sds((tokens_here, features), bf16), (tokens_here // 2, features), by_row),
        ],
    )
    sent = lax.ppermute(sent, SEQ, [(i, i ^ 2) for i in range(n_seq)])
    grad_input, finished = call(
        finish_kernel,
        "finish",
        3,
        steps,
        [
            (near,) + wide_block,
            (sent,) + wide_block,
            (grad_mid,) + wide_block,
            (block_input,) + wide_block,
            (gain_first,) + whole,
        ],
        [(tok,) + wide_block],
    )
    grad_expert_down = to_owner(down_part + attention_done[0, 0].astype(bf16))
    in_grads = to_owner(far_sum(in_sum) + finished[0, 0].astype(bf16))
    grad_expert_gate, grad_expert_up = in_grads[:, 0], in_grads[:, 1]

    last = last + added[0, 0].astype(bf16)
    last = to_plane(last)
    cols = last[:, :, :, : 3 * wide].reshape(n_in, n_seq, n_out, rows_here, 3 * wide)
    cols = (jnp.sum(cols.astype(f32), 0) + finished[0, 0]).astype(bf16).transpose(1, 2, 0, 3)
    rest = jnp.sum(last[:, :, :, 3 * wide : 3 * wide + 2 * n_small].astype(f32), 0)
    rest = rest[:, :, :n_small] + rest[:, :, n_small:]
    last = jnp.concatenate(
        [cols.reshape(n_out, rows_here, -1), out_grad, two_parts(rest, 2)], 2
    )
    last = jnp.pad(last, ((0, 0), (0, 0), (0, -last.shape[2] % 128)))
    last = jnp.sum(exchange(last, OUTER).astype(f32), 0)
    grad_input_proj = (
        last[:, : 3 * features]
        .reshape(rows_here, n_seq, 3, wide)
        .transpose(0, 2, 1, 3)
        .reshape(rows_here, 3 * features)
    )
    grad_output_proj = last[:, 3 * features : 4 * features]
    last = last[:, 4 * features : 4 * features + 2 * n_small]
    small_grads = last[:, :n_small] + last[:, n_small:]
    mean_loss = small_grads[0, 20] / (2.0 * features * valid_count)
    return (
        full_output,
        mean_loss,
        grad_input,
        grad_input_proj,
        grad_output_proj,
        small_grads[:, 0],
        small_grads[:, 1],
        small_grads[:, 2:14],
        small_grads[:, 14:18],
        small_grads[:, 18:20].T,
        grad_expert_gate,
        grad_expert_up,
        grad_expert_down,
    )


def solution(mesh):
    cut = Mesh(mesh.devices.reshape(-1, 2, 2, 2, mesh.shape["seq"] // 2), ALL)
    rows = P(ALL, None)
    line = P(ALL)
    cols = P(None, ALL)
    expert = P(SEQ, OUTER + ("d",), None)
    return jax.shard_map(
        body,
        mesh=cut,
        in_specs=(rows, rows, rows, line, line, rows, rows, rows, line, line, rows, rows, cols)
        + (expert,) * 3,
        out_specs=(rows, P(), rows, rows, rows, line, line, rows, rows, cols) + (expert,) * 3,
        check_vma=False,
    )
```

```python
import functools

import jax
import jax.numpy as jnp
import numpy as np
from jax import lax
from jax.experimental import pallas as pl
from jax.experimental.pallas import tpu as pltpu
from jax.sharding import Mesh, PartitionSpec as P

HEAD = 64
EXPERTS = 8
ROUTES = 12
CAP = 160
BLK = 512

OUTER = ("a", "b")
SEQ = ("sx", "sc")
ALL = OUTER + ("d",) + SEQ
PLANE = ("d",) + SEQ
ROWS = ("b", "d", "sx")

exact = lax.Precision.HIGHEST
epsilon = 1e-06
masked_out = -1e30
bf16 = jnp.bfloat16
f32 = jnp.float32


def rms_scale(values):
    return lax.rsqrt(jnp.mean(values * values, -1, keepdims=True) + epsilon)


def dot_rows(left, right, precision=None):
    return lax.dot_general(
        left,
        right,
        (((0,), (0,)), ((), ())),
        preferred_element_type=jnp.float32,
        precision=precision,
    )


def dot_last(left, right, precision=None):
    return lax.dot_general(
        left,
        right,
        (((1,), (1,)), ((), ())),
        preferred_element_type=jnp.float32,
        precision=precision,
    )


def nt(a,b): return lax.dot_general(a,b,(((1,),(1,)),((),())),preferred_element_type=f32)
def nn(a,b): return jnp.dot(a,b,preferred_element_type=f32)
def tn(a,b): return lax.dot_general(a,b,(((0,),(0,)),((),())),preferred_element_type=f32)

def fwd_kernel(tbl, held, held_far, gain, win, winT, start, inputs, normed, att, oT, lse, qn, kn, vn, qT, kT, kbuf, vbuf):
    i=pl.program_id(0)
    wide=win.shape[1]//3
    heads=wide//HEAD
    per=held.shape[1]//BLK
    t=tbl[i//per]
    off=pl.multiple_of((i%per)*BLK,BLK)
    half = held.shape[0]

    @pl.when(t < half)
    def _():
        inputs[...] = held[t, pl.ds(off, BLK), :]

    @pl.when(t >= half)
    def _():
        inputs[...] = held_far[t - half, pl.ds(off, BLK), :]

    x = inputs[...].astype(f32)
    scale=lax.rsqrt(jnp.mean(x*x,-1,keepdims=True)+epsilon)
    nb=(x*scale*gain[...]).astype(bf16)
    normed[...]=nb
    proj=nn(nb,win[...]).astype(bf16)
    projT=nt(winT[...],nb).astype(bf16)
    qs=projT[:wide]*bf16(HEAD ** -0.5)
    qT[...]=qs
    kT[...]=projT[wide:2*wide]
    vbuf[i]=projT[2*wide:]
    for h in range(heads):
        qn[h]=proj[:,h*HEAD:(h+1)*HEAD]*bf16(HEAD ** -0.5)
        kh=proj[:,wide+h*HEAD:wide+(h+1)*HEAD]
        kn[h]=kh
        kbuf[i,h]=kh
        vn[h]=proj[:,2*wide+h*HEAD:2*wide+(h+1)*HEAD]
    rows=lax.broadcasted_iota(jnp.int32,(BLK,BLK),0)
    cols=lax.broadcasted_iota(jnp.int32,(BLK,BLK),1)
    first=start[...]
    def tile(j,h,mask):
        s=nn(kbuf[j,h],qs[h*HEAD:(h+1)*HEAD])
        return jnp.where(mask,s,masked_out)
    mask=(rows+i*BLK>=first)&(rows<=cols)
    state=[]
    for h in range(heads):
        s=tile(i,h,mask)
        m=jnp.max(s,0,keepdims=True)
        e=jnp.exp(s-m)
        l=jnp.sum(e,0,keepdims=True)
        o=nn(vbuf[i,h*HEAD:(h+1)*HEAD],e.astype(bf16))
        state.append((m,l,o))
    def step(j,state):
        mask=rows+j*BLK>=first
        new=[]
        for h in range(heads):
            m,l,o=state[h]
            s=tile(j,h,mask)
            n=jnp.maximum(m,jnp.max(s,0,keepdims=True))
            a=jnp.exp(m-n)
            e=jnp.exp(s-n)
            l=l*a+jnp.sum(e,0,keepdims=True)
            o=o*a+nn(vbuf[j,h*HEAD:(h+1)*HEAD],e.astype(bf16))
            new.append((n,l,o))
        return tuple(new)
    state=lax.fori_loop(0,i,step,tuple(state))
    for h in range(heads):
        m,l,o=state[h]
        o=o/l
        oT[h*HEAD:(h+1)*HEAD]=o
        att[0,h*HEAD:(h+1)*HEAD]=o.astype(bf16)
        lse[h:h+1]=m+jnp.log(l)
    lse[heads:]=jnp.zeros((lse.shape[0]-heads,BLK),f32)

def attend_forward(table, held, gain, win, win_t, start, tokens, after):
    feat = held[0].shape[2]
    length = start.shape[1]
    wide = win.shape[1] // 3
    heads = wide // HEAD
    nb = length // BLK
    per = tokens // BLK
    whole = (None, None)
    heads_out = (sds((heads, length, HEAD), bf16), (heads, BLK, HEAD), by_mid)
    cols_out = (sds((wide, length), bf16), (wide, BLK), by_col)
    return call(
        fwd_kernel,
        "attend_forward",
        26,
        (nb,),
        [
            (table,) + whole,
            (held[0],) + whole,
            (held[1],) + whole,
            (gain,) + whole,
            (win,) + whole,
            (win_t,) + whole,
            (start, (1, BLK), by_col),
        ],
        [
            (sds((length, feat), bf16), (BLK, feat), by_row),
            (sds((length, feat), bf16), (BLK, feat), by_row),
            (sds((length // tokens, wide, tokens), bf16), (1, wide, BLK), lambda i, *_: (i // per, 0, i % per)),
            (sds((wide, length), f32), (wide, BLK), by_col),
            (sds((8, length), f32), (8, BLK), by_col),
            heads_out,
            heads_out,
            heads_out,
            cols_out,
            cols_out,
        ],
        [pltpu.VMEM((nb, heads, BLK, HEAD), bf16), pltpu.VMEM((nb, wide, BLK), bf16)],
        prefetch=1,
        after=after,
    )


def bwd_kernel(
    table, go, o_t, lse, qn, kn, vn, q_t, k_t, start, held, normed, win, small,
    keep, send, gin, g_nat, dq, delta, gin_acc, gain_acc,
):
    j = pl.program_id(0)
    nb = pl.num_programs(0)
    heads = kn.shape[0]
    wide = q_t.shape[0]
    per = go.shape[2] // BLK
    rows = lax.broadcasted_iota(jnp.int32, (BLK, BLK), 0)
    cols = lax.broadcasted_iota(jnp.int32, (BLK, BLK), 1)

    def chunk(ref, i, lanes):
        return ref[i // per, lanes, pl.ds(pl.multiple_of(i % per * BLK, BLK), BLK)]

    @pl.when(j == 0)
    def _():
        dq[...] = jnp.zeros_like(dq)
        gin_acc[...] = jnp.zeros_like(gin_acc)
        gain_acc[...] = jnp.zeros_like(gain_acc)
        for b in range(g_nat.shape[0]):
            g = chunk(go, b, slice(None)).astype(f32)
            g_nat[b] = g.T.astype(bf16)
            prod = g * o_t[:, b * BLK : (b + 1) * BLK]
            for h in range(heads):
                delta[b, h : h + 1] = jnp.sum(prod[h * HEAD : (h + 1) * HEAD], 0, keepdims=True)

    def tile(i, accs, mask):
        new = []
        here = pl.ds(pl.multiple_of(i * BLK, BLK), BLK)
        inside = rows + j * BLK >= start[:, here]
        mask = inside if mask is None else mask & inside
        g_all = g_nat[i]
        for h in range(heads):
            dk, dv = accs[h]
            hs = slice(h * HEAD, (h + 1) * HEAD)
            s = nn(kn[h], q_t[hs, here])
            p = jnp.exp(jnp.where(mask, s, masked_out) - lse[h : h + 1, here])
            dv = dv + nn(p.astype(bf16), g_all[:, hs])
            dp = nn(vn[h], chunk(go, i, hs))
            d = (p * (dp - delta[i, h : h + 1])).astype(bf16)
            dk = dk + nn(d, qn[h, here])
            dq[i, hs] += nn(k_t[hs], d)
            new.append((dk, dv))
        return tuple(new)

    zero = jnp.zeros((BLK, HEAD), f32)
    accs = tile(j, tuple((zero, zero) for _ in range(heads)), rows <= cols)
    accs = lax.fori_loop(j + 1, nb, lambda i, a: tile(i, a, None), accs)
    gp = jnp.concatenate(
        [(dq[j] * HEAD**-0.5).T] + [a[0] for a in accs] + [a[1] for a in accs], 1
    ).astype(bf16)
    back = nt(gp, win[...])
    x = held[...].astype(f32)
    scale = lax.rsqrt(jnp.mean(x * x, -1, keepdims=True) + epsilon)
    gain_acc[0:1] += jnp.sum(back * (x * scale), 0, keepdims=True)
    gin_acc[...] += tn(normed[...], gp)
    place = table[j // per]
    half = keep.shape[0]
    here = pl.ds(pl.multiple_of(j % per * BLK, BLK), BLK)

    @pl.when(place < half)
    def _():
        keep[place, here, :] = back

    @pl.when(place >= half)
    def _():
        send[place - half, here, :] = back.astype(bf16)

    @pl.when(j == nb - 1)
    def _():
        gain = gain_acc[...].T[:, 0:1]
        high = gain.astype(bf16).astype(f32)
        lane = lax.broadcasted_iota(jnp.int32, small.shape, 1)
        tail = jnp.where(lane == 0, high, small[...].astype(f32))
        tail = jnp.where(lane == 21, gain - high, tail)
        gin[...] = jnp.concatenate([gin_acc[...], tail], 1).astype(bf16)


def attend_backward(
    table, go, o_t, lse, qn, kn, vn, q_t, k_t, start, held, normed, win, small, after
):
    n_seq, wide, tokens = go.shape
    length = n_seq * tokens
    heads = wide // HEAD
    feat = win.shape[0]
    nb = length // BLK
    per = tokens // BLK
    half = n_seq // 2
    whole = (None, None)

    return call(
        bwd_kernel,
        "attend_backward",
        7600,
        (nb,),
        [
            (table,) + whole,
            (go,) + whole,
            (o_t,) + whole,
            (lse,) + whole,
            (qn,) + whole,
            (kn, (heads, BLK, HEAD), by_mid),
            (vn, (heads, BLK, HEAD), by_mid),
            (q_t,) + whole,
            (k_t, (wide, BLK), by_col),
            (start,) + whole,
            (held, (BLK, feat), by_row),
            (normed, (BLK, feat), by_row),
            (win,) + whole,
            (small,) + whole,
        ],
        [
            (sds((half, tokens, feat), f32),) + whole,
            (sds((half, tokens, feat), bf16),) + whole,
            (sds((feat, 3 * wide + small.shape[1]), bf16),) + whole,
        ],
        [
            pltpu.VMEM((nb, BLK, wide), bf16),
            pltpu.VMEM((nb, wide, BLK), f32),
            pltpu.VMEM((nb, 8, BLK), f32),
            pltpu.VMEM((feat, 3 * wide), f32),
            pltpu.VMEM((8, feat), f32),
        ],
        prefetch=1,
        after=after,
    )


def call(kernel, name, cost, grid, ins, outs, scratch=(), prefetch=0, limit=60, after=()):
    def spec(shape, block, index):
        if block is None:
            return pl.BlockSpec(shape, lambda *_: (0,) * len(shape))
        return pl.BlockSpec(block, index)

    n_in, n_out = len(ins), len(outs)

    def ordered(*refs):
        rest = refs[n_in + len(after) :]
        rest[n_out][...] = jnp.zeros_like(rest[n_out])
        kernel(*refs[:n_in], *rest[:n_out], *rest[n_out + 1 :])

    outs = list(outs) + [(sds((1, 1), f32), None, None)]
    return pl.pallas_call(
        ordered,
        grid_spec=pltpu.PrefetchScalarGridSpec(
            num_scalar_prefetch=prefetch,
            grid=grid,
            in_specs=[spec(a.shape, b, i) for a, b, i in ins[prefetch:]]
            + [pl.BlockSpec(memory_space=pl.ANY)] * len(after),
            out_specs=[spec(s.shape, b, i) for s, b, i in outs],
            scratch_shapes=list(scratch),
        ),
        out_shape=[s for s, _, _ in outs],
        compiler_params=pltpu.CompilerParams(vmem_limit_bytes=limit << 20),
        cost_estimate=pl.CostEstimate(
            flops=int(cost * 5750000),
            bytes_accessed=sum(v.size * v.dtype.itemsize for v, _, _ in ins[prefetch:] + outs),
            transcendentals=0,
        ),
        name=name,
    )(*[a for a, _, _ in ins], *after)


def sds(shape, dtype):
    return jax.ShapeDtypeStruct(shape, dtype)


def by_row(i, *_):
    return (i, 0)


def by_col(i, *_):
    return (0, i)


def by_first(i, *_):
    return (i, 0, 0)


def by_last(i, *_):
    return (0, 0, i)


def by_mid(i, *_):
    return (0, i, 0)


def exact_dot(a, b, dims=((1,), (0,))):
    return lax.dot_general(a, b, (dims, ((), ())), preferred_element_type=f32, precision=exact)


def dispatch_rows(dest, rows, send):
    hosts, cap, features = send.shape
    group = max(g for g in range(1, hosts + 1) if hosts % g == 0 and g * cap <= 640)

    def one(h, carry):
        slot = lax.broadcasted_iota(jnp.int32, (group * cap, dest.shape[1]), 0) + h * group * cap
        hits = [slot == dest[r : r + 1] for r in range(2)]
        if len(rows) == 1:
            hits = [hits[0] | hits[1]]
        total = None
        for hit, part in zip(hits, rows):
            term = nn(jnp.where(hit, 1.0, 0.0).astype(bf16), part[...])
            total = term if total is None else total + term
        send[pl.ds(h * group, group)] = total.astype(bf16).reshape(group, cap, features)
        return carry

    lax.fori_loop(0, hosts // group, one, 0)


def mid_kernel(att, x, wo, gain, wrm, prev, dest, res, normed, soft, send, low):
    i = pl.program_id(0)
    n_seq, wide, block = att.shape
    acc = x[...].astype(f32)
    for s in range(n_seq):
        acc = acc + tn(att[s], wo[s * wide : (s + 1) * wide])
    res[...] = acc
    scale = lax.rsqrt(jnp.mean(acc * acc, -1, keepdims=True) + epsilon)
    unit = acc * scale * gain[...]
    normed[...] = unit
    low[pl.ds(pl.multiple_of(i * block, block), block), :] = unit.astype(bf16)
    logits = exact_dot(unit, wrm[...]) + prev[...]
    lane = lax.broadcasted_iota(jnp.int32, logits.shape, 1)
    result = jnp.zeros_like(logits)
    for lo, hi in ((0, ROUTES), (ROUTES, ROUTES + 2), (ROUTES + 2, ROUTES + 4)):
        inside = (lane >= lo) & (lane < hi)
        part = jnp.where(inside, logits, masked_out)
        expo = jnp.where(inside, jnp.exp(part - jnp.max(part, -1, keepdims=True)), 0.0)
        result = result + expo / jnp.sum(expo, -1, keepdims=True)
    soft[...] = result

    @pl.when(i == pl.num_programs(0) - 1)
    def _():
        dispatch_rows(dest, (low,), send)


def prepare_kernel(got, win, win_t, gains, wrm, out):
    inner = win.shape[1]
    out[...] = got[:, got.shape[1] - out.shape[1] :]
    turned = got[:, : got.shape[1] - out.shape[1]].astype(f32).T
    win[...] = got[:, :inner]
    win_t[...] = turned[:inner].astype(bf16)
    gains[0:2] = turned[inner : inner + 2]
    gains[2:4] = turned[inner + 18 : inner + 20]
    gains[4:8] = jnp.zeros_like(gains[4:8])
    wrm[...] = got[:, inner + 2 : inner + 18].astype(f32)


def gate_parts(soft, routes):
    lane = lax.broadcasted_iota(jnp.int32, soft.shape, 1)
    hits = [(lane == routes[:, r : r + 1]).astype(f32) for r in range(2)]
    picked = [jnp.sum(h * soft, -1, keepdims=True) for h in hits]
    total = picked[0] + picked[1]
    gates = [p / total for p in picked]
    spread = gates[0] * hits[0] + gates[1] * hits[1]

    def lane_of(values, k):
        return values[:, k : k + 1]

    copy = lane_of(spread, EXPERTS + 1)
    const = [lane_of(spread, EXPERTS + 2 + c) for c in range(2)]
    mix = [[lane_of(soft, ROUTES + 2 * c + k) for k in range(2)] for c in range(2)]
    return lane, hits, total, gates, copy, const, mix


def loss_kernel(
    back, dest_col, dest, routes, soft, normed, res, teacher, valid, vectors, factor,
    out, grad, stats, send, squared, low0, low1,
):
    i = pl.program_id(0)
    block = res.shape[0]
    hosts, cap, features = back.shape
    rows = back[...].reshape(hosts * cap, features)
    slot = lax.broadcasted_iota(jnp.int32, (block, hosts * cap), 1)
    terms = [
        nn(jnp.where(slot == dest_col[:, r : r + 1], 1.0, 0.0).astype(bf16), rows)
        for r in range(2)
    ]
    lane, hits, total, gates, copy, const, mix = gate_parts(soft[...], routes[...])
    vec = [vectors[c : c + 1] for c in range(2)]
    unit = normed[...]
    full = res[...] + (copy + const[0] * mix[0][0] + const[1] * mix[1][0]) * unit
    full = full + (const[0] * mix[0][1]) * vec[0] + (const[1] * mix[1][1]) * vec[1]
    full = full + gates[0] * terms[0] + gates[1] * terms[1]
    out[...] = full.astype(bf16)
    ok = valid[...]
    differ = (full - teacher[...].astype(f32)) * ok
    gf = differ * factor[0, 0]
    grad[...] = gf
    here = pl.ds(pl.multiple_of(i * block, block), block)
    low0[here, :] = (gates[0] * gf).astype(bf16)
    low1[here, :] = (gates[1] * gf).astype(bf16)

    def over(values):
        return jnp.sum(gf * values, -1, keepdims=True)

    parts = [over(terms[0]), over(terms[1]), over(unit), over(vec[0]), over(vec[1])]
    tile = lax.broadcasted_iota(jnp.int32, stats.shape, 1)
    filled = jnp.zeros(stats.shape, f32)
    for k, part in enumerate(parts):
        filled = jnp.where(tile == k, part, filled)
    stats[...] = filled

    @pl.when(i == 0)
    def _():
        squared[...] = jnp.zeros_like(squared)

    squared[...] += jnp.sum(differ * differ, 0, keepdims=True)

    @pl.when(i == pl.num_programs(0) - 1)
    def _():
        dispatch_rows(dest, (low0, low1), send)


def route_kernel(soft, routes, stats, grad, normed, wrm, partial, small, small_vec):
    i = pl.program_id(0)
    probs = soft[...]
    lane, hits, total, gates, copy, const, mix = gate_parts(probs, routes[...])
    s = stats[...]
    dots = [s[:, k : k + 1] for k in range(5)]
    const_dot = [mix[c][0] * dots[2] + mix[c][1] * dots[3 + c] for c in range(2)]
    grad_gates = []
    for r in range(2):
        h = hits[r]
        grad_gates.append(
            dots[r]
            + h[:, EXPERTS + 1 : EXPERTS + 2] * dots[2]
            + h[:, EXPERTS + 2 : EXPERTS + 3] * const_dot[0]
            + h[:, EXPERTS + 3 : EXPERTS + 4] * const_dot[1]
        )
    mean = gates[0] * grad_gates[0] + gates[1] * grad_gates[1]
    grad_probs = sum(hits[r] * ((grad_gates[r] - mean) / total) for r in range(2))
    only = jnp.where(lane < ROUTES, probs, 0.0)
    both = only * (grad_probs - jnp.sum(only * grad_probs, -1, keepdims=True))
    for c in range(2):
        grad_mix = [const[c] * dots[2], const[c] * dots[3 + c]]
        inner = mix[c][0] * grad_mix[0] + mix[c][1] * grad_mix[1]
        for k in range(2):
            both = jnp.where(lane == ROUTES + 2 * c + k, mix[c][k] * (grad_mix[k] - inner), both)
    gf = grad[...]
    unit = normed[...]
    coef = copy + const[0] * mix[0][0] + const[1] * mix[1][0]
    partial[...] = coef * gf + exact_dot(both, wrm[...], ((1,), (1,)))
    spread = jnp.where(lane == 0, const[0] * mix[0][1], 0.0)
    spread = jnp.where(lane == 1, const[1] * mix[1][1], spread)

    @pl.when(i == 0)
    def _():
        small[...] = jnp.zeros_like(small)
        small_vec[...] = jnp.zeros_like(small_vec)

    small[...] += exact_dot(unit, both, ((0,), (0,)))
    small_vec[...] += exact_dot(gf, spread, ((0,), (0,)))


def join_kernel(
    back, dest_col, partial, res, grad, gain, wo, mid, branch, out, gain_grad
):
    i = pl.program_id(0)
    block = res.shape[0]
    hosts, cap, features = back.shape
    rows = back[...].reshape(hosts * cap, features)
    slot = lax.broadcasted_iota(jnp.int32, (block, hosts * cap), 1)
    hit = (slot == dest_col[:, 0:1]) | (slot == dest_col[:, 1:2])
    grad_normed = partial[...] + nn(jnp.where(hit, 1.0, 0.0).astype(bf16), rows)
    r = res[...]
    scale = lax.rsqrt(jnp.mean(r * r, -1, keepdims=True) + epsilon)
    unit = r * scale

    @pl.when(i == 0)
    def _():
        gain_grad[...] = jnp.zeros_like(gain_grad)

    gain_grad[...] += jnp.sum(grad_normed * unit, 0, keepdims=True)
    hat = grad_normed * gain[...]
    total = grad[...] + scale * (hat - unit * jnp.mean(hat * unit, -1, keepdims=True))
    mid[...] = total
    low = total.astype(bf16)
    branch[...] = low
    n_seq, wide, _ = out.shape
    for s in range(n_seq):
        out[s] = nt(wo[s * wide : (s + 1) * wide], low).astype(bf16)


def out_grad_kernel(att, branch, out):
    n_seq, wide, _ = att.shape
    for s in range(n_seq):
        out[s * wide : (s + 1) * wide] = nn(att[s], branch[...]).astype(bf16)


def whole_tile(me, parts, tile):
    far, core = me[0], me[1]
    for part, f, c in zip(parts, (far, 1 - far, far, 1 - far), (core, core, 1 - core, 1 - core)):
        tile[pl.ds(f, 1), :, pl.ds(c, 1)] = part[None, :, None]
    return tile[...].reshape(-1, tile.shape[-1])


def pick_kernel(index, *refs):
    shards, same, other = refs[:-2], refs[-2], refs[-1]
    for k, shard in enumerate(shards):
        same[k] = shard[index[0]]
        other[k] = shard[1 - index[0]]


def total_kernel(n_small, parts, gin, gout, router, mix, small, vectors):
    total = jnp.sum(parts[...].astype(f32), 0)
    features = gout.shape[1]
    wide = HEAD * (features // HEAD // 4)
    for s in range(features // wide):
        for k in range(3):
            at = (3 * s + k) * wide
            gin[:, k * features + s * wide : k * features + (s + 1) * wide] = total[:, at : at + wide]
    gout[...] = total[:, 3 * features : 4 * features]
    tail = total[:, 4 * features :]
    both = tail[:, :n_small] + tail[:, n_small : 2 * n_small]
    n_pad = small.shape[0]
    unit = lax.broadcasted_iota(jnp.int32, (n_pad, tail.shape[1]), 0)
    unit = (unit == lax.broadcasted_iota(jnp.int32, unit.shape, 1)).astype(f32)
    wide_both = tail + jnp.concatenate([tail[:, n_small:], tail[:, :n_small]], 1)
    small[...] = exact_dot(unit, wide_both, ((1,), (1,)))
    vectors[...] = small[18:20]
    router[...] = both[:, 2 : 2 + ROUTES]
    mix[...] = both[:, 2 + ROUTES : 6 + ROUTES]


def owner_kernel(which, part, alike, unlike, gate, up):
    mine = part[which[0]]
    first = jnp.where(which[1] == 1, mine, alike[...])
    for k, out in enumerate((gate, up)):
        out[which[0]] = first[k].astype(f32)
        out[1 - which[0]] = unlike[k].astype(f32)


def cross_kernel(which, same, alike, unlike, out):
    @pl.when(which[1] == 1)
    def _():
        out[pl.ds(which[0], 1)] = same[...][None]

    @pl.when(which[1] != 1)
    def _():
        out[pl.ds(which[0], 1)] = alike[...][None]

    out[pl.ds(1 - which[0], 1)] = unlike[...][None]


def split_tile(me, values, tile):
    tile[...] = values.reshape(tile.shape)
    return tile[:, pl.ds(me[1], 1)][:, 0], tile[:, pl.ds(1 - me[1], 1)][:, 0]


def expert_hidden_kernel(
    me, rows, near, far, near_other, far_other, gate_part, up_part, hidden, gate, up
):
    x = rows[...]
    parts = (near, far, near_other, far_other)
    g = nn(x, whole_tile(me, [p[:, 0] for p in parts], gate))
    u = nn(x, whole_tile(me, [p[:, 1] for p in parts], up))
    gate_part[...] = g
    up_part[...] = u
    hidden[...] = (g / (1.0 + jnp.exp(-g)) * u).astype(bf16)


def expert_result_kernel(me, hidden, near, far, near_other, far_other, result, down):
    @pl.when(pl.program_id(0) == 0)
    def _():
        whole_tile(me, [p[...] for p in (near, far, near_other, far_other)], down)

    result[...] = nn(hidden[...], down[...].reshape(-1, down.shape[-1])).astype(bf16)


def down_grad_kernel(me, hidden, grad, own, other, parts):
    own[...], other[...] = split_tile(me, tn(hidden[...], grad[...]).astype(bf16), parts)


def expert_backward_kernel(
    me, rows, grad, gate_part, up_part, near, far, near_other, far_other,
    down_near, down_far, down_near_other, down_far_other,
    d_own, d_other, result, gate, up, down, parts, acc,
):
    f = pl.program_id(0)

    @pl.when(f == 0)
    def _():
        pieces = (down_near, down_far, down_near_other, down_far_other)
        whole_tile(me, [p[...] for p in pieces], down)

    gh = nt(grad[...], down[f // 2, f % 2].reshape(-1, down.shape[-1]))
    g = gate_part[...]
    u = up_part[...]
    sig = 1.0 / (1.0 + jnp.exp(-g))
    dg = (gh * u * sig * (1.0 + g * (1.0 - sig))).astype(bf16)
    du = (gh * (g * sig)).astype(bf16)
    for k, d in enumerate((dg, du)):
        d_own[:, k], d_other[:, k] = split_tile(me, tn(rows[...], d).astype(bf16), parts)
    weights = (near, far, near_other, far_other)
    part = nt(dg, whole_tile(me, [p[:, 0] for p in weights], gate))
    part = part + nt(du, whole_tile(me, [p[:, 1] for p in weights], up))

    @pl.when(f == 0)
    def _():
        acc[...] = part

    @pl.when(f > 0)
    def _():
        acc[...] += part

    @pl.when(f == pl.num_programs(0) - 1)
    def _():
        result[...] = acc[...].astype(bf16)


def seq_add_kernel(keep, given, near, far):
    near[...] = keep[0] + given[0].astype(f32)
    far[...] = (keep[1] + given[1].astype(f32)).astype(bf16)


def finish_kernel(near, given, mid, x, gain, out):
    grad = near[...] + given[...].astype(f32)
    values = x[...].astype(f32)
    scale = lax.rsqrt(jnp.mean(values * values, -1, keepdims=True) + epsilon)
    unit = values * scale
    hat = grad * gain[...]
    out[...] = mid[...] + scale * (hat - unit * jnp.mean(hat * unit, -1, keepdims=True))


def exchange(blocks, axes):
    return lax.all_to_all(blocks, axes, split_axis=0, concat_axis=0, tiled=True)


def to_all(block, count):
    return exchange(jnp.broadcast_to(block[None], (count,) + block.shape), ALL)


def gather_seq(block, size):
    held = block[None]
    step = size // 2
    while step > 1:
        pairs = [(i, i ^ step) for i in range(size)]
        held = jnp.concatenate([held, lax.ppermute(held, SEQ, pairs)], 0)
        step //= 2
    held = (held, lax.ppermute(held, SEQ, [(i, i ^ 1) for i in range(size)]))
    order = [0]
    step = size // 2
    while step:
        order = order + [k ^ step for k in order]
        step //= 2
    return held, order


def body(
    block_input,
    teacher,
    prev_logits,
    valid_mask,
    segments,
    routes,
    input_proj,
    output_proj,
    attention_gain,
    mixture_gain,
    router,
    const_mix,
    const_vectors,
    expert_gate,
    expert_up,
    expert_down,
):
    n_out, n_in, n_seq = (lax.axis_size(a) for a in (OUTER, "d", SEQ))
    n_all = n_out * n_in * n_seq
    n_far = lax.axis_size("a")
    tokens_here, features = block_input.shape
    rows_here = input_proj.shape[0]
    wide = features // n_seq
    seq_id = lax.axis_index(SEQ)

    a_id, b_id, d_id, c_id = (lax.axis_index(x) for x in ("a", "b", "d", "sc"))
    me = jnp.stack([a_id * (n_far == 2), c_id])
    swap = [(0, 1), (1, 0)]
    cross = [(1, 2), (2, 1)]

    def item(values, index):
        return lax.dynamic_index_in_dim(values, index, 0, keepdims=False)

    def in_order(index, mine, given):
        return jnp.where(index == 0, jnp.stack([mine, given]), jnp.stack([given, mine]))

    which = jnp.stack([b_id, (c_id == d_id).astype(jnp.int32)])

    place = [(b, d, c) for b in range(2) for d in range(2) for c in range(2)]
    alike = [(4 * b + 2 * d + c, 4 * b + 2 * c + d) for b, d, c in place if d != c]
    unlike = [(4 * b + 2 * d + c, 4 * (1 - b) + 2 * c + d) for b, d, c in place]

    def crossed(same, other):
        same = jnp.where(c_id == d_id, same, lax.ppermute(same, ("b", "d", "sc"), alike))
        return in_order(b_id, same, lax.ppermute(other, ("b", "d", "sc"), unlike))

    def cross(same, other, after):
        given = [lax.ppermute(same, ("b", "d", "sc"), alike)]
        given.append(lax.ppermute(other, ("b", "d", "sc"), unlike))
        count, height, width = same.shape
        quarter = width // (4 if width % 512 == 0 else 2)
        block = ((count, height, quarter), by_last)
        pair, _ = call(
            cross_kernel,
            "cross",
            2,
            (width // quarter,),
            [(which, None, None)] + [(x,) + block for x in [same] + given],
            [(sds((2,) + same.shape, bf16), (2,) + block[0], lambda i, *_: (0, 0, 0, i))],
            prefetch=1,
            after=after,
        )
        return pair

    def far_pair(pair):
        return lax.all_gather(pair, "a", axis=0, tiled=False)

    def far_parts(far, done):
        if n_far == 2:
            far = item(far, 1 - a_id)
        far = far + done[0, 0].astype(bf16)
        return far, lax.ppermute(far, "sc", swap)

    def core_sum(own, other, done=None):
        total = own.astype(f32) + lax.ppermute(other, "sc", swap).astype(f32)
        if done is not None:
            total = total + done[0, 0]
        return total.astype(bf16).reshape((n_far, 2) + own.shape[1:])

    def far_sum(part):
        return lax.psum_scatter(part, "a", scatter_dimension=0, tiled=False)

    def to_owner(part):
        return crossed(item(part, b_id), item(part, 1 - b_id)).astype(f32)

    def regroup(near, far, near_other, far_other):
        if n_far == 2:
            return near, far, near_other, far_other
        pair = in_order(c_id, far, far_other).transpose(3, 1, 2, 0, 4, 5)
        pair = pair.reshape(pair.shape[:1] + (2, 2, 2, -1) + pair.shape[5:])
        pair = pair.transpose(1, 3, 2, 0, 4, 5)
        return tuple(item(pair[f], c) for c in (c_id, 1 - c_id) for f in range(2))

    def owner_slices(own, other):
        if n_far == 2:
            return own, other
        pair = in_order(c_id, own, other).transpose(2, 1, 0, 3, 4)
        pair = pair.reshape(pair.shape[:1] + (n_out, 2, -1) + pair.shape[4:])
        pair = pair.transpose(2, 1, 0, 3, 4)
        return item(pair, c_id), item(pair, 1 - c_id)

    def pick(shards, after=()):
        _, height, width = shards[0].shape
        quarter = width // (4 if width % 512 == 0 else 2)
        block = ((2, height, quarter), by_last)
        out_block = ((len(shards), height, quarter), by_last)
        return call(
            pick_kernel,
            "pick",
            3,
            (width // quarter,),
            [(b_id.reshape(1), None, None)] + [(x,) + block for x in shards],
            [(sds((len(shards), height, width), bf16),) + out_block] * 2,
            prefetch=1,
            after=after,
        )

    same_in, other_in, picked = pick([expert_gate, expert_up])
    seg_row = jnp.pad(segments.astype(bf16), (0, features * 2 - tokens_here)).reshape(2, features)
    with_seg = jnp.concatenate(
        [block_input, jnp.pad(seg_row, ((0, 14), (0, 0)))], 0
    )
    held, order = gather_seq(with_seg, n_seq)
    where = [order.index(j) for j in range(n_seq)]
    chosen = jnp.array(where, jnp.int32)[jnp.arange(n_seq) ^ seq_id]
    length = n_seq * tokens_here
    seg_rows = [h[:, tokens_here : tokens_here + 2] for h in held]
    seq_segments = (
        jnp.concatenate(seg_rows, 0)
        .reshape(n_seq, 2 * features)[:, :tokens_here][chosen]
        .reshape(1, -1)
    )
    positions = jnp.arange(length, dtype=jnp.int32)[None]
    fresh = seq_segments != jnp.pad(seq_segments[:, :-1], ((0, 0), (1, 0)), constant_values=-1)
    start = lax.cummax(jnp.where(fresh, positions, 0), axis=1)

    flat_routes = routes.reshape(-1)
    onehot_e = (flat_routes[:, None] == jnp.arange(EXPERTS, dtype=jnp.int32)[None, :]).astype(
        jnp.int32
    )
    slot_rank = jnp.sum((jnp.cumsum(onehot_e, 0) - onehot_e) * onehot_e, -1)
    host = (flat_routes % 2) * 4 + flat_routes // 2 % 2 * 2 + flat_routes // 4
    slot_dest = jnp.where(flat_routes < EXPERTS, host * CAP + slot_rank, EXPERTS * CAP)
    slot_dest = slot_dest.reshape(tokens_here, 2)
    slot_row = jnp.pad(slot_dest.T, ((0, 6), (0, 0)))

    in_pair = cross(same_in, other_in, [held[1], start, slot_row])
    in_far = far_pair(in_pair)
    in_other = lax.ppermute(in_pair, "sc", swap)
    same_down, other_down, _ = pick([expert_down], [in_pair])

    own_cols = (input_proj + picked[0, 0].astype(bf16)).reshape(rows_here, 3, n_seq, wide)
    own_cols = own_cols.transpose(0, 2, 1, 3).reshape(rows_here, -1)
    count_here = jnp.sum(valid_mask)
    count_cols = jnp.stack([count_here // 32, count_here % 32]).astype(bf16)
    small = jnp.concatenate(
        [
            attention_gain[:, None],
            mixture_gain[:, None],
            router,
            const_mix,
            const_vectors.T,
            jnp.broadcast_to(count_cols[None], (rows_here, 2)),
        ],
        1,
    )
    n_small = small.shape[1]
    small = jnp.pad(small, ((0, 0), (0, -(3 * wide + n_small) % 128)))
    packed = jnp.concatenate(
        [
            own_cols.reshape(rows_here, n_seq, 3 * wide).transpose(1, 0, 2),
            jnp.broadcast_to(small[None], (n_seq,) + small.shape),
        ],
        2,
    )
    n_plane = n_in * n_seq
    piece = features // n_plane
    out_piece = output_proj.reshape(rows_here, n_in, n_seq, piece).transpose(1, 2, 0, 3)
    inner = packed.shape[2]
    packed = jnp.concatenate(
        [jnp.broadcast_to(packed[None], (n_in,) + packed.shape), out_piece], 3
    )
    packed = jnp.pad(packed, ((0, 0),) * 3 + ((0, -packed.shape[3] % 128),))
    packed = jnp.broadcast_to(packed[None], (n_out,) + packed.shape)
    got = exchange(packed.reshape((n_all,) + packed.shape[3:]), ALL)
    counts = got[:, 0, 3 * wide + 20 : 3 * wide + 22].astype(f32)
    valid_count = jnp.sum(counts[:, 0]) * 32.0 + jnp.sum(counts[:, 1])
    got = got.reshape(features, -1)
    own_in, own_in_t, gains, wrm, out_cols, prepared = call(
        prepare_kernel,
        "prepare",
        3,
        (1,),
        [(got, None, None)],
        [
            (sds((features, 3 * wide), bf16), None, None),
            (sds((3 * wide, features), bf16), None, None),
            (sds((8, features), f32), None, None),
            (sds((features, ROUTES + 4), f32), None, None),
            (sds((features, got.shape[1] - inner), bf16), None, None),
        ],
    )
    gain_first, gain_mid, vectors_f = gains[0:1], gains[1:2], gains[2:4]
    out_part = jnp.broadcast_to(out_cols[None], (n_plane,) + out_cols.shape)
    full_out = exchange(out_part, PLANE)[:, :, :piece].transpose(1, 0, 2)
    full_out = full_out.reshape(features, features)

    seq_inputs, normed_first, attended, attended_t, log_totals, *heads_saved, forward_done = attend_forward(
        chosen, held, gain_first, own_in, own_in_t, start, tokens_here,
        [in_other],
    )
    attended_tok = exchange(attended, SEQ)

    down_pair = cross(same_down, other_down, [normed_first])
    down_far = far_pair(down_pair)
    down_other = lax.ppermute(down_pair, "sc", swap)

    whole = (None, None)
    rows_block = 128
    steps = (tokens_here // rows_block,)
    wide_block = ((rows_block, features), by_row)
    soft_block = ((rows_block, ROUTES + 4), by_row)
    pair_block = ((rows_block, 2), by_row)
    slots_shape = (EXPERTS, CAP, features)
    tok = sds((tokens_here, features), f32)
    residual_mid, normed, soft, send_rows, mid_done = call(
        mid_kernel,
        "mid",
        10,
        steps,
        [
            (attended_tok, (n_seq, wide, rows_block), by_last),
            (block_input,) + wide_block,
            (full_out,) + whole,
            (gain_mid,) + whole,
            (wrm,) + whole,
            (jnp.pad(prev_logits, ((0, 0), (0, 4))),) + soft_block,
            (slot_row,) + whole,
        ],
        [
            (tok,) + wide_block,
            (tok,) + wide_block,
            (sds((tokens_here, ROUTES + 4), f32),) + soft_block,
            (sds(slots_shape, bf16),) + whole,
        ],
        [pltpu.VMEM((tokens_here, features), bf16)],
        after=[down_other, in_far],
    )
    in_far, in_far_other = far_parts(in_far, mid_done)
    in_parts_w = regroup(in_pair, in_far, in_other, in_far_other)
    recv_rows = exchange(send_rows, ROWS).reshape(-1, features)
    n_rows = recv_rows.shape[0]
    hid = expert_gate.shape[2]
    tile = 512 if hid % 512 == 0 else hid
    tiles = (hid // tile,)
    _, _, piece_rows, _ = in_parts_w[0].shape
    w_part = ((2, 2, piece_rows, tile), lambda i, *_: (0, 0, 0, i))
    w_tile = pltpu.VMEM((2, 2, 2, piece_rows, tile), bf16)
    h_col = ((n_rows, tile), by_col)
    in_parts = [(w,) + w_part for w in in_parts_w]
    gate_part, up_part, hidden, hidden_done = call(
        expert_hidden_kernel,
        "expert_hidden",
        14,
        tiles,
        [(me,) + whole, (recv_rows,) + whole] + in_parts,
        [
            (sds((n_rows, hid), f32),) + h_col,
            (sds((n_rows, hid), f32),) + h_col,
            (sds((n_rows, hid), bf16),) + h_col,
        ],
        [w_tile] * 2,
        prefetch=1,
    )
    down_far, down_far_other = far_parts(down_far, hidden_done)
    down_parts_w = [p[:, 0] for p in regroup(down_pair, down_far, down_other, down_far_other)]
    far_rows = down_parts_w[0].shape[1]
    down_tile = pltpu.VMEM((2, 2, 2, far_rows, features), bf16)
    row_tile = n_rows // 4
    result_rows, _ = call(
        expert_result_kernel,
        "expert_result",
        8,
        (4,),
        [
            (me,) + whole,
            (hidden, (row_tile, hid), by_row),
        ]
        + [(p,) + whole for p in down_parts_w],
        [(sds((n_rows, features), bf16), (row_tile, features), by_row)],
        [down_tile],
        prefetch=1,
    )
    back_rows = exchange(result_rows.reshape(slots_shape), ROWS)
    valid_f = valid_mask.astype(f32)[:, None]
    factor = (tokens_here * n_all / valid_count).reshape(1, 1)
    full_output, grad_full, stats, grad_send, squared, _ = call(
        loss_kernel,
        "loss",
        11,
        steps,
        [
            (back_rows,) + whole,
            (slot_dest,) + pair_block,
            (slot_row,) + whole,
            (routes,) + pair_block,
            (soft,) + soft_block,
            (normed,) + wide_block,
            (residual_mid,) + wide_block,
            (teacher,) + wide_block,
            (valid_f, (rows_block, 1), by_row),
            (vectors_f,) + whole,
            (factor,) + whole,
        ],
        [
            (sds((tokens_here, features), bf16),) + wide_block,
            (tok,) + wide_block,
            (sds((tokens_here, 8), f32), (rows_block, 8), by_row),
            (sds(slots_shape, bf16),) + whole,
            (sds((1, features), f32),) + whole,
        ],
        [pltpu.VMEM((tokens_here, features), bf16)] * 2,
    )
    grad_recv = exchange(grad_send, ROWS).reshape(-1, features)
    *down_grads, _ = call(
        down_grad_kernel,
        "down_grad",
        8,
        tiles,
        [(me,) + whole, (hidden,) + h_col, (grad_recv,) + whole],
        [(sds((4, far_rows, features), bf16), (1, far_rows, features), by_first)] * 2,
        [pltpu.VMEM((1, 2, far_rows, features), bf16)],
        prefetch=1,
    )
    down_sum = core_sum(*owner_slices(*(p[:, None] for p in down_grads)))
    part_out = (sds((4, 2, piece_rows, hid), bf16), (4, 2, piece_rows, tile), w_part[1])
    *in_grads, grad_rows, backward_done = call(
        expert_backward_kernel,
        "expert_backward",
        32,
        tiles,
        [
            (me,) + whole,
            (recv_rows,) + whole,
            (grad_recv,) + whole,
            (gate_part,) + h_col,
            (up_part,) + h_col,
        ]
        + in_parts
        + [(p,) + whole for p in down_parts_w],
        [part_out] * 2 + [(sds((n_rows, features), bf16),) + whole],
        [w_tile] * 2
        + [
            down_tile,
            pltpu.VMEM((4, 2, piece_rows, tile), bf16),
            pltpu.VMEM((n_rows, features), f32),
        ],
        prefetch=1,
        after=[down_sum],
    )
    grad_back = exchange(grad_rows.reshape(slots_shape), ROWS)
    down_part = far_sum(down_sum)
    partial_normed, small_cols, vector_cols, route_done = call(
        route_kernel,
        "route",
        14,
        steps,
        [
            (soft,) + soft_block,
            (routes,) + pair_block,
            (stats, (rows_block, 8), by_row),
            (grad_full,) + wide_block,
            (normed,) + wide_block,
            (wrm,) + whole,
        ],
        [
            (tok,) + wide_block,
            (sds((features, ROUTES + 4), f32),) + whole,
            (sds((features, ROUTES + 4), f32),) + whole,
        ],
    )

    in_sum = core_sum(*owner_slices(*in_grads), route_done)

    grad_mid, grad_branch, grad_attended, grad_mixture_gain, join_done = call(
        join_kernel,
        "join",
        8,
        steps,
        [
            (grad_back,) + whole,
            (slot_dest,) + pair_block,
            (partial_normed,) + wide_block,
            (residual_mid,) + wide_block,
            (grad_full,) + wide_block,
            (gain_mid,) + whole,
            (full_out,) + whole,
        ],
        [
            (tok,) + wide_block,
            (sds((tokens_here, features), bf16),) + wide_block,
            (sds((n_seq, wide, tokens_here), bf16), (n_seq, wide, rows_block), by_last),
            (sds((1, features), f32),) + whole,
        ],
        after=[in_sum],
    )
    grad_output_proj, _ = call(
        out_grad_kernel,
        "out_grad",
        3,
        (1,),
        [(attended_tok,) + whole, (grad_branch,) + whole],
        [(sds((features, features), bf16),) + whole],
    )
    grad_heads = exchange(grad_attended, SEQ)

    def plane_blocks(part):
        return part.reshape(n_out, n_plane, rows_here, -1).transpose(1, 0, 2, 3)

    out_blocks = plane_blocks(grad_output_proj)
    out_grad = jnp.sum(exchange(out_blocks, PLANE).astype(f32), 0).astype(bf16)

    small_grads = jnp.concatenate(
        [
            jnp.zeros((features, 1), f32),
            grad_mixture_gain.T,
            small_cols,
            vector_cols[:, :2],
            jnp.broadcast_to(jnp.sum(squared), (features, 1)),
        ],
        1,
    )
    n_small = small_grads.shape[1]

    def two_parts(values, axis):
        high = values.astype(bf16)
        rest = (values - high.astype(f32)).astype(bf16)
        both = jnp.concatenate([high, rest], axis)
        return both

    small_low = two_parts(small_grads, 1)
    small_low = jnp.pad(small_low, ((0, 0), (0, -(3 * wide + 2 * n_small) % 128)))
    keep, sent, last, attention_done = attend_backward(
        chosen, grad_heads, attended_t, log_totals, *heads_saved, start, seq_inputs, normed_first,
        own_in, small_low, [out_blocks],
    )

    in_part = far_sum(in_sum) + attention_done[0, 0].astype(bf16)
    given = [
        lax.ppermute(item(part, i), ("b", "d", "sc"), pairs)
        for part, i, pairs in ((in_part, b_id, alike), (in_part, 1 - b_id, unlike))
    ]

    sent = lax.ppermute(sent, SEQ, [(i, i ^ 1) for i in range(n_seq)])
    near, sent, added = call(
        seq_add_kernel,
        "seq_add",
        3,
        (2,),
        [
            (keep, (2, tokens_here // 2, features), by_mid),
            (sent, (2, tokens_here // 2, features), by_mid),
        ],
        [
            (tok, (tokens_here // 2, features), by_row),
            (sds((tokens_here, features), bf16), (tokens_here // 2, features), by_row),
        ],
        after=[in_part],
    )
    last = exchange(plane_blocks(last + added[0, 0].astype(bf16)), PLANE)
    sent = lax.ppermute(sent, SEQ, [(i, i ^ 2) for i in range(n_seq)])
    grad_input, finished = call(
        finish_kernel,
        "finish",
        3,
        steps,
        [
            (near,) + wide_block,
            (sent,) + wide_block,
            (grad_mid,) + wide_block,
            (block_input,) + wide_block,
            (gain_first,) + whole,
        ],
        [(tok,) + wide_block],
        after=[last],
    )

    in_shape = (2,) + in_part.shape[2:]
    in_block = (in_shape[0], in_shape[1], hid // 4)
    cols_part = ((2,) + in_block, lambda i, *_: (0, 0, 0, i))
    cols_item = (in_block, by_last)
    grad_expert_gate, grad_expert_up, _ = call(
        owner_kernel,
        "owner",
        4,
        (4,),
        [(which, None, None), (in_part,) + cols_part] + [(x,) + cols_item for x in given],
        [(sds(in_shape, f32),) + cols_item] * 2,
        prefetch=1,
        after=[grad_input],
    )
    cols = last[:, :, :, : 3 * wide].reshape(n_in, n_seq, n_out, rows_here, 3 * wide)
    cols = (jnp.sum(cols.astype(f32), 0) + finished[0, 0]).astype(bf16).transpose(1, 2, 0, 3)
    rest = jnp.sum(last[:, :, :, 3 * wide : 3 * wide + 2 * n_small].astype(f32), 0)
    rest = rest[:, :, :n_small] + rest[:, :, n_small:]
    last = jnp.concatenate(
        [cols.reshape(n_out, rows_here, -1), out_grad, two_parts(rest, 2)], 2
    )
    last = jnp.pad(last, ((0, 0), (0, 0), (0, -last.shape[2] % 128)))
    *last, small_grads, grad_const_vectors, _ = call(
        functools.partial(total_kernel, n_small),
        "total",
        2,
        (1,),
        [(exchange(last, OUTER),) + whole],
        [
            (sds((rows_here, 3 * features), f32),) + whole,
            (sds((rows_here, features), f32),) + whole,
            (sds((rows_here, ROUTES), f32),) + whole,
            (sds((rows_here, 4), f32),) + whole,
            (sds((24, rows_here), f32),) + whole,
            (sds((2, rows_here), f32),) + whole,
        ],
    )
    grad_expert_down = to_owner(down_part + finished[0, 0].astype(bf16))[:, 0]
    grad_input_proj, grad_output_proj, grad_router, grad_const_mix = last
    mean_loss = small_grads[20, 0] / (2.0 * features * valid_count)
    return (
        full_output,
        mean_loss,
        grad_input,
        grad_input_proj,
        grad_output_proj,
        small_grads[0],
        small_grads[1],
        grad_router,
        grad_const_mix,
        grad_const_vectors,
        grad_expert_gate,
        grad_expert_up,
        grad_expert_down,
    )


def solution(mesh):
    cut = Mesh(mesh.devices.reshape(-1, 2, 2, 2, mesh.shape["seq"] // 2), ALL)
    rows = P(ALL, None)
    line = P(ALL)
    cols = P(None, ALL)
    expert = P(SEQ, OUTER + ("d",), None)
    return jax.shard_map(
        body,
        mesh=cut,
        in_specs=(rows, rows, rows, line, line, rows, rows, rows, line, line, rows, rows, cols)
        + (expert,) * 3,
        out_specs=(rows, P(), rows, rows, rows, line, line, rows, rows, cols) + (expert,) * 3,
        check_vma=False,
    )
```

```python
import functools

import jax
import jax.numpy as jnp
import numpy as np
from jax import lax
from jax.experimental import pallas as pl
from jax.experimental.pallas import tpu as pltpu
from jax.sharding import Mesh, PartitionSpec as P

HEAD = 64
EXPERTS = 8
ROUTES = 12
CAP = 160
BLK = 512

OUTER = ("a", "b")
SEQ = ("sx", "sc")
ALL = OUTER + ("d",) + SEQ
PLANE = ("d",) + SEQ
ROWS = ("b", "d", "sx")

exact = lax.Precision.HIGHEST
epsilon = 1e-06
masked_out = -1e30
bf16 = jnp.bfloat16
f32 = jnp.float32


def rms_scale(values):
    return lax.rsqrt(jnp.mean(values * values, -1, keepdims=True) + epsilon)


def dot_rows(left, right, precision=None):
    return lax.dot_general(
        left,
        right,
        (((0,), (0,)), ((), ())),
        preferred_element_type=jnp.float32,
        precision=precision,
    )


def dot_last(left, right, precision=None):
    return lax.dot_general(
        left,
        right,
        (((1,), (1,)), ((), ())),
        preferred_element_type=jnp.float32,
        precision=precision,
    )


def nt(a,b): return lax.dot_general(a,b,(((1,),(1,)),((),())),preferred_element_type=f32)
def nn(a,b): return jnp.dot(a,b,preferred_element_type=f32)
def tn(a,b): return lax.dot_general(a,b,(((0,),(0,)),((),())),preferred_element_type=f32)

def fwd_kernel(tbl, held, held_far, gain, win, winT, start, inputs, normed, att, oT, lse, qn, kn, vn, qT, kT, kbuf, vbuf):
    i=pl.program_id(0)
    wide=win.shape[1]//3
    heads=wide//HEAD
    per=held.shape[1]//BLK
    t=tbl[i//per]
    off=pl.multiple_of((i%per)*BLK,BLK)
    half = held.shape[0]

    @pl.when(t < half)
    def _():
        inputs[...] = held[t, pl.ds(off, BLK), :]

    @pl.when(t >= half)
    def _():
        inputs[...] = held_far[t - half, pl.ds(off, BLK), :]

    x = inputs[...].astype(f32)
    scale=lax.rsqrt(jnp.mean(x*x,-1,keepdims=True)+epsilon)
    nb=(x*scale*gain[...]).astype(bf16)
    normed[...]=nb
    proj=nn(nb,win[...]).astype(bf16)
    projT=nt(winT[...],nb).astype(bf16)
    qs=projT[:wide]*bf16(HEAD ** -0.5)
    qT[...]=qs
    kT[...]=projT[wide:2*wide]
    vbuf[i]=projT[2*wide:]
    for h in range(heads):
        qn[h]=proj[:,h*HEAD:(h+1)*HEAD]*bf16(HEAD ** -0.5)
        kh=proj[:,wide+h*HEAD:wide+(h+1)*HEAD]
        kn[h]=kh
        kbuf[i,h]=kh
        vn[h]=proj[:,2*wide+h*HEAD:2*wide+(h+1)*HEAD]
    rows=lax.broadcasted_iota(jnp.int32,(BLK,BLK),0)
    cols=lax.broadcasted_iota(jnp.int32,(BLK,BLK),1)
    first=start[...]
    def tile(j,h,mask):
        s=nn(kbuf[j,h],qs[h*HEAD:(h+1)*HEAD])
        return jnp.where(mask,s,masked_out)
    mask=(rows+i*BLK>=first)&(rows<=cols)
    state=[]
    for h in range(heads):
        s=tile(i,h,mask)
        m=jnp.max(s,0,keepdims=True)
        e=jnp.exp(s-m)
        l=jnp.sum(e,0,keepdims=True)
        o=nn(vbuf[i,h*HEAD:(h+1)*HEAD],e.astype(bf16))
        state.append((m,l,o))
    def step(j,state):
        mask=rows+j*BLK>=first
        new=[]
        for h in range(heads):
            m,l,o=state[h]
            s=tile(j,h,mask)
            n=jnp.maximum(m,jnp.max(s,0,keepdims=True))
            a=jnp.exp(m-n)
            e=jnp.exp(s-n)
            l=l*a+jnp.sum(e,0,keepdims=True)
            o=o*a+nn(vbuf[j,h*HEAD:(h+1)*HEAD],e.astype(bf16))
            new.append((n,l,o))
        return tuple(new)
    state=lax.fori_loop(0,i,step,tuple(state))
    for h in range(heads):
        m,l,o=state[h]
        o=o/l
        oT[h*HEAD:(h+1)*HEAD]=o
        att[0,h*HEAD:(h+1)*HEAD]=o.astype(bf16)
        lse[h:h+1]=m+jnp.log(l)
    lse[heads:]=jnp.zeros((lse.shape[0]-heads,BLK),f32)

def attend_forward(table, held, gain, win, win_t, start, tokens, after):
    feat = held[0].shape[2]
    length = start.shape[1]
    wide = win.shape[1] // 3
    heads = wide // HEAD
    nb = length // BLK
    per = tokens // BLK
    whole = (None, None)
    heads_out = (sds((heads, length, HEAD), bf16), (heads, BLK, HEAD), by_mid)
    cols_out = (sds((wide, length), bf16), (wide, BLK), by_col)
    return call(
        fwd_kernel,
        "attend_forward",
        26,
        (nb,),
        [
            (table,) + whole,
            (held[0],) + whole,
            (held[1],) + whole,
            (gain,) + whole,
            (win,) + whole,
            (win_t,) + whole,
            (start, (1, BLK), by_col),
        ],
        [
            (sds((length, feat), bf16), (BLK, feat), by_row),
            (sds((length, feat), bf16), (BLK, feat), by_row),
            (sds((length // tokens, wide, tokens), bf16), (1, wide, BLK), lambda i, *_: (i // per, 0, i % per)),
            (sds((wide, length), f32), (wide, BLK), by_col),
            (sds((8, length), f32), (8, BLK), by_col),
            heads_out,
            heads_out,
            heads_out,
            cols_out,
            cols_out,
        ],
        [pltpu.VMEM((nb, heads, BLK, HEAD), bf16), pltpu.VMEM((nb, wide, BLK), bf16)],
        prefetch=1,
        after=after,
    )


def bwd_kernel(
    table, go, o_t, lse, qn, kn, vn, q_t, k_t, start, held, normed, win, small,
    keep, send, gin, g_nat, dq, delta, gin_acc, gain_acc,
):
    j = pl.program_id(0)
    nb = pl.num_programs(0)
    heads = kn.shape[0]
    wide = q_t.shape[0]
    per = go.shape[2] // BLK
    rows = lax.broadcasted_iota(jnp.int32, (BLK, BLK), 0)
    cols = lax.broadcasted_iota(jnp.int32, (BLK, BLK), 1)

    def chunk(ref, i, lanes):
        return ref[i // per, lanes, pl.ds(pl.multiple_of(i % per * BLK, BLK), BLK)]

    @pl.when(j == 0)
    def _():
        dq[...] = jnp.zeros_like(dq)
        gin_acc[...] = jnp.zeros_like(gin_acc)
        gain_acc[...] = jnp.zeros_like(gain_acc)
        for b in range(g_nat.shape[0]):
            g = chunk(go, b, slice(None)).astype(f32)
            g_nat[b] = g.T.astype(bf16)
            prod = g * o_t[:, b * BLK : (b + 1) * BLK]
            for h in range(heads):
                delta[b, h : h + 1] = jnp.sum(prod[h * HEAD : (h + 1) * HEAD], 0, keepdims=True)

    def tile(i, accs, mask):
        new = []
        here = pl.ds(pl.multiple_of(i * BLK, BLK), BLK)
        inside = rows + j * BLK >= start[:, here]
        mask = inside if mask is None else mask & inside
        g_all = g_nat[i]
        for h in range(heads):
            dk, dv = accs[h]
            hs = slice(h * HEAD, (h + 1) * HEAD)
            s = nn(kn[h], q_t[hs, here])
            p = jnp.exp(jnp.where(mask, s, masked_out) - lse[h : h + 1, here])
            dv = dv + nn(p.astype(bf16), g_all[:, hs])
            dp = nn(vn[h], chunk(go, i, hs))
            d = (p * (dp - delta[i, h : h + 1])).astype(bf16)
            dk = dk + nn(d, qn[h, here])
            dq[i, hs] += nn(k_t[hs], d)
            new.append((dk, dv))
        return tuple(new)

    zero = jnp.zeros((BLK, HEAD), f32)
    accs = tile(j, tuple((zero, zero) for _ in range(heads)), rows <= cols)
    accs = lax.fori_loop(j + 1, nb, lambda i, a: tile(i, a, None), accs)
    gp = jnp.concatenate(
        [(dq[j] * HEAD**-0.5).T] + [a[0] for a in accs] + [a[1] for a in accs], 1
    ).astype(bf16)
    back = nt(gp, win[...])
    x = held[...].astype(f32)
    scale = lax.rsqrt(jnp.mean(x * x, -1, keepdims=True) + epsilon)
    gain_acc[0:1] += jnp.sum(back * (x * scale), 0, keepdims=True)
    gin_acc[...] += tn(normed[...], gp)
    place = table[j // per]
    half = keep.shape[0]
    here = pl.ds(pl.multiple_of(j % per * BLK, BLK), BLK)

    @pl.when(place < half)
    def _():
        keep[place, here, :] = back

    @pl.when(place >= half)
    def _():
        send[place - half, here, :] = back.astype(bf16)

    @pl.when(j == nb - 1)
    def _():
        gain = gain_acc[...].T[:, 0:1]
        high = gain.astype(bf16).astype(f32)
        lane = lax.broadcasted_iota(jnp.int32, small.shape, 1)
        tail = jnp.where(lane == 0, high, small[...].astype(f32))
        tail = jnp.where(lane == 21, gain - high, tail)
        gin[...] = jnp.concatenate([gin_acc[...], tail], 1).astype(bf16)


def attend_backward(
    table, go, o_t, lse, qn, kn, vn, q_t, k_t, start, held, normed, win, small, after
):
    n_seq, wide, tokens = go.shape
    length = n_seq * tokens
    heads = wide // HEAD
    feat = win.shape[0]
    nb = length // BLK
    per = tokens // BLK
    half = n_seq // 2
    whole = (None, None)

    return call(
        bwd_kernel,
        "attend_backward",
        7600,
        (nb,),
        [
            (table,) + whole,
            (go,) + whole,
            (o_t,) + whole,
            (lse,) + whole,
            (qn,) + whole,
            (kn, (heads, BLK, HEAD), by_mid),
            (vn, (heads, BLK, HEAD), by_mid),
            (q_t,) + whole,
            (k_t, (wide, BLK), by_col),
            (start,) + whole,
            (held, (BLK, feat), by_row),
            (normed, (BLK, feat), by_row),
            (win,) + whole,
            (small,) + whole,
        ],
        [
            (sds((half, tokens, feat), f32),) + whole,
            (sds((half, tokens, feat), bf16),) + whole,
            (sds((feat, 3 * wide + small.shape[1]), bf16),) + whole,
        ],
        [
            pltpu.VMEM((nb, BLK, wide), bf16),
            pltpu.VMEM((nb, wide, BLK), f32),
            pltpu.VMEM((nb, 8, BLK), f32),
            pltpu.VMEM((feat, 3 * wide), f32),
            pltpu.VMEM((8, feat), f32),
        ],
        prefetch=1,
        after=after,
    )


def call(kernel, name, cost, grid, ins, outs, scratch=(), prefetch=0, limit=60, after=()):
    def spec(shape, block, index):
        if block is None:
            return pl.BlockSpec(shape, lambda *_: (0,) * len(shape))
        return pl.BlockSpec(block, index)

    n_in, n_out = len(ins), len(outs)

    def ordered(*refs):
        rest = refs[n_in + len(after) :]
        rest[n_out][...] = jnp.zeros_like(rest[n_out])
        kernel(*refs[:n_in], *rest[:n_out], *rest[n_out + 1 :])

    outs = list(outs) + [(sds((1, 1), f32), None, None)]
    return pl.pallas_call(
        ordered,
        grid_spec=pltpu.PrefetchScalarGridSpec(
            num_scalar_prefetch=prefetch,
            grid=grid,
            in_specs=[spec(a.shape, b, i) for a, b, i in ins[prefetch:]]
            + [pl.BlockSpec(memory_space=pl.ANY)] * len(after),
            out_specs=[spec(s.shape, b, i) for s, b, i in outs],
            scratch_shapes=list(scratch),
        ),
        out_shape=[s for s, _, _ in outs],
        compiler_params=pltpu.CompilerParams(vmem_limit_bytes=limit << 20),
        cost_estimate=pl.CostEstimate(
            flops=int(cost * 5750000),
            bytes_accessed=sum(v.size * v.dtype.itemsize for v, _, _ in ins[prefetch:] + outs),
            transcendentals=0,
        ),
        name=name,
    )(*[a for a, _, _ in ins], *after)


def sds(shape, dtype):
    return jax.ShapeDtypeStruct(shape, dtype)


def by_row(i, *_):
    return (i, 0)


def by_col(i, *_):
    return (0, i)


def by_first(i, *_):
    return (i, 0, 0)


def by_last(i, *_):
    return (0, 0, i)


def by_mid(i, *_):
    return (0, i, 0)


def exact_dot(a, b, dims=((1,), (0,))):
    return lax.dot_general(a, b, (dims, ((), ())), preferred_element_type=f32, precision=exact)


def dispatch_rows(dest, rows, send):
    hosts, cap, features = send.shape
    group = max(g for g in range(1, hosts + 1) if hosts % g == 0 and g * cap <= 640)

    def one(h, carry):
        slot = lax.broadcasted_iota(jnp.int32, (group * cap, dest.shape[1]), 0) + h * group * cap
        hits = [slot == dest[r : r + 1] for r in range(2)]
        if len(rows) == 1:
            hits = [hits[0] | hits[1]]
        total = None
        for hit, part in zip(hits, rows):
            term = nn(jnp.where(hit, 1.0, 0.0).astype(bf16), part[...])
            total = term if total is None else total + term
        send[pl.ds(h * group, group)] = total.astype(bf16).reshape(group, cap, features)
        return carry

    lax.fori_loop(0, hosts // group, one, 0)


def mid_kernel(att, x, wo, gain, wrm, prev, dest, res, normed, soft, send, low):
    i = pl.program_id(0)
    n_seq, wide, block = att.shape
    acc = x[...].astype(f32)
    for s in range(n_seq):
        acc = acc + tn(att[s], wo[s * wide : (s + 1) * wide])
    res[...] = acc
    scale = lax.rsqrt(jnp.mean(acc * acc, -1, keepdims=True) + epsilon)
    unit = acc * scale * gain[...]
    normed[...] = unit
    low[pl.ds(pl.multiple_of(i * block, block), block), :] = unit.astype(bf16)
    logits = exact_dot(unit, wrm[...]) + prev[...]
    lane = lax.broadcasted_iota(jnp.int32, logits.shape, 1)
    result = jnp.zeros_like(logits)
    for lo, hi in ((0, ROUTES), (ROUTES, ROUTES + 2), (ROUTES + 2, ROUTES + 4)):
        inside = (lane >= lo) & (lane < hi)
        part = jnp.where(inside, logits, masked_out)
        expo = jnp.where(inside, jnp.exp(part - jnp.max(part, -1, keepdims=True)), 0.0)
        result = result + expo / jnp.sum(expo, -1, keepdims=True)
    soft[...] = result

    @pl.when(i == pl.num_programs(0) - 1)
    def _():
        dispatch_rows(dest, (low,), send)


def prepare_kernel(got, win, win_t, gains, wrm, out):
    inner = win.shape[1]
    split = got.shape[1] - out.shape[2]
    for k in range(out.shape[0]):
        out[k] = got[:, split:]
    turned = got[:, :split].astype(f32).T
    win[...] = got[:, :inner]
    win_t[...] = turned[:inner].astype(bf16)
    gains[0:2] = turned[inner : inner + 2]
    gains[2:4] = turned[inner + 18 : inner + 20]
    gains[4:8] = jnp.zeros_like(gains[4:8])
    wrm[...] = got[:, inner + 2 : inner + 18].astype(f32)


def gate_parts(soft, routes):
    lane = lax.broadcasted_iota(jnp.int32, soft.shape, 1)
    hits = [(lane == routes[:, r : r + 1]).astype(f32) for r in range(2)]
    picked = [jnp.sum(h * soft, -1, keepdims=True) for h in hits]
    total = picked[0] + picked[1]
    gates = [p / total for p in picked]
    spread = gates[0] * hits[0] + gates[1] * hits[1]

    def lane_of(values, k):
        return values[:, k : k + 1]

    copy = lane_of(spread, EXPERTS + 1)
    const = [lane_of(spread, EXPERTS + 2 + c) for c in range(2)]
    mix = [[lane_of(soft, ROUTES + 2 * c + k) for k in range(2)] for c in range(2)]
    return lane, hits, total, gates, copy, const, mix


def loss_kernel(
    back, dest_col, dest, routes, soft, normed, res, teacher, valid, vectors, factor,
    out, grad, stats, send, squared, low0, low1,
):
    i = pl.program_id(0)
    block = res.shape[0]
    hosts, cap, features = back.shape
    rows = back[...].reshape(hosts * cap, features)
    slot = lax.broadcasted_iota(jnp.int32, (block, hosts * cap), 1)
    terms = [
        nn(jnp.where(slot == dest_col[:, r : r + 1], 1.0, 0.0).astype(bf16), rows)
        for r in range(2)
    ]
    lane, hits, total, gates, copy, const, mix = gate_parts(soft[...], routes[...])
    vec = [vectors[c : c + 1] for c in range(2)]
    unit = normed[...]
    full = res[...] + (copy + const[0] * mix[0][0] + const[1] * mix[1][0]) * unit
    full = full + (const[0] * mix[0][1]) * vec[0] + (const[1] * mix[1][1]) * vec[1]
    full = full + gates[0] * terms[0] + gates[1] * terms[1]
    out[...] = full.astype(bf16)
    ok = valid[...]
    differ = (full - teacher[...].astype(f32)) * ok
    gf = differ * factor[0, 0]
    grad[...] = gf
    here = pl.ds(pl.multiple_of(i * block, block), block)
    low0[here, :] = (gates[0] * gf).astype(bf16)
    low1[here, :] = (gates[1] * gf).astype(bf16)

    def over(values):
        return jnp.sum(gf * values, -1, keepdims=True)

    parts = [over(terms[0]), over(terms[1]), over(unit), over(vec[0]), over(vec[1])]
    tile = lax.broadcasted_iota(jnp.int32, stats.shape, 1)
    filled = jnp.zeros(stats.shape, f32)
    for k, part in enumerate(parts):
        filled = jnp.where(tile == k, part, filled)
    stats[...] = filled

    @pl.when(i == 0)
    def _():
        squared[...] = jnp.zeros_like(squared)

    squared[...] += jnp.sum(differ * differ, 0, keepdims=True)

    @pl.when(i == pl.num_programs(0) - 1)
    def _():
        dispatch_rows(dest, (low0, low1), send)


def route_kernel(soft, routes, stats, grad, normed, wrm, partial, small, small_vec):
    i = pl.program_id(0)
    probs = soft[...]
    lane, hits, total, gates, copy, const, mix = gate_parts(probs, routes[...])
    s = stats[...]
    dots = [s[:, k : k + 1] for k in range(5)]
    const_dot = [mix[c][0] * dots[2] + mix[c][1] * dots[3 + c] for c in range(2)]
    grad_gates = []
    for r in range(2):
        h = hits[r]
        grad_gates.append(
            dots[r]
            + h[:, EXPERTS + 1 : EXPERTS + 2] * dots[2]
            + h[:, EXPERTS + 2 : EXPERTS + 3] * const_dot[0]
            + h[:, EXPERTS + 3 : EXPERTS + 4] * const_dot[1]
        )
    mean = gates[0] * grad_gates[0] + gates[1] * grad_gates[1]
    grad_probs = sum(hits[r] * ((grad_gates[r] - mean) / total) for r in range(2))
    only = jnp.where(lane < ROUTES, probs, 0.0)
    both = only * (grad_probs - jnp.sum(only * grad_probs, -1, keepdims=True))
    for c in range(2):
        grad_mix = [const[c] * dots[2], const[c] * dots[3 + c]]
        inner = mix[c][0] * grad_mix[0] + mix[c][1] * grad_mix[1]
        for k in range(2):
            both = jnp.where(lane == ROUTES + 2 * c + k, mix[c][k] * (grad_mix[k] - inner), both)
    gf = grad[...]
    unit = normed[...]
    coef = copy + const[0] * mix[0][0] + const[1] * mix[1][0]
    partial[...] = coef * gf + exact_dot(both, wrm[...], ((1,), (1,)))
    spread = jnp.where(lane == 0, const[0] * mix[0][1], 0.0)
    spread = jnp.where(lane == 1, const[1] * mix[1][1], spread)

    @pl.when(i == 0)
    def _():
        small[...] = jnp.zeros_like(small)
        small_vec[...] = jnp.zeros_like(small_vec)

    small[...] += exact_dot(unit, both, ((0,), (0,)))
    small_vec[...] += exact_dot(gf, spread, ((0,), (0,)))


def join_kernel(
    back, dest_col, partial, res, grad, gain, wo, mid, branch, out, gain_grad
):
    i = pl.program_id(0)
    block = res.shape[0]
    hosts, cap, features = back.shape
    rows = back[...].reshape(hosts * cap, features)
    slot = lax.broadcasted_iota(jnp.int32, (block, hosts * cap), 1)
    hit = (slot == dest_col[:, 0:1]) | (slot == dest_col[:, 1:2])
    grad_normed = partial[...] + nn(jnp.where(hit, 1.0, 0.0).astype(bf16), rows)
    r = res[...]
    scale = lax.rsqrt(jnp.mean(r * r, -1, keepdims=True) + epsilon)
    unit = r * scale

    @pl.when(i == 0)
    def _():
        gain_grad[...] = jnp.zeros_like(gain_grad)

    gain_grad[...] += jnp.sum(grad_normed * unit, 0, keepdims=True)
    hat = grad_normed * gain[...]
    total = grad[...] + scale * (hat - unit * jnp.mean(hat * unit, -1, keepdims=True))
    mid[...] = total
    low = total.astype(bf16)
    branch[...] = low
    n_seq, wide, _ = out.shape
    for s in range(n_seq):
        out[s] = nt(wo[s * wide : (s + 1) * wide], low).astype(bf16)


def out_grad_kernel(att, branch, out):
    n_seq, wide, _ = att.shape
    for s in range(n_seq):
        out[s * wide : (s + 1) * wide] = nn(att[s], branch[...]).astype(bf16)


def whole_tile(me, parts, tile):
    far, core = me[0], me[1]
    for part, f, c in zip(parts, (far, 1 - far, far, 1 - far), (core, core, 1 - core, 1 - core)):
        tile[pl.ds(f, 1), :, pl.ds(c, 1)] = part[None, :, None]
    return tile[...].reshape(-1, tile.shape[-1])


def pick_kernel(index, *refs):
    shards, same, other = refs[:-2], refs[-2], refs[-1]
    for k, shard in enumerate(shards):
        same[k] = shard[index[0]]
        other[k] = shard[1 - index[0]]


def total_kernel(n_small, parts, share, gin, gout, router, mix, small, vectors, loss, gain_first, gain_mid):
    total = jnp.sum(parts[...].astype(f32), 0)
    features = gout.shape[1]
    wide = HEAD * (features // HEAD // 4)
    for s in range(features // wide):
        for k in range(3):
            at = (3 * s + k) * wide
            gin[:, k * features + s * wide : k * features + (s + 1) * wide] = total[:, at : at + wide]
    gout[...] = total[:, 3 * features : 4 * features]
    tail = total[:, 4 * features :]
    both = tail[:, :n_small] + tail[:, n_small : 2 * n_small]
    n_pad = small.shape[0]
    unit = lax.broadcasted_iota(jnp.int32, (n_pad, tail.shape[1]), 0)
    unit = (unit == lax.broadcasted_iota(jnp.int32, unit.shape, 1)).astype(f32)
    wide_both = tail + jnp.concatenate([tail[:, n_small:], tail[:, :n_small]], 1)
    small[...] = exact_dot(unit, wide_both, ((1,), (1,)))
    vectors[...] = small[18:20]
    loss[...] = small[20:21, 0:1] * share[...]
    gain_first[...] = small[0:1]
    gain_mid[...] = small[1:2]
    router[...] = both[:, 2 : 2 + ROUTES]
    mix[...] = both[:, 2 + ROUTES : 6 + ROUTES]


def in_sum_kernel(gate, gate_given, up, up_given, out):
    for k, (own, given) in enumerate(((gate, gate_given), (up, up_given))):
        out[:, k] = (own[...].astype(f32) + given[...].astype(f32)).astype(bf16)


def part_kernel(which, part, same, other):
    same[...] = part[which[0]]
    other[...] = part[1 - which[0]]


def owner_kernel(which, same, alike, unlike, *outs):
    mine = jnp.where(which[1] == 1, same[...], alike[...]).astype(f32)
    theirs = unlike[...].astype(f32)
    height = outs[0].shape[1]
    for k, out in enumerate(outs):
        here = slice(k * height, (k + 1) * height)
        out[which[0]] = mine[here]
        out[1 - which[0]] = theirs[here]


def cross_kernel(which, same, alike, unlike, out):
    @pl.when(which[1] == 1)
    def _():
        out[pl.ds(which[0], 1)] = same[...][None]

    @pl.when(which[1] != 1)
    def _():
        out[pl.ds(which[0], 1)] = alike[...][None]

    out[pl.ds(1 - which[0], 1)] = unlike[...][None]


def split_tile(me, values, tile):
    tile[...] = values.reshape(tile.shape)
    return tile[:, pl.ds(me[1], 1)][:, 0], tile[:, pl.ds(1 - me[1], 1)][:, 0]


def expert_hidden_kernel(
    me, rows, near, far, near_other, far_other, gate_part, up_part, hidden, gate, up
):
    parts = (near, far, near_other, far_other)
    w_gate = whole_tile(me, [p[:, 0] for p in parts], gate)
    w_up = whole_tile(me, [p[:, 1] for p in parts], up)
    step = rows.shape[0] // 2
    for k in range(2):
        here = slice(k * step, (k + 1) * step)
        g = nn(rows[here], w_gate)
        u = nn(rows[here], w_up)
        gate_part[here] = g
        up_part[here] = u
        hidden[here] = (g / (1.0 + jnp.exp(-g)) * u).astype(bf16)


def expert_result_kernel(me, hidden, near, far, near_other, far_other, result, down):
    @pl.when(pl.program_id(0) == 0)
    def _():
        whole_tile(me, [p[...] for p in (near, far, near_other, far_other)], down)

    result[...] = nn(hidden[...], down[...].reshape(-1, down.shape[-1])).astype(bf16)


def down_grad_kernel(me, hidden, grad, own, other, parts):
    own[...], other[...] = split_tile(me, tn(hidden[...], grad[...]).astype(bf16), parts)


def expert_backward_kernel(
    me, grad, gate_part, up_part, near, far, near_other, far_other,
    down_near, down_far, down_near_other, down_far_other,
    d_gate, d_up, result, gate, up, down, acc,
):
    f = pl.program_id(0)

    @pl.when(f == 0)
    def _():
        pieces = (down_near, down_far, down_near_other, down_far_other)
        whole_tile(me, [p[...] for p in pieces], down)

    w_down = down[f // 2, f % 2].reshape(-1, down.shape[-1])
    weights = (near, far, near_other, far_other)
    w_gate = whole_tile(me, [p[:, 0] for p in weights], gate)
    w_up = whole_tile(me, [p[:, 1] for p in weights], up)

    @pl.when(f == 0)
    def _():
        acc[...] = jnp.zeros_like(acc)

    step = grad.shape[0] // 2
    for k in range(2):
        here = slice(k * step, (k + 1) * step)
        gh = nt(grad[here], w_down)
        g = gate_part[here]
        sig = 1.0 / (1.0 + jnp.exp(-g))
        silu = g * sig
        dg = (gh * up_part[here] * (sig + silu * (1.0 - sig))).astype(bf16)
        du = (gh * silu).astype(bf16)
        d_gate[here] = dg
        d_up[here] = du
        acc[here] += nt(dg, w_gate) + nt(du, w_up)

    @pl.when(f == pl.num_programs(0) - 1)
    def _():
        result[...] = acc[...].astype(bf16)


def in_grad_kernel(me, rows, d, own, other, parts, turned):
    @pl.when(pl.program_id(0) == 0)
    def _():
        turned[...] = rows[...].astype(f32).T.astype(bf16)

    own[...], other[...] = split_tile(me, nn(turned[...], d[...]).astype(bf16), parts)


def seq_add_kernel(keep, given, near, far):
    near[...] = keep[0] + given[0].astype(f32)
    far[...] = (keep[1] + given[1].astype(f32)).astype(bf16)


def finish_kernel(near, given, mid, x, gain, out):
    grad = near[...] + given[...].astype(f32)
    values = x[...].astype(f32)
    scale = lax.rsqrt(jnp.mean(values * values, -1, keepdims=True) + epsilon)
    unit = values * scale
    hat = grad * gain[...]
    out[...] = mid[...] + scale * (hat - unit * jnp.mean(hat * unit, -1, keepdims=True))


def exchange(blocks, axes):
    return lax.all_to_all(blocks, axes, split_axis=0, concat_axis=0, tiled=True)


def to_all(block, count):
    return exchange(jnp.broadcast_to(block[None], (count,) + block.shape), ALL)


def gather_seq(block, size):
    held = block[None]
    step = size // 2
    while step > 1:
        pairs = [(i, i ^ step) for i in range(size)]
        held = jnp.concatenate([held, lax.ppermute(held, SEQ, pairs)], 0)
        step //= 2
    held = (held, lax.ppermute(held, SEQ, [(i, i ^ 1) for i in range(size)]))
    order = [0]
    step = size // 2
    while step:
        order = order + [k ^ step for k in order]
        step //= 2
    return held, order


def body(
    block_input,
    teacher,
    prev_logits,
    valid_mask,
    segments,
    routes,
    input_proj,
    output_proj,
    attention_gain,
    mixture_gain,
    router,
    const_mix,
    const_vectors,
    expert_gate,
    expert_up,
    expert_down,
):
    n_out, n_in, n_seq = (lax.axis_size(a) for a in (OUTER, "d", SEQ))
    n_all = n_out * n_in * n_seq
    n_far = lax.axis_size("a")
    tokens_here, features = block_input.shape
    rows_here = input_proj.shape[0]
    wide = features // n_seq
    seq_id = lax.axis_index(SEQ)

    a_id, b_id, d_id, c_id = (lax.axis_index(x) for x in ("a", "b", "d", "sc"))
    me = jnp.stack([a_id * (n_far == 2), c_id])
    swap = [(0, 1), (1, 0)]
    cross = [(1, 2), (2, 1)]

    def item(values, index):
        return lax.dynamic_index_in_dim(values, index, 0, keepdims=False)

    def in_order(index, mine, given):
        return jnp.where(index == 0, jnp.stack([mine, given]), jnp.stack([given, mine]))

    which = jnp.stack([b_id, (c_id == d_id).astype(jnp.int32)])

    place = [(b, d, c) for b in range(2) for d in range(2) for c in range(2)]
    alike = [(4 * b + 2 * d + c, 4 * b + 2 * c + d) for b, d, c in place if d != c]
    unlike = [(4 * b + 2 * d + c, 4 * (1 - b) + 2 * c + d) for b, d, c in place]

    def crossed(same, other):
        same = jnp.where(c_id == d_id, same, lax.ppermute(same, ("b", "d", "sc"), alike))
        return in_order(b_id, same, lax.ppermute(other, ("b", "d", "sc"), unlike))

    def cross(same, other, after):
        given = [lax.ppermute(same, ("b", "d", "sc"), alike)]
        given.append(lax.ppermute(other, ("b", "d", "sc"), unlike))
        count, height, width = same.shape
        quarter = width // (4 if width % 512 == 0 else 2)
        block = ((count, height, quarter), by_last)
        pair, _ = call(
            cross_kernel,
            "cross",
            2,
            (width // quarter,),
            [(which, None, None)] + [(x,) + block for x in [same] + given],
            [(sds((2,) + same.shape, bf16), (2,) + block[0], lambda i, *_: (0, 0, 0, i))],
            prefetch=1,
            after=after,
        )
        return pair

    def far_pair(pair):
        return lax.all_gather(pair, "a", axis=0, tiled=False)

    def far_parts(far, done):
        if n_far == 2:
            far = item(far, 1 - a_id)
        far = far + done[0, 0].astype(bf16)
        return far, lax.ppermute(far, "sc", swap)

    def core_sum(own, other, done=None):
        total = own.astype(f32) + lax.ppermute(other, "sc", swap).astype(f32)
        if done is not None:
            total = total + done[0, 0]
        return total.astype(bf16).reshape((n_far, 2) + own.shape[1:])

    def far_sum(part):
        return lax.psum_scatter(part, "a", scatter_dimension=0, tiled=False)

    def to_owner(part, after):
        _, height, width = part.shape
        steps = 4 if width % 512 == 0 else 2
        one = ((height, width // steps), by_col)
        same, other, done = call(
            part_kernel,
            "part",
            3,
            (steps,),
            [(which, None, None), (part, (2, height, width // steps), by_last)],
            [(sds((height, width), bf16),) + one] * 2,
            prefetch=1,
            after=after,
        )
        given = [
            lax.ppermute(same, ("b", "d", "sc"), alike),
            lax.ppermute(other, ("b", "d", "sc"), unlike),
        ]

        def kept(count, after):
            shape = (2, height // count, width)
            return call(
                owner_kernel,
                "owner",
                4,
                (steps,),
                [(which, None, None)] + [(x,) + one for x in [same] + given],
                [(sds(shape, f32), shape[:2] + (width // steps,), by_last)] * count,
                prefetch=1,
                after=after,
            )

        return kept, done

    slice_rows = expert_gate.shape[1]

    def regroup(near, far, near_other, far_other):
        if n_far == 2:
            return near, far, near_other, far_other
        pair = in_order(c_id, far, far_other).transpose(3, 1, 2, 0, 4, 5)
        pair = pair.reshape(pair.shape[:1] + (2, 2, 2, -1) + pair.shape[5:])
        pair = pair.transpose(1, 3, 2, 0, 4, 5)
        return tuple(item(pair[f], c) for c in (c_id, 1 - c_id) for f in range(2))

    def owner_slices(own, other):
        if n_far == 2:
            return own, other
        pair = in_order(c_id, own, other).transpose(2, 1, 0, 3, 4)
        pair = pair.reshape(pair.shape[:1] + (n_out, 2, -1) + pair.shape[4:])
        pair = pair.transpose(2, 1, 0, 3, 4)
        return item(pair, c_id), item(pair, 1 - c_id)

    def pick(shards, after=()):
        _, height, width = shards[0].shape
        quarter = width // (4 if width % 512 == 0 else 2)
        block = ((2, height, quarter), by_last)
        out_block = ((len(shards), height, quarter), by_last)
        return call(
            pick_kernel,
            "pick",
            3,
            (width // quarter,),
            [(b_id.reshape(1), None, None)] + [(x,) + block for x in shards],
            [(sds((len(shards), height, width), bf16),) + out_block] * 2,
            prefetch=1,
            after=after,
        )

    same_in, other_in, picked = pick([expert_gate, expert_up])
    seg_row = jnp.pad(segments.astype(bf16), (0, features * 2 - tokens_here)).reshape(2, features)
    with_seg = jnp.concatenate(
        [block_input, jnp.pad(seg_row, ((0, 14), (0, 0)))], 0
    )
    held, order = gather_seq(with_seg, n_seq)
    where = [order.index(j) for j in range(n_seq)]
    chosen = jnp.array(where, jnp.int32)[jnp.arange(n_seq) ^ seq_id]
    length = n_seq * tokens_here
    seg_rows = [h[:, tokens_here : tokens_here + 2] for h in held]
    seq_segments = (
        jnp.concatenate(seg_rows, 0)
        .reshape(n_seq, 2 * features)[:, :tokens_here][chosen]
        .reshape(1, -1)
    )
    positions = jnp.arange(length, dtype=jnp.int32)[None]
    fresh = seq_segments != jnp.pad(seq_segments[:, :-1], ((0, 0), (1, 0)), constant_values=-1)
    start = lax.cummax(jnp.where(fresh, positions, 0), axis=1)

    flat_routes = routes.reshape(-1)
    onehot_e = (flat_routes[:, None] == jnp.arange(EXPERTS, dtype=jnp.int32)[None, :]).astype(
        jnp.int32
    )
    slot_rank = jnp.sum((jnp.cumsum(onehot_e, 0) - onehot_e) * onehot_e, -1)
    host = (flat_routes % 2) * 4 + flat_routes // 2 % 2 * 2 + flat_routes // 4
    slot_dest = jnp.where(flat_routes < EXPERTS, host * CAP + slot_rank, EXPERTS * CAP)
    slot_dest = slot_dest.reshape(tokens_here, 2)
    slot_row = jnp.pad(slot_dest.T, ((0, 6), (0, 0)))

    in_pair = cross(same_in, other_in, [held[1], start, slot_row])
    in_far = far_pair(in_pair)
    in_other = lax.ppermute(in_pair, "sc", swap)

    same_down, other_down, _ = pick([expert_down], [in_pair])

    own_cols = (input_proj + picked[0, 0].astype(bf16)).reshape(rows_here, 3, n_seq, wide)
    own_cols = own_cols.transpose(0, 2, 1, 3).reshape(rows_here, -1)
    count_here = jnp.sum(valid_mask)
    count_cols = jnp.stack([count_here // 32, count_here % 32]).astype(bf16)
    small = jnp.concatenate(
        [
            attention_gain[:, None],
            mixture_gain[:, None],
            router,
            const_mix,
            const_vectors.T,
            jnp.broadcast_to(count_cols[None], (rows_here, 2)),
        ],
        1,
    )
    n_small = small.shape[1]
    small = jnp.pad(small, ((0, 0), (0, -(3 * wide + n_small) % 128)))
    packed = jnp.concatenate(
        [
            own_cols.reshape(rows_here, n_seq, 3 * wide).transpose(1, 0, 2),
            jnp.broadcast_to(small[None], (n_seq,) + small.shape),
        ],
        2,
    )
    n_plane = n_in * n_seq
    piece = features // n_plane
    out_piece = output_proj.reshape(rows_here, n_in, n_seq, piece).transpose(1, 2, 0, 3)
    inner = packed.shape[2]
    packed = jnp.concatenate(
        [jnp.broadcast_to(packed[None], (n_in,) + packed.shape), out_piece], 3
    )
    packed = jnp.pad(packed, ((0, 0),) * 3 + ((0, -packed.shape[3] % 128),))
    packed = jnp.broadcast_to(packed[None], (n_out,) + packed.shape)
    got = exchange(packed.reshape((n_all,) + packed.shape[3:]), ALL)
    counts = got[:, 0, 3 * wide + 20 : 3 * wide + 22].astype(f32)
    valid_count = jnp.sum(counts[:, 0]) * 32.0 + jnp.sum(counts[:, 1])
    got = got.reshape(features, -1)
    own_in, own_in_t, gains, wrm, out_cols, prepared = call(
        prepare_kernel,
        "prepare",
        3,
        (1,),
        [(got, None, None)],
        [
            (sds((features, 3 * wide), bf16), None, None),
            (sds((3 * wide, features), bf16), None, None),
            (sds((8, features), f32), None, None),
            (sds((features, ROUTES + 4), f32), None, None),
            (sds((n_plane, features, got.shape[1] - inner), bf16), None, None),
        ],
    )
    gain_first, gain_mid, vectors_f = gains[0:1], gains[1:2], gains[2:4]
    full_out = exchange(out_cols, PLANE)[:, :, :piece].transpose(1, 0, 2)
    full_out = full_out.reshape(features, features)

    seq_inputs, normed_first, attended, attended_t, log_totals, *heads_saved, forward_done = attend_forward(
        chosen, held, gain_first, own_in, own_in_t, start, tokens_here,
        [in_other],
    )
    attended_tok = exchange(attended, SEQ)

    down_pair = cross(same_down, other_down, [normed_first])
    down_far = far_pair(down_pair)
    down_other = lax.ppermute(down_pair, "sc", swap)

    whole = (None, None)
    rows_block = 128
    steps = (tokens_here // rows_block,)
    wide_block = ((rows_block, features), by_row)
    soft_block = ((rows_block, ROUTES + 4), by_row)
    pair_block = ((rows_block, 2), by_row)
    slots_shape = (EXPERTS, CAP, features)
    tok = sds((tokens_here, features), f32)
    residual_mid, normed, soft, send_rows, mid_done = call(
        mid_kernel,
        "mid",
        10,
        steps,
        [
            (attended_tok, (n_seq, wide, rows_block), by_last),
            (block_input,) + wide_block,
            (full_out,) + whole,
            (gain_mid,) + whole,
            (wrm,) + whole,
            (jnp.pad(prev_logits, ((0, 0), (0, 4))),) + soft_block,
            (slot_row,) + whole,
        ],
        [
            (tok,) + wide_block,
            (tok,) + wide_block,
            (sds((tokens_here, ROUTES + 4), f32),) + soft_block,
            (sds(slots_shape, bf16),) + whole,
        ],
        [pltpu.VMEM((tokens_here, features), bf16)],
        after=[down_other, in_far],
    )
    in_far, in_far_other = far_parts(in_far, mid_done)
    in_parts_w = regroup(in_pair, in_far, in_other, in_far_other)
    recv_rows = exchange(send_rows, ROWS).reshape(-1, features)
    n_rows = recv_rows.shape[0]
    hid = expert_gate.shape[2]
    tile = 512 if hid % 512 == 0 else hid
    tiles = (hid // tile,)
    _, _, piece_rows, _ = in_parts_w[0].shape
    w_part = ((2, 2, piece_rows, tile), lambda i, *_: (0, 0, 0, i))
    w_tile = pltpu.VMEM((2, 2, 2, piece_rows, tile), bf16)
    h_col = ((n_rows, tile), by_col)
    in_parts = [(w,) + w_part for w in in_parts_w]
    gate_part, up_part, hidden, hidden_done = call(
        expert_hidden_kernel,
        "expert_hidden",
        14,
        tiles,
        [(me,) + whole, (recv_rows,) + whole] + in_parts,
        [
            (sds((n_rows, hid), f32),) + h_col,
            (sds((n_rows, hid), f32),) + h_col,
            (sds((n_rows, hid), bf16),) + h_col,
        ],
        [w_tile] * 2,
        prefetch=1,
    )
    down_far, down_far_other = far_parts(down_far, hidden_done)
    down_parts_w = [p[:, 0] for p in regroup(down_pair, down_far, down_other, down_far_other)]
    far_rows = down_parts_w[0].shape[1]
    down_tile = pltpu.VMEM((2, 2, 2, far_rows, features), bf16)
    row_tile = n_rows // 4
    result_rows, _ = call(
        expert_result_kernel,
        "expert_result",
        8,
        (4,),
        [
            (me,) + whole,
            (hidden, (row_tile, hid), by_row),
        ]
        + [(p,) + whole for p in down_parts_w],
        [(sds((n_rows, features), bf16), (row_tile, features), by_row)],
        [down_tile],
        prefetch=1,
    )
    back_rows = exchange(result_rows.reshape(slots_shape), ROWS)
    valid_f = valid_mask.astype(f32)[:, None]
    factor = (tokens_here * n_all / valid_count).reshape(1, 1)
    full_output, grad_full, stats, grad_send, squared, _ = call(
        loss_kernel,
        "loss",
        11,
        steps,
        [
            (back_rows,) + whole,
            (slot_dest,) + pair_block,
            (slot_row,) + whole,
            (routes,) + pair_block,
            (soft,) + soft_block,
            (normed,) + wide_block,
            (residual_mid,) + wide_block,
            (teacher,) + wide_block,
            (valid_f, (rows_block, 1), by_row),
            (vectors_f,) + whole,
            (factor,) + whole,
        ],
        [
            (sds((tokens_here, features), bf16),) + wide_block,
            (tok,) + wide_block,
            (sds((tokens_here, 8), f32), (rows_block, 8), by_row),
            (sds(slots_shape, bf16),) + whole,
            (sds((1, features), f32),) + whole,
        ],
        [pltpu.VMEM((tokens_here, features), bf16)] * 2,
    )
    grad_recv = exchange(grad_send, ROWS).reshape(-1, features)
    partial_normed, small_cols, vector_cols, route_done = call(
        route_kernel,
        "route",
        14,
        steps,
        [
            (soft,) + soft_block,
            (routes,) + pair_block,
            (stats, (rows_block, 8), by_row),
            (grad_full,) + wide_block,
            (normed,) + wide_block,
            (wrm,) + whole,
        ],
        [
            (tok,) + wide_block,
            (sds((features, ROUTES + 4), f32),) + whole,
            (sds((features, ROUTES + 4), f32),) + whole,
        ],
    )

    d_gate, d_up, grad_rows, backward_done = call(
        expert_backward_kernel,
        "expert_backward",
        20,
        tiles,
        [
            (me,) + whole,
            (grad_recv,) + whole,
            (gate_part,) + h_col,
            (up_part,) + h_col,
        ]
        + in_parts
        + [(p,) + whole for p in down_parts_w],
        [(sds((n_rows, hid), bf16),) + h_col] * 2
        + [(sds((n_rows, features), bf16),) + whole],
        [w_tile] * 2 + [down_tile, pltpu.VMEM((n_rows, features), f32)],
        prefetch=1,
        after=[partial_normed],
    )
    grad_back = exchange(grad_rows.reshape(slots_shape), ROWS)
    def in_grad(name, d, after):
        shape = (4, piece_rows, tile)
        out = (sds((4, piece_rows, hid), bf16), shape, by_last)
        *grads, _ = call(
            in_grad_kernel,
            name,
            8,
            tiles,
            [(me,) + whole, (recv_rows,) + whole, (d,) + h_col],
            [out] * 2,
            [
                pltpu.VMEM((4, 2, piece_rows, tile), bf16),
                pltpu.VMEM((features, n_rows), bf16),
            ],
            prefetch=1,
            after=after,
        )
        return grads

    gate_grads = in_grad("gate_grad", d_gate, [grad_rows])
    up_grads = in_grad("up_grad", d_up, [gate_grads[0]])
    *down_grads, _ = call(
        down_grad_kernel,
        "down_grad",
        8,
        tiles,
        [(me,) + whole, (hidden,) + h_col, (grad_recv,) + whole],
        [(sds((4, far_rows, features), bf16), (1, far_rows, features), by_first)] * 2,
        [pltpu.VMEM((1, 2, far_rows, features), bf16)],
        prefetch=1,
        after=[up_grads[0]],
    )

    pairs = [owner_slices(*(q[:, None] for q in pair)) for pair in (gate_grads, up_grads)]
    terms = [x[:, 0] for own, other in pairs for x in (own, lax.ppermute(other, "sc", swap))]
    in_sum, _ = call(
        in_sum_kernel,
        "in_sum",
        4,
        (4,),
        [(x, (n_out // 4, slice_rows, hid), by_first) for x in terms],
        [
            (
                sds((n_out, 2, slice_rows, hid), bf16),
                (n_out // 4, 2, slice_rows, hid),
                lambda i, *_: (i, 0, 0, 0),
            )
        ],
        after=[down_grads[0]],
    )
    in_part = far_sum(in_sum.reshape(n_far, 2, 2 * slice_rows, hid))
    grad_mid, grad_branch, grad_attended, grad_mixture_gain, join_done = call(
        join_kernel,
        "join",
        8,
        steps,
        [
            (grad_back,) + whole,
            (slot_dest,) + pair_block,
            (partial_normed,) + wide_block,
            (residual_mid,) + wide_block,
            (grad_full,) + wide_block,
            (gain_mid,) + whole,
            (full_out,) + whole,
        ],
        [
            (tok,) + wide_block,
            (sds((tokens_here, features), bf16),) + wide_block,
            (sds((n_seq, wide, tokens_here), bf16), (n_seq, wide, rows_block), by_last),
            (sds((1, features), f32),) + whole,
        ],
        after=[in_sum],
    )
    grad_output_proj, out_done = call(
        out_grad_kernel,
        "out_grad",
        3,
        (1,),
        [(attended_tok,) + whole, (grad_branch,) + whole],
        [(sds((features, features), bf16),) + whole],
        after=[in_sum],
    )
    down_sum = core_sum(*owner_slices(*(p[:, None] for p in down_grads)), out_done)
    down_part = far_sum(down_sum)[:, 0]
    grad_heads = exchange(grad_attended, SEQ)

    def plane_blocks(part):
        return part.reshape(n_out, n_plane, rows_here, -1).transpose(1, 0, 2, 3)

    out_blocks = plane_blocks(grad_output_proj)
    out_grad = jnp.sum(exchange(out_blocks, PLANE).astype(f32), 0).astype(bf16)

    small_grads = jnp.concatenate(
        [
            jnp.zeros((features, 1), f32),
            grad_mixture_gain.T,
            small_cols,
            vector_cols[:, :2],
            jnp.broadcast_to(jnp.sum(squared), (features, 1)),
        ],
        1,
    )
    n_small = small_grads.shape[1]

    def two_parts(values, axis):
        high = values.astype(bf16)
        rest = (values - high.astype(f32)).astype(bf16)
        both = jnp.concatenate([high, rest], axis)
        return both

    small_low = two_parts(small_grads, 1)
    small_low = jnp.pad(small_low, ((0, 0), (0, -(3 * wide + 2 * n_small) % 128)))
    keep, sent, last, attention_done = attend_backward(
        chosen, grad_heads, attended_t, log_totals, *heads_saved, start, seq_inputs, normed_first,
        own_in, small_low, [out_blocks, down_sum],
    )

    sent = lax.ppermute(sent, SEQ, [(i, i ^ 1) for i in range(n_seq)])
    near, sent, added = call(
        seq_add_kernel,
        "seq_add",
        3,
        (2,),
        [
            (keep, (2, tokens_here // 2, features), by_mid),
            (sent, (2, tokens_here // 2, features), by_mid),
        ],
        [
            (tok, (tokens_here // 2, features), by_row),
            (sds((tokens_here, features), bf16), (tokens_here // 2, features), by_row),
        ],
    )
    kept_in, parted = to_owner(in_part, [near])
    sent = lax.ppermute(sent, SEQ, [(i, i ^ 2) for i in range(n_seq)])
    grad_input, finished = call(
        finish_kernel,
        "finish",
        3,
        steps,
        [
            (near,) + wide_block,
            (sent,) + wide_block,
            (grad_mid,) + wide_block,
            (block_input,) + wide_block,
            (gain_first,) + whole,
        ],
        [(tok,) + wide_block],
        after=[parted],
    )

    grad_expert_gate, grad_expert_up, owned = kept_in(2, [])
    last = last + (finished[0, 0] + owned[0, 0]).astype(bf16)
    last = exchange(plane_blocks(last), PLANE)
    kept_down, _ = to_owner(down_part, [grad_expert_gate])
    cols = last[:, :, :, : 3 * wide].reshape(n_in, n_seq, n_out, rows_here, 3 * wide)
    cols = jnp.sum(cols.astype(f32), 0).astype(bf16).transpose(1, 2, 0, 3)
    rest = jnp.sum(last[:, :, :, 3 * wide : 3 * wide + 2 * n_small].astype(f32), 0)
    rest = rest[:, :, :n_small] + rest[:, :, n_small:]
    last = jnp.concatenate(
        [cols.reshape(n_out, rows_here, -1), out_grad, two_parts(rest, 2)], 2
    )
    last = jnp.pad(last, ((0, 0), (0, 0), (0, -last.shape[2] % 128)))
    loss_share = 1.0 / (2.0 * features * valid_count)
    *last, _, grad_const_vectors, mean_loss, gain_first_row, gain_mid_row, _ = call(
        functools.partial(total_kernel, n_small),
        "total",
        2,
        (1,),
        [(exchange(last, OUTER),) + whole, (loss_share.reshape(1, 1),) + whole],
        [
            (sds((rows_here, 3 * features), f32),) + whole,
            (sds((rows_here, features), f32),) + whole,
            (sds((rows_here, ROUTES), f32),) + whole,
            (sds((rows_here, 4), f32),) + whole,
            (sds((24, rows_here), f32),) + whole,
            (sds((2, rows_here), f32),) + whole,
            (sds((1, 1), f32),) + whole,
            (sds((1, rows_here), f32),) + whole,
            (sds((1, rows_here), f32),) + whole,
        ],
    )
    grad_expert_down, _ = kept_down(1, [mean_loss])
    grad_input_proj, grad_output_proj, grad_router, grad_const_mix = last
    return (
        full_output,
        mean_loss.reshape(()),
        grad_input,
        grad_input_proj,
        grad_output_proj,
        gain_first_row.reshape(-1),
        gain_mid_row.reshape(-1),
        grad_router,
        grad_const_mix,
        grad_const_vectors,
        grad_expert_gate,
        grad_expert_up,
        grad_expert_down,
    )


def solution(mesh):
    cut = Mesh(mesh.devices.reshape(-1, 2, 2, 2, mesh.shape["seq"] // 2), ALL)
    rows = P(ALL, None)
    line = P(ALL)
    cols = P(None, ALL)
    expert = P(SEQ, OUTER + ("d",), None)
    return jax.shard_map(
        body,
        mesh=cut,
        in_specs=(rows, rows, rows, line, line, rows, rows, rows, line, line, rows, rows, cols)
        + (expert,) * 3,
        out_specs=(rows, P(), rows, rows, rows, line, line, rows, rows, cols) + (expert,) * 3,
        check_vma=False,
    )
```

```python
import functools

import jax
import jax.numpy as jnp
import numpy as np
from jax import lax
from jax.experimental import pallas as pl
from jax.experimental.pallas import tpu as pltpu
from jax.sharding import Mesh, PartitionSpec as P

HEAD = 64
EXPERTS = 8
ROUTES = 12
CAP = 160
BLK = 512

OUTER = ("a", "b")
SEQ = ("sx", "sc")
ALL = OUTER + ("d",) + SEQ
PLANE = ("d",) + SEQ
ROWS = ("b", "d", "sx")

exact = lax.Precision.HIGHEST
epsilon = 1e-06
masked_out = -1e30
bf16 = jnp.bfloat16
f32 = jnp.float32


def rms_scale(values):
    return lax.rsqrt(jnp.mean(values * values, -1, keepdims=True) + epsilon)


def dot_rows(left, right, precision=None):
    return lax.dot_general(
        left,
        right,
        (((0,), (0,)), ((), ())),
        preferred_element_type=jnp.float32,
        precision=precision,
    )


def dot_last(left, right, precision=None):
    return lax.dot_general(
        left,
        right,
        (((1,), (1,)), ((), ())),
        preferred_element_type=jnp.float32,
        precision=precision,
    )


def nt(a,b): return lax.dot_general(a,b,(((1,),(1,)),((),())),preferred_element_type=f32)
def nn(a,b): return jnp.dot(a,b,preferred_element_type=f32)
def tn(a,b): return lax.dot_general(a,b,(((0,),(0,)),((),())),preferred_element_type=f32)

def fwd_kernel(tbl, held, held_far, gain, win, winT, start, inputs, normed, att, oT, lse, qn, kn, vn, qT, kT, kbuf, vbuf):
    i=pl.program_id(0)
    wide=win.shape[1]//3
    heads=wide//HEAD
    per=held.shape[1]//BLK
    t=tbl[i//per]
    off=pl.multiple_of((i%per)*BLK,BLK)
    half = held.shape[0]

    @pl.when(t < half)
    def _():
        inputs[...] = held[t, pl.ds(off, BLK), :]

    @pl.when(t >= half)
    def _():
        inputs[...] = held_far[t - half, pl.ds(off, BLK), :]

    x = inputs[...].astype(f32)
    scale=lax.rsqrt(jnp.mean(x*x,-1,keepdims=True)+epsilon)
    nb=(x*scale*gain[...]).astype(bf16)
    normed[...]=nb
    proj=nn(nb,win[...]).astype(bf16)
    projT=nt(winT[...],nb).astype(bf16)
    qs=projT[:wide]*bf16(HEAD ** -0.5)
    qT[...]=qs
    kT[...]=projT[wide:2*wide]
    vbuf[i]=projT[2*wide:]
    for h in range(heads):
        qn[h]=proj[:,h*HEAD:(h+1)*HEAD]*bf16(HEAD ** -0.5)
        kh=proj[:,wide+h*HEAD:wide+(h+1)*HEAD]
        kn[h]=kh
        kbuf[i,h]=kh
        vn[h]=proj[:,2*wide+h*HEAD:2*wide+(h+1)*HEAD]
    rows=lax.broadcasted_iota(jnp.int32,(BLK,BLK),0)
    cols=lax.broadcasted_iota(jnp.int32,(BLK,BLK),1)
    first=start[...]
    def tile(j,h,mask):
        s=nn(kbuf[j,h],qs[h*HEAD:(h+1)*HEAD])
        return jnp.where(mask,s,masked_out)
    mask=(rows+i*BLK>=first)&(rows<=cols)
    state=[]
    for h in range(heads):
        s=tile(i,h,mask)
        m=jnp.max(s,0,keepdims=True)
        e=jnp.exp(s-m)
        l=jnp.sum(e,0,keepdims=True)
        o=nn(vbuf[i,h*HEAD:(h+1)*HEAD],e.astype(bf16))
        state.append((m,l,o))
    def step(j,state):
        mask=rows+j*BLK>=first
        new=[]
        for h in range(heads):
            m,l,o=state[h]
            s=tile(j,h,mask)
            n=jnp.maximum(m,jnp.max(s,0,keepdims=True))
            a=jnp.exp(m-n)
            e=jnp.exp(s-n)
            l=l*a+jnp.sum(e,0,keepdims=True)
            o=o*a+nn(vbuf[j,h*HEAD:(h+1)*HEAD],e.astype(bf16))
            new.append((n,l,o))
        return tuple(new)
    state=lax.fori_loop(0,i,step,tuple(state))
    for h in range(heads):
        m,l,o=state[h]
        o=o/l
        oT[h*HEAD:(h+1)*HEAD]=o
        att[0,h*HEAD:(h+1)*HEAD]=o.astype(bf16)
        lse[h:h+1]=m+jnp.log(l)
    lse[heads:]=jnp.zeros((lse.shape[0]-heads,BLK),f32)

def attend_forward(table, held, gain, win, win_t, start, tokens, after):
    feat = held[0].shape[2]
    length = start.shape[1]
    wide = win.shape[1] // 3
    heads = wide // HEAD
    nb = length // BLK
    per = tokens // BLK
    whole = (None, None)
    heads_out = (sds((heads, length, HEAD), bf16), (heads, BLK, HEAD), by_mid)
    cols_out = (sds((wide, length), bf16), (wide, BLK), by_col)
    return call(
        fwd_kernel,
        "attend_forward",
        26,
        (nb,),
        [
            (table,) + whole,
            (held[0],) + whole,
            (held[1],) + whole,
            (gain,) + whole,
            (win,) + whole,
            (win_t,) + whole,
            (start, (1, BLK), by_col),
        ],
        [
            (sds((length, feat), bf16), (BLK, feat), by_row),
            (sds((length, feat), bf16), (BLK, feat), by_row),
            (sds((length // tokens, wide, tokens), bf16), (1, wide, BLK), lambda i, *_: (i // per, 0, i % per)),
            (sds((wide, length), f32), (wide, BLK), by_col),
            (sds((8, length), f32), (8, BLK), by_col),
            heads_out,
            heads_out,
            heads_out,
            cols_out,
            cols_out,
        ],
        [pltpu.VMEM((nb, heads, BLK, HEAD), bf16), pltpu.VMEM((nb, wide, BLK), bf16)],
        prefetch=1,
        after=after,
    )


def bwd_kernel(
    table, go, o_t, lse, qn, kn, vn, q_t, k_t, start, held, normed, win, small,
    keep, send, gin, g_nat, dq, delta, gin_acc, gain_acc,
):
    j = pl.program_id(0)
    nb = pl.num_programs(0)
    heads = kn.shape[0]
    wide = q_t.shape[0]
    per = go.shape[2] // BLK
    rows = lax.broadcasted_iota(jnp.int32, (BLK, BLK), 0)
    cols = lax.broadcasted_iota(jnp.int32, (BLK, BLK), 1)

    def chunk(ref, i, lanes):
        return ref[i // per, lanes, pl.ds(pl.multiple_of(i % per * BLK, BLK), BLK)]

    @pl.when(j == 0)
    def _():
        dq[...] = jnp.zeros_like(dq)
        gin_acc[...] = jnp.zeros_like(gin_acc)
        gain_acc[...] = jnp.zeros_like(gain_acc)
        for b in range(g_nat.shape[0]):
            g = chunk(go, b, slice(None)).astype(f32)
            g_nat[b] = g.T.astype(bf16)
            prod = g * o_t[:, b * BLK : (b + 1) * BLK]
            for h in range(heads):
                delta[b, h : h + 1] = jnp.sum(prod[h * HEAD : (h + 1) * HEAD], 0, keepdims=True)

    def tile(i, accs, mask):
        new = []
        here = pl.ds(pl.multiple_of(i * BLK, BLK), BLK)
        inside = rows + j * BLK >= start[:, here]
        mask = inside if mask is None else mask & inside
        g_all = g_nat[i]
        for h in range(heads):
            dk, dv = accs[h]
            hs = slice(h * HEAD, (h + 1) * HEAD)
            s = nn(kn[h], q_t[hs, here])
            p = jnp.exp(jnp.where(mask, s, masked_out) - lse[h : h + 1, here])
            dv = dv + nn(p.astype(bf16), g_all[:, hs])
            dp = nn(vn[h], chunk(go, i, hs))
            d = (p * (dp - delta[i, h : h + 1])).astype(bf16)
            dk = dk + nn(d, qn[h, here])
            dq[i, hs] += nn(k_t[hs], d)
            new.append((dk, dv))
        return tuple(new)

    zero = jnp.zeros((BLK, HEAD), f32)
    accs = tile(j, tuple((zero, zero) for _ in range(heads)), rows <= cols)
    accs = lax.fori_loop(j + 1, nb, lambda i, a: tile(i, a, None), accs)
    gp = jnp.concatenate(
        [(dq[j] * HEAD**-0.5).T] + [a[0] for a in accs] + [a[1] for a in accs], 1
    ).astype(bf16)
    back = nt(gp, win[...])
    x = held[...].astype(f32)
    scale = lax.rsqrt(jnp.mean(x * x, -1, keepdims=True) + epsilon)
    gain_acc[0:1] += jnp.sum(back * (x * scale), 0, keepdims=True)
    gin_acc[...] += tn(normed[...], gp)
    place = table[j // per]
    half = keep.shape[0]
    here = pl.ds(pl.multiple_of(j % per * BLK, BLK), BLK)

    @pl.when(place < half)
    def _():
        keep[place, here, :] = back

    @pl.when(place >= half)
    def _():
        send[place - half, here, :] = back.astype(bf16)

    @pl.when(j == nb - 1)
    def _():
        gain = gain_acc[...].T[:, 0:1]
        high = gain.astype(bf16).astype(f32)
        lane = lax.broadcasted_iota(jnp.int32, small.shape, 1)
        tail = jnp.where(lane == 0, high, small[...].astype(f32))
        tail = jnp.where(lane == 21, gain - high, tail)
        gin[...] = jnp.concatenate([gin_acc[...], tail], 1).astype(bf16)


def attend_backward(
    table, go, o_t, lse, qn, kn, vn, q_t, k_t, start, held, normed, win, small, after
):
    n_seq, wide, tokens = go.shape
    length = n_seq * tokens
    heads = wide // HEAD
    feat = win.shape[0]
    nb = length // BLK
    per = tokens // BLK
    half = n_seq // 2
    whole = (None, None)

    return call(
        bwd_kernel,
        "attend_backward",
        7600,
        (nb,),
        [
            (table,) + whole,
            (go,) + whole,
            (o_t,) + whole,
            (lse,) + whole,
            (qn,) + whole,
            (kn, (heads, BLK, HEAD), by_mid),
            (vn, (heads, BLK, HEAD), by_mid),
            (q_t,) + whole,
            (k_t, (wide, BLK), by_col),
            (start,) + whole,
            (held, (BLK, feat), by_row),
            (normed, (BLK, feat), by_row),
            (win,) + whole,
            (small,) + whole,
        ],
        [
            (sds((half, tokens, feat), f32),) + whole,
            (sds((half, tokens, feat), bf16),) + whole,
            (sds((feat, 3 * wide + small.shape[1]), bf16),) + whole,
        ],
        [
            pltpu.VMEM((nb, BLK, wide), bf16),
            pltpu.VMEM((nb, wide, BLK), f32),
            pltpu.VMEM((nb, 8, BLK), f32),
            pltpu.VMEM((feat, 3 * wide), f32),
            pltpu.VMEM((8, feat), f32),
        ],
        prefetch=1,
        after=after,
    )


def call(kernel, name, cost, grid, ins, outs, scratch=(), prefetch=0, limit=60, after=()):
    def spec(shape, block, index):
        if block is None:
            return pl.BlockSpec(shape, lambda *_: (0,) * len(shape))
        return pl.BlockSpec(block, index)

    n_in, n_out = len(ins), len(outs)

    def ordered(*refs):
        rest = refs[n_in + len(after) :]
        rest[n_out][...] = jnp.zeros_like(rest[n_out])
        kernel(*refs[:n_in], *rest[:n_out], *rest[n_out + 1 :])

    outs = list(outs) + [(sds((1, 1), f32), None, None)]
    return pl.pallas_call(
        ordered,
        grid_spec=pltpu.PrefetchScalarGridSpec(
            num_scalar_prefetch=prefetch,
            grid=grid,
            in_specs=[spec(a.shape, b, i) for a, b, i in ins[prefetch:]]
            + [pl.BlockSpec(memory_space=pl.ANY)] * len(after),
            out_specs=[spec(s.shape, b, i) for s, b, i in outs],
            scratch_shapes=list(scratch),
        ),
        out_shape=[s for s, _, _ in outs],
        compiler_params=pltpu.CompilerParams(vmem_limit_bytes=limit << 20),
        cost_estimate=pl.CostEstimate(
            flops=int(cost * 5750000),
            bytes_accessed=sum(v.size * v.dtype.itemsize for v, _, _ in ins[prefetch:] + outs),
            transcendentals=0,
        ),
        name=name,
    )(*[a for a, _, _ in ins], *after)


def sds(shape, dtype):
    return jax.ShapeDtypeStruct(shape, dtype)


def by_row(i, *_):
    return (i, 0)


def by_col(i, *_):
    return (0, i)


def by_first(i, *_):
    return (i, 0, 0)


def by_last(i, *_):
    return (0, 0, i)


def by_mid(i, *_):
    return (0, i, 0)


def exact_dot(a, b, dims=((1,), (0,))):
    return lax.dot_general(a, b, (dims, ((), ())), preferred_element_type=f32, precision=exact)


def dispatch_rows(dest, rows, send):
    hosts, cap, features = send.shape
    group = max(g for g in range(1, hosts + 1) if hosts % g == 0 and g * cap <= 640)

    def one(h, carry):
        slot = lax.broadcasted_iota(jnp.int32, (group * cap, dest.shape[1]), 0) + h * group * cap
        hits = [slot == dest[r : r + 1] for r in range(2)]
        if len(rows) == 1:
            hits = [hits[0] | hits[1]]
        total = None
        for hit, part in zip(hits, rows):
            term = nn(jnp.where(hit, 1.0, 0.0).astype(bf16), part[...])
            total = term if total is None else total + term
        send[pl.ds(h * group, group)] = total.astype(bf16).reshape(group, cap, features)
        return carry

    lax.fori_loop(0, hosts // group, one, 0)


def mid_kernel(att, x, wo, gain, wrm, prev, dest, res, normed, soft, send, low):
    i = pl.program_id(0)
    n_seq, wide, block = att.shape
    acc = x[...].astype(f32)
    for s in range(n_seq):
        acc = acc + tn(att[s], wo[s * wide : (s + 1) * wide])
    res[...] = acc
    scale = lax.rsqrt(jnp.mean(acc * acc, -1, keepdims=True) + epsilon)
    unit = acc * scale * gain[...]
    normed[...] = unit
    low[pl.ds(pl.multiple_of(i * block, block), block), :] = unit.astype(bf16)
    logits = exact_dot(unit, wrm[...]) + prev[...]
    lane = lax.broadcasted_iota(jnp.int32, logits.shape, 1)
    result = jnp.zeros_like(logits)
    for lo, hi in ((0, ROUTES), (ROUTES, ROUTES + 2), (ROUTES + 2, ROUTES + 4)):
        inside = (lane >= lo) & (lane < hi)
        part = jnp.where(inside, logits, masked_out)
        expo = jnp.where(inside, jnp.exp(part - jnp.max(part, -1, keepdims=True)), 0.0)
        result = result + expo / jnp.sum(expo, -1, keepdims=True)
    soft[...] = result

    @pl.when(i == pl.num_programs(0) - 1)
    def _():
        dispatch_rows(dest, (low,), send)


def prepare_kernel(got, win, win_t, gains, wrm, out):
    inner = win.shape[1]
    split = got.shape[1] - out.shape[2]
    for k in range(out.shape[0]):
        out[k] = got[:, split:]
    turned = got[:, :split].astype(f32).T
    win[...] = got[:, :inner]
    win_t[...] = turned[:inner].astype(bf16)
    gains[0:2] = turned[inner : inner + 2]
    gains[2:4] = turned[inner + 18 : inner + 20]
    gains[4:8] = jnp.zeros_like(gains[4:8])
    wrm[...] = got[:, inner + 2 : inner + 18].astype(f32)


def gate_parts(soft, routes):
    lane = lax.broadcasted_iota(jnp.int32, soft.shape, 1)
    hits = [(lane == routes[:, r : r + 1]).astype(f32) for r in range(2)]
    picked = [jnp.sum(h * soft, -1, keepdims=True) for h in hits]
    total = picked[0] + picked[1]
    gates = [p / total for p in picked]
    spread = gates[0] * hits[0] + gates[1] * hits[1]

    def lane_of(values, k):
        return values[:, k : k + 1]

    copy = lane_of(spread, EXPERTS + 1)
    const = [lane_of(spread, EXPERTS + 2 + c) for c in range(2)]
    mix = [[lane_of(soft, ROUTES + 2 * c + k) for k in range(2)] for c in range(2)]
    return lane, hits, total, gates, copy, const, mix


def loss_kernel(
    back, dest_col, dest, routes, soft, normed, res, teacher, valid, vectors, factor,
    out, grad, stats, send, squared, low0, low1,
):
    i = pl.program_id(0)
    block = res.shape[0]
    hosts, cap, features = back.shape
    rows = back[...].reshape(hosts * cap, features)
    slot = lax.broadcasted_iota(jnp.int32, (block, hosts * cap), 1)
    terms = [
        nn(jnp.where(slot == dest_col[:, r : r + 1], 1.0, 0.0).astype(bf16), rows)
        for r in range(2)
    ]
    lane, hits, total, gates, copy, const, mix = gate_parts(soft[...], routes[...])
    vec = [vectors[c : c + 1] for c in range(2)]
    unit = normed[...]
    full = res[...] + (copy + const[0] * mix[0][0] + const[1] * mix[1][0]) * unit
    full = full + (const[0] * mix[0][1]) * vec[0] + (const[1] * mix[1][1]) * vec[1]
    full = full + gates[0] * terms[0] + gates[1] * terms[1]
    out[...] = full.astype(bf16)
    ok = valid[...]
    differ = (full - teacher[...].astype(f32)) * ok
    gf = differ * factor[0, 0]
    grad[...] = gf
    here = pl.ds(pl.multiple_of(i * block, block), block)
    low0[here, :] = (gates[0] * gf).astype(bf16)
    low1[here, :] = (gates[1] * gf).astype(bf16)

    def over(values):
        return jnp.sum(gf * values, -1, keepdims=True)

    parts = [over(terms[0]), over(terms[1]), over(unit), over(vec[0]), over(vec[1])]
    tile = lax.broadcasted_iota(jnp.int32, stats.shape, 1)
    filled = jnp.zeros(stats.shape, f32)
    for k, part in enumerate(parts):
        filled = jnp.where(tile == k, part, filled)
    stats[...] = filled

    @pl.when(i == 0)
    def _():
        squared[...] = jnp.zeros_like(squared)

    squared[...] += jnp.sum(differ * differ, 0, keepdims=True)

    @pl.when(i == pl.num_programs(0) - 1)
    def _():
        dispatch_rows(dest, (low0, low1), send)


def route_kernel(soft, routes, stats, grad, normed, wrm, partial, small, small_vec):
    i = pl.program_id(0)
    probs = soft[...]
    lane, hits, total, gates, copy, const, mix = gate_parts(probs, routes[...])
    s = stats[...]
    dots = [s[:, k : k + 1] for k in range(5)]
    const_dot = [mix[c][0] * dots[2] + mix[c][1] * dots[3 + c] for c in range(2)]
    grad_gates = []
    for r in range(2):
        h = hits[r]
        grad_gates.append(
            dots[r]
            + h[:, EXPERTS + 1 : EXPERTS + 2] * dots[2]
            + h[:, EXPERTS + 2 : EXPERTS + 3] * const_dot[0]
            + h[:, EXPERTS + 3 : EXPERTS + 4] * const_dot[1]
        )
    mean = gates[0] * grad_gates[0] + gates[1] * grad_gates[1]
    grad_probs = sum(hits[r] * ((grad_gates[r] - mean) / total) for r in range(2))
    only = jnp.where(lane < ROUTES, probs, 0.0)
    both = only * (grad_probs - jnp.sum(only * grad_probs, -1, keepdims=True))
    for c in range(2):
        grad_mix = [const[c] * dots[2], const[c] * dots[3 + c]]
        inner = mix[c][0] * grad_mix[0] + mix[c][1] * grad_mix[1]
        for k in range(2):
            both = jnp.where(lane == ROUTES + 2 * c + k, mix[c][k] * (grad_mix[k] - inner), both)
    gf = grad[...]
    unit = normed[...]
    coef = copy + const[0] * mix[0][0] + const[1] * mix[1][0]
    partial[...] = coef * gf + exact_dot(both, wrm[...], ((1,), (1,)))
    spread = jnp.where(lane == 0, const[0] * mix[0][1], 0.0)
    spread = jnp.where(lane == 1, const[1] * mix[1][1], spread)

    @pl.when(i == 0)
    def _():
        small[...] = jnp.zeros_like(small)
        small_vec[...] = jnp.zeros_like(small_vec)

    small[...] += exact_dot(unit, both, ((0,), (0,)))
    small_vec[...] += exact_dot(gf, spread, ((0,), (0,)))


def join_kernel(
    back, dest_col, partial, res, grad, gain, wo, mid, branch, out, gain_grad
):
    i = pl.program_id(0)
    block = res.shape[0]
    hosts, cap, features = back.shape
    rows = back[...].reshape(hosts * cap, features)
    slot = lax.broadcasted_iota(jnp.int32, (block, hosts * cap), 1)
    hit = (slot == dest_col[:, 0:1]) | (slot == dest_col[:, 1:2])
    grad_normed = partial[...] + nn(jnp.where(hit, 1.0, 0.0).astype(bf16), rows)
    r = res[...]
    scale = lax.rsqrt(jnp.mean(r * r, -1, keepdims=True) + epsilon)
    unit = r * scale

    @pl.when(i == 0)
    def _():
        gain_grad[...] = jnp.zeros_like(gain_grad)

    gain_grad[...] += jnp.sum(grad_normed * unit, 0, keepdims=True)
    hat = grad_normed * gain[...]
    total = grad[...] + scale * (hat - unit * jnp.mean(hat * unit, -1, keepdims=True))
    mid[...] = total
    low = total.astype(bf16)
    branch[...] = low
    n_seq, wide, _ = out.shape
    for s in range(n_seq):
        out[s] = nt(wo[s * wide : (s + 1) * wide], low).astype(bf16)


def out_grad_kernel(att, branch, out):
    n_seq, wide, _ = att.shape
    for s in range(n_seq):
        out[s * wide : (s + 1) * wide] = nn(att[s], branch[...]).astype(bf16)


def whole_tile(me, parts, tile):
    far, core = me[0], me[1]
    for part, f, c in zip(parts, (far, 1 - far, far, 1 - far), (core, core, 1 - core, 1 - core)):
        tile[pl.ds(f, 1), :, pl.ds(c, 1)] = part[None, :, None]
    return tile[...].reshape(-1, tile.shape[-1])


def pick_kernel(index, *refs):
    shards, same, other = refs[:-2], refs[-2], refs[-1]
    for k, shard in enumerate(shards):
        same[k] = shard[index[0]]
        other[k] = shard[1 - index[0]]


def total_kernel(n_small, parts, share, gin, gout, router, mix, small, vectors, loss, gain_first, gain_mid):
    total = jnp.sum(parts[...].astype(f32), 0)
    features = gout.shape[1]
    wide = HEAD * (features // HEAD // 4)
    for s in range(features // wide):
        for k in range(3):
            at = (3 * s + k) * wide
            gin[:, k * features + s * wide : k * features + (s + 1) * wide] = total[:, at : at + wide]
    gout[...] = total[:, 3 * features : 4 * features]
    tail = total[:, 4 * features :]
    both = tail[:, :n_small] + tail[:, n_small : 2 * n_small]
    n_pad = small.shape[0]
    unit = lax.broadcasted_iota(jnp.int32, (n_pad, tail.shape[1]), 0)
    unit = (unit == lax.broadcasted_iota(jnp.int32, unit.shape, 1)).astype(f32)
    wide_both = tail + jnp.concatenate([tail[:, n_small:], tail[:, :n_small]], 1)
    small[...] = exact_dot(unit, wide_both, ((1,), (1,)))
    vectors[...] = small[18:20]
    loss[...] = small[20:21, 0:1] * share[...]
    gain_first[...] = small[0:1]
    gain_mid[...] = small[1:2]
    router[...] = both[:, 2 : 2 + ROUTES]
    mix[...] = both[:, 2 + ROUTES : 6 + ROUTES]


def in_sum_kernel(gate, gate_given, up, up_given, out):
    for k, (own, given) in enumerate(((gate, gate_given), (up, up_given))):
        out[:, k] = (own[...].astype(f32) + given[...].astype(f32)).astype(bf16)


def part_kernel(which, part, same, other):
    same[...] = part[which[0]]
    other[...] = part[1 - which[0]]


def owner_kernel(which, same, alike, unlike, *outs):
    mine = jnp.where(which[1] == 1, same[...], alike[...]).astype(f32)
    theirs = unlike[...].astype(f32)
    height = outs[0].shape[1]
    for k, out in enumerate(outs):
        here = slice(k * height, (k + 1) * height)
        out[which[0]] = mine[here]
        out[1 - which[0]] = theirs[here]


def cross_kernel(which, same, alike, unlike, out):
    @pl.when(which[1] == 1)
    def _():
        out[pl.ds(which[0], 1)] = same[...][None]

    @pl.when(which[1] != 1)
    def _():
        out[pl.ds(which[0], 1)] = alike[...][None]

    out[pl.ds(1 - which[0], 1)] = unlike[...][None]


def split_tile(me, values, tile):
    tile[...] = values.reshape(tile.shape)
    return tile[:, pl.ds(me[1], 1)][:, 0], tile[:, pl.ds(1 - me[1], 1)][:, 0]


def expert_hidden_kernel(
    me, rows, near, far, near_other, far_other, gate_part, up_part, hidden, gate, up
):
    parts = (near, far, near_other, far_other)
    w_gate = whole_tile(me, [p[:, 0] for p in parts], gate)
    w_up = whole_tile(me, [p[:, 1] for p in parts], up)
    step = rows.shape[0] // 2
    for k in range(2):
        here = slice(k * step, (k + 1) * step)
        g = nn(rows[here], w_gate)
        u = nn(rows[here], w_up)
        gate_part[here] = g
        up_part[here] = u
        hidden[here] = (g / (1.0 + jnp.exp(-g)) * u).astype(bf16)


def expert_result_kernel(me, hidden, near, far, near_other, far_other, result, down):
    @pl.when(pl.program_id(0) == 0)
    def _():
        whole_tile(me, [p[...] for p in (near, far, near_other, far_other)], down)

    result[...] = nn(hidden[...], down[...].reshape(-1, down.shape[-1])).astype(bf16)


def down_grad_kernel(me, hidden, grad, own, other, parts):
    own[...], other[...] = split_tile(me, tn(hidden[...], grad[...]).astype(bf16), parts)


def expert_backward_kernel(
    me, grad, gate_part, up_part, near, far, near_other, far_other,
    down_near, down_far, down_near_other, down_far_other,
    d_gate, d_up, result, gate, up, down, acc,
):
    f = pl.program_id(0)

    @pl.when(f == 0)
    def _():
        pieces = (down_near, down_far, down_near_other, down_far_other)
        whole_tile(me, [p[...] for p in pieces], down)

    w_down = down[f // 2, f % 2].reshape(-1, down.shape[-1])
    weights = (near, far, near_other, far_other)
    w_gate = whole_tile(me, [p[:, 0] for p in weights], gate)
    w_up = whole_tile(me, [p[:, 1] for p in weights], up)

    @pl.when(f == 0)
    def _():
        acc[...] = jnp.zeros_like(acc)

    step = grad.shape[0] // 2
    for k in range(2):
        here = slice(k * step, (k + 1) * step)
        gh = nt(grad[here], w_down)
        g = gate_part[here]
        sig = 1.0 / (1.0 + jnp.exp(-g))
        silu = g * sig
        dg = (gh * up_part[here] * (sig + silu * (1.0 - sig))).astype(bf16)
        du = (gh * silu).astype(bf16)
        d_gate[here] = dg
        d_up[here] = du
        acc[here] += nt(dg, w_gate) + nt(du, w_up)

    @pl.when(f == pl.num_programs(0) - 1)
    def _():
        result[...] = acc[...].astype(bf16)


def in_grad_kernel(me, rows, d, own, other, parts, turned):
    @pl.when(pl.program_id(0) == 0)
    def _():
        turned[...] = rows[...].astype(f32).T.astype(bf16)

    own[...], other[...] = split_tile(me, nn(turned[...], d[...]).astype(bf16), parts)


def seq_add_kernel(keep, given, near, far):
    near[...] = keep[0] + given[0].astype(f32)
    far[...] = (keep[1] + given[1].astype(f32)).astype(bf16)


def finish_kernel(near, given, mid, x, gain, out):
    grad = near[...] + given[...].astype(f32)
    values = x[...].astype(f32)
    scale = lax.rsqrt(jnp.mean(values * values, -1, keepdims=True) + epsilon)
    unit = values * scale
    hat = grad * gain[...]
    out[...] = mid[...] + scale * (hat - unit * jnp.mean(hat * unit, -1, keepdims=True))


def exchange(blocks, axes):
    return lax.all_to_all(blocks, axes, split_axis=0, concat_axis=0, tiled=True)


def to_all(block, count):
    return exchange(jnp.broadcast_to(block[None], (count,) + block.shape), ALL)


def gather_seq(block, size):
    held = block[None]
    step = size // 2
    while step > 1:
        pairs = [(i, i ^ step) for i in range(size)]
        held = jnp.concatenate([held, lax.ppermute(held, SEQ, pairs)], 0)
        step //= 2
    held = (held, lax.ppermute(held, SEQ, [(i, i ^ 1) for i in range(size)]))
    order = [0]
    step = size // 2
    while step:
        order = order + [k ^ step for k in order]
        step //= 2
    return held, order


def body(
    block_input,
    teacher,
    prev_logits,
    valid_mask,
    segments,
    routes,
    input_proj,
    output_proj,
    attention_gain,
    mixture_gain,
    router,
    const_mix,
    const_vectors,
    expert_gate,
    expert_up,
    expert_down,
):
    n_out, n_in, n_seq = (lax.axis_size(a) for a in (OUTER, "d", SEQ))
    n_all = n_out * n_in * n_seq
    n_far = lax.axis_size("a")
    tokens_here, features = block_input.shape
    rows_here = input_proj.shape[0]
    wide = features // n_seq
    seq_id = lax.axis_index(SEQ)

    a_id, b_id, d_id, c_id = (lax.axis_index(x) for x in ("a", "b", "d", "sc"))
    me = jnp.stack([a_id * (n_far == 2), c_id])
    swap = [(0, 1), (1, 0)]
    cross = [(1, 2), (2, 1)]

    def item(values, index):
        return lax.dynamic_index_in_dim(values, index, 0, keepdims=False)

    def in_order(index, mine, given):
        return jnp.where(index == 0, jnp.stack([mine, given]), jnp.stack([given, mine]))

    which = jnp.stack([b_id, (c_id == d_id).astype(jnp.int32)])

    place = [(b, d, c) for b in range(2) for d in range(2) for c in range(2)]
    alike = [(4 * b + 2 * d + c, 4 * b + 2 * c + d) for b, d, c in place if d != c]
    unlike = [(4 * b + 2 * d + c, 4 * (1 - b) + 2 * c + d) for b, d, c in place]

    def crossed(same, other):
        same = jnp.where(c_id == d_id, same, lax.ppermute(same, ("b", "d", "sc"), alike))
        return in_order(b_id, same, lax.ppermute(other, ("b", "d", "sc"), unlike))

    def cross(same, other, after):
        given = [lax.ppermute(same, ("b", "d", "sc"), alike)]
        given.append(lax.ppermute(other, ("b", "d", "sc"), unlike))
        count, height, width = same.shape
        quarter = width // (4 if width % 512 == 0 else 2)
        block = ((count, height, quarter), by_last)
        pair, _ = call(
            cross_kernel,
            "cross",
            2,
            (width // quarter,),
            [(which, None, None)] + [(x,) + block for x in [same] + given],
            [(sds((2,) + same.shape, bf16), (2,) + block[0], lambda i, *_: (0, 0, 0, i))],
            prefetch=1,
            after=after,
        )
        return pair

    def far_pair(pair):
        return lax.all_gather(pair, "a", axis=0, tiled=False)

    def far_parts(far, done):
        if n_far == 2:
            far = item(far, 1 - a_id)
        far = far + done[0, 0].astype(bf16)
        return far, lax.ppermute(far, "sc", swap)

    def core_sum(own, other, done=None):
        total = own.astype(f32) + lax.ppermute(other, "sc", swap).astype(f32)
        if done is not None:
            total = total + done[0, 0]
        return total.astype(bf16).reshape((n_far, 2) + own.shape[1:])

    def far_sum(part):
        return lax.psum_scatter(part, "a", scatter_dimension=0, tiled=False)

    def to_owner(part, after):
        _, height, width = part.shape
        steps = 4 if width % 512 == 0 else 2
        one = ((height, width // steps), by_col)
        same, other, done = call(
            part_kernel,
            "part",
            3,
            (steps,),
            [(which, None, None), (part, (2, height, width // steps), by_last)],
            [(sds((height, width), bf16),) + one] * 2,
            prefetch=1,
            after=after,
        )
        given = [
            lax.ppermute(same, ("b", "d", "sc"), alike),
            lax.ppermute(other, ("b", "d", "sc"), unlike),
        ]

        def kept(count, after):
            shape = (2, height // count, width)
            return call(
                owner_kernel,
                "owner",
                4,
                (steps,),
                [(which, None, None)] + [(x,) + one for x in [same] + given],
                [(sds(shape, f32), shape[:2] + (width // steps,), by_last)] * count,
                prefetch=1,
                after=after,
            )

        return kept, done

    slice_rows = expert_gate.shape[1]

    def regroup(near, far, near_other, far_other):
        if n_far == 2:
            return near, far, near_other, far_other
        pair = in_order(c_id, far, far_other).transpose(3, 1, 2, 0, 4, 5)
        pair = pair.reshape(pair.shape[:1] + (2, 2, 2, -1) + pair.shape[5:])
        pair = pair.transpose(1, 3, 2, 0, 4, 5)
        return tuple(item(pair[f], c) for c in (c_id, 1 - c_id) for f in range(2))

    def owner_slices(own, other):
        if n_far == 2:
            return own, other
        pair = in_order(c_id, own, other).transpose(2, 1, 0, 3, 4)
        pair = pair.reshape(pair.shape[:1] + (n_out, 2, -1) + pair.shape[4:])
        pair = pair.transpose(2, 1, 0, 3, 4)
        return item(pair, c_id), item(pair, 1 - c_id)

    def pick(shards, after=()):
        _, height, width = shards[0].shape
        quarter = width // (4 if width % 512 == 0 else 2)
        block = ((2, height, quarter), by_last)
        out_block = ((len(shards), height, quarter), by_last)
        return call(
            pick_kernel,
            "pick",
            3,
            (width // quarter,),
            [(b_id.reshape(1), None, None)] + [(x,) + block for x in shards],
            [(sds((len(shards), height, width), bf16),) + out_block] * 2,
            prefetch=1,
            after=after,
        )

    same_in, other_in, picked = pick([expert_gate, expert_up])
    seg_row = jnp.pad(segments.astype(bf16), (0, features * 2 - tokens_here)).reshape(2, features)
    with_seg = jnp.concatenate(
        [block_input, jnp.pad(seg_row, ((0, 14), (0, 0)))], 0
    )
    held, order = gather_seq(with_seg, n_seq)
    where = [order.index(j) for j in range(n_seq)]
    chosen = jnp.array(where, jnp.int32)[jnp.arange(n_seq) ^ seq_id]
    length = n_seq * tokens_here
    seg_rows = [h[:, tokens_here : tokens_here + 2] for h in held]
    seq_segments = (
        jnp.concatenate(seg_rows, 0)
        .reshape(n_seq, 2 * features)[:, :tokens_here][chosen]
        .reshape(1, -1)
    )
    positions = jnp.arange(length, dtype=jnp.int32)[None]
    fresh = seq_segments != jnp.pad(seq_segments[:, :-1], ((0, 0), (1, 0)), constant_values=-1)
    start = lax.cummax(jnp.where(fresh, positions, 0), axis=1)

    flat_routes = routes.reshape(-1)
    onehot_e = (flat_routes[:, None] == jnp.arange(EXPERTS, dtype=jnp.int32)[None, :]).astype(
        jnp.int32
    )
    slot_rank = jnp.sum((jnp.cumsum(onehot_e, 0) - onehot_e) * onehot_e, -1)
    host = (flat_routes % 2) * 4 + flat_routes // 2 % 2 * 2 + flat_routes // 4
    slot_dest = jnp.where(flat_routes < EXPERTS, host * CAP + slot_rank, EXPERTS * CAP)
    slot_dest = slot_dest.reshape(tokens_here, 2)
    slot_row = jnp.pad(slot_dest.T, ((0, 6), (0, 0)))

    in_pair = cross(same_in, other_in, [held[1], start, slot_row])
    in_far = far_pair(in_pair)
    in_other = lax.ppermute(in_pair, "sc", swap)

    same_down, other_down, _ = pick([expert_down], [in_pair])

    own_cols = (input_proj + picked[0, 0].astype(bf16)).reshape(rows_here, 3, n_seq, wide)
    own_cols = own_cols.transpose(0, 2, 1, 3).reshape(rows_here, -1)
    count_here = jnp.sum(valid_mask)
    count_cols = jnp.stack([count_here // 32, count_here % 32]).astype(bf16)
    small = jnp.concatenate(
        [
            attention_gain[:, None],
            mixture_gain[:, None],
            router,
            const_mix,
            const_vectors.T,
            jnp.broadcast_to(count_cols[None], (rows_here, 2)),
        ],
        1,
    )
    n_small = small.shape[1]
    small = jnp.pad(small, ((0, 0), (0, -(3 * wide + n_small) % 128)))
    packed = jnp.concatenate(
        [
            own_cols.reshape(rows_here, n_seq, 3 * wide).transpose(1, 0, 2),
            jnp.broadcast_to(small[None], (n_seq,) + small.shape),
        ],
        2,
    )
    n_plane = n_in * n_seq
    piece = features // n_plane
    out_piece = output_proj.reshape(rows_here, n_in, n_seq, piece).transpose(1, 2, 0, 3)
    inner = packed.shape[2]
    packed = jnp.concatenate(
        [jnp.broadcast_to(packed[None], (n_in,) + packed.shape), out_piece], 3
    )
    packed = jnp.pad(packed, ((0, 0),) * 3 + ((0, -packed.shape[3] % 128),))
    packed = jnp.broadcast_to(packed[None], (n_out,) + packed.shape)
    got = exchange(packed.reshape((n_all,) + packed.shape[3:]), ALL)
    counts = got[:, 0, 3 * wide + 20 : 3 * wide + 22].astype(f32)
    valid_count = jnp.sum(counts[:, 0]) * 32.0 + jnp.sum(counts[:, 1])
    got = got.reshape(features, -1)
    own_in, own_in_t, gains, wrm, out_cols, prepared = call(
        prepare_kernel,
        "prepare",
        3,
        (1,),
        [(got, None, None)],
        [
            (sds((features, 3 * wide), bf16), None, None),
            (sds((3 * wide, features), bf16), None, None),
            (sds((8, features), f32), None, None),
            (sds((features, ROUTES + 4), f32), None, None),
            (sds((n_plane, features, got.shape[1] - inner), bf16), None, None),
        ],
    )
    gain_first, gain_mid, vectors_f = gains[0:1], gains[1:2], gains[2:4]
    full_out = exchange(out_cols, PLANE)[:, :, :piece].transpose(1, 0, 2)
    full_out = full_out.reshape(features, features)

    seq_inputs, normed_first, attended, attended_t, log_totals, *heads_saved, forward_done = attend_forward(
        chosen, held, gain_first, own_in, own_in_t, start, tokens_here,
        [in_other],
    )
    attended_tok = exchange(attended, SEQ)

    down_pair = cross(same_down, other_down, [normed_first])
    down_far = far_pair(down_pair)
    down_other = lax.ppermute(down_pair, "sc", swap)

    whole = (None, None)
    rows_block = 256
    steps = (tokens_here // rows_block,)
    wide_block = ((rows_block, features), by_row)
    soft_block = ((rows_block, ROUTES + 4), by_row)
    pair_block = ((rows_block, 2), by_row)
    slots_shape = (EXPERTS, CAP, features)
    tok = sds((tokens_here, features), f32)
    residual_mid, normed, soft, send_rows, mid_done = call(
        mid_kernel,
        "mid",
        10,
        steps,
        [
            (attended_tok, (n_seq, wide, rows_block), by_last),
            (block_input,) + wide_block,
            (full_out,) + whole,
            (gain_mid,) + whole,
            (wrm,) + whole,
            (jnp.pad(prev_logits, ((0, 0), (0, 4))),) + soft_block,
            (slot_row,) + whole,
        ],
        [
            (tok,) + wide_block,
            (tok,) + wide_block,
            (sds((tokens_here, ROUTES + 4), f32),) + soft_block,
            (sds(slots_shape, bf16),) + whole,
        ],
        [pltpu.VMEM((tokens_here, features), bf16)],
        after=[down_other, in_far],
    )
    in_far, in_far_other = far_parts(in_far, mid_done)
    in_parts_w = regroup(in_pair, in_far, in_other, in_far_other)
    recv_rows = exchange(send_rows, ROWS).reshape(-1, features)
    n_rows = recv_rows.shape[0]
    hid = expert_gate.shape[2]
    tile = 512 if hid % 512 == 0 else hid
    tiles = (hid // tile,)
    _, _, piece_rows, _ = in_parts_w[0].shape
    w_part = ((2, 2, piece_rows, tile), lambda i, *_: (0, 0, 0, i))
    w_tile = pltpu.VMEM((2, 2, 2, piece_rows, tile), bf16)
    h_col = ((n_rows, tile), by_col)
    in_parts = [(w,) + w_part for w in in_parts_w]
    gate_part, up_part, hidden, hidden_done = call(
        expert_hidden_kernel,
        "expert_hidden",
        14,
        tiles,
        [(me,) + whole, (recv_rows,) + whole] + in_parts,
        [
            (sds((n_rows, hid), f32),) + h_col,
            (sds((n_rows, hid), f32),) + h_col,
            (sds((n_rows, hid), bf16),) + h_col,
        ],
        [w_tile] * 2,
        prefetch=1,
    )
    down_far, down_far_other = far_parts(down_far, hidden_done)
    down_parts_w = [p[:, 0] for p in regroup(down_pair, down_far, down_other, down_far_other)]
    far_rows = down_parts_w[0].shape[1]
    down_tile = pltpu.VMEM((2, 2, 2, far_rows, features), bf16)
    row_tile = n_rows // 2
    result_rows, _ = call(
        expert_result_kernel,
        "expert_result",
        8,
        (2,),
        [
            (me,) + whole,
            (hidden, (row_tile, hid), by_row),
        ]
        + [(p,) + whole for p in down_parts_w],
        [(sds((n_rows, features), bf16), (row_tile, features), by_row)],
        [down_tile],
        prefetch=1,
    )
    back_rows = exchange(result_rows.reshape(slots_shape), ROWS)
    valid_f = valid_mask.astype(f32)[:, None]
    factor = (tokens_here * n_all / valid_count).reshape(1, 1)
    full_output, grad_full, stats, grad_send, squared, _ = call(
        loss_kernel,
        "loss",
        11,
        steps,
        [
            (back_rows,) + whole,
            (slot_dest,) + pair_block,
            (slot_row,) + whole,
            (routes,) + pair_block,
            (soft,) + soft_block,
            (normed,) + wide_block,
            (residual_mid,) + wide_block,
            (teacher,) + wide_block,
            (valid_f, (rows_block, 1), by_row),
            (vectors_f,) + whole,
            (factor,) + whole,
        ],
        [
            (sds((tokens_here, features), bf16),) + wide_block,
            (tok,) + wide_block,
            (sds((tokens_here, 8), f32), (rows_block, 8), by_row),
            (sds(slots_shape, bf16),) + whole,
            (sds((1, features), f32),) + whole,
        ],
        [pltpu.VMEM((tokens_here, features), bf16)] * 2,
    )
    grad_recv = exchange(grad_send, ROWS).reshape(-1, features)
    partial_normed, small_cols, vector_cols, route_done = call(
        route_kernel,
        "route",
        14,
        steps,
        [
            (soft,) + soft_block,
            (routes,) + pair_block,
            (stats, (rows_block, 8), by_row),
            (grad_full,) + wide_block,
            (normed,) + wide_block,
            (wrm,) + whole,
        ],
        [
            (tok,) + wide_block,
            (sds((features, ROUTES + 4), f32),) + whole,
            (sds((features, ROUTES + 4), f32),) + whole,
        ],
    )

    d_gate, d_up, grad_rows, backward_done = call(
        expert_backward_kernel,
        "expert_backward",
        20,
        tiles,
        [
            (me,) + whole,
            (grad_recv,) + whole,
            (gate_part,) + h_col,
            (up_part,) + h_col,
        ]
        + in_parts
        + [(p,) + whole for p in down_parts_w],
        [(sds((n_rows, hid), bf16),) + h_col] * 2
        + [(sds((n_rows, features), bf16),) + whole],
        [w_tile] * 2 + [down_tile, pltpu.VMEM((n_rows, features), f32)],
        prefetch=1,
        after=[partial_normed],
    )
    grad_back = exchange(grad_rows.reshape(slots_shape), ROWS)
    def in_grad(name, d, after):
        shape = (4, piece_rows, tile)
        out = (sds((4, piece_rows, hid), bf16), shape, by_last)
        *grads, _ = call(
            in_grad_kernel,
            name,
            8,
            tiles,
            [(me,) + whole, (recv_rows,) + whole, (d,) + h_col],
            [out] * 2,
            [
                pltpu.VMEM((4, 2, piece_rows, tile), bf16),
                pltpu.VMEM((features, n_rows), bf16),
            ],
            prefetch=1,
            after=after,
        )
        return grads

    gate_grads = in_grad("gate_grad", d_gate, [grad_rows])
    up_grads = in_grad("up_grad", d_up, [gate_grads[0]])
    *down_grads, _ = call(
        down_grad_kernel,
        "down_grad",
        8,
        tiles,
        [(me,) + whole, (hidden,) + h_col, (grad_recv,) + whole],
        [(sds((4, far_rows, features), bf16), (1, far_rows, features), by_first)] * 2,
        [pltpu.VMEM((1, 2, far_rows, features), bf16)],
        prefetch=1,
        after=[up_grads[0]],
    )

    pairs = [owner_slices(*(q[:, None] for q in pair)) for pair in (gate_grads, up_grads)]
    terms = [x[:, 0] for own, other in pairs for x in (own, lax.ppermute(other, "sc", swap))]
    in_sum, _ = call(
        in_sum_kernel,
        "in_sum",
        4,
        (4,),
        [(x, (n_out // 4, slice_rows, hid), by_first) for x in terms],
        [
            (
                sds((n_out, 2, slice_rows, hid), bf16),
                (n_out // 4, 2, slice_rows, hid),
                lambda i, *_: (i, 0, 0, 0),
            )
        ],
        after=[down_grads[0]],
    )
    in_part = far_sum(in_sum.reshape(n_far, 2, 2 * slice_rows, hid))
    grad_mid, grad_branch, grad_attended, grad_mixture_gain, join_done = call(
        join_kernel,
        "join",
        8,
        steps,
        [
            (grad_back,) + whole,
            (slot_dest,) + pair_block,
            (partial_normed,) + wide_block,
            (residual_mid,) + wide_block,
            (grad_full,) + wide_block,
            (gain_mid,) + whole,
            (full_out,) + whole,
        ],
        [
            (tok,) + wide_block,
            (sds((tokens_here, features), bf16),) + wide_block,
            (sds((n_seq, wide, tokens_here), bf16), (n_seq, wide, rows_block), by_last),
            (sds((1, features), f32),) + whole,
        ],
        after=[in_sum],
    )
    grad_output_proj, out_done = call(
        out_grad_kernel,
        "out_grad",
        3,
        (1,),
        [(attended_tok,) + whole, (grad_branch,) + whole],
        [(sds((features, features), bf16),) + whole],
        after=[in_sum],
    )
    down_sum = core_sum(*owner_slices(*(p[:, None] for p in down_grads)), out_done)
    down_part = far_sum(down_sum)[:, 0]
    grad_heads = exchange(grad_attended, SEQ)

    def plane_blocks(part):
        return part.reshape(n_out, n_plane, rows_here, -1).transpose(1, 0, 2, 3)

    out_blocks = plane_blocks(grad_output_proj)
    out_grad = jnp.sum(exchange(out_blocks, PLANE).astype(f32), 0).astype(bf16)

    small_grads = jnp.concatenate(
        [
            jnp.zeros((features, 1), f32),
            grad_mixture_gain.T,
            small_cols,
            vector_cols[:, :2],
            jnp.broadcast_to(jnp.sum(squared), (features, 1)),
        ],
        1,
    )
    n_small = small_grads.shape[1]

    def two_parts(values, axis):
        high = values.astype(bf16)
        rest = (values - high.astype(f32)).astype(bf16)
        both = jnp.concatenate([high, rest], axis)
        return both

    small_low = two_parts(small_grads, 1)
    small_low = jnp.pad(small_low, ((0, 0), (0, -(3 * wide + 2 * n_small) % 128)))
    keep, sent, last, attention_done = attend_backward(
        chosen, grad_heads, attended_t, log_totals, *heads_saved, start, seq_inputs, normed_first,
        own_in, small_low, [out_blocks, down_sum],
    )

    sent = lax.ppermute(sent, SEQ, [(i, i ^ 1) for i in range(n_seq)])
    near, sent, added = call(
        seq_add_kernel,
        "seq_add",
        3,
        (2,),
        [
            (keep, (2, tokens_here // 2, features), by_mid),
            (sent, (2, tokens_here // 2, features), by_mid),
        ],
        [
            (tok, (tokens_here // 2, features), by_row),
            (sds((tokens_here, features), bf16), (tokens_here // 2, features), by_row),
        ],
    )
    kept_in, parted = to_owner(in_part, [near])
    sent = lax.ppermute(sent, SEQ, [(i, i ^ 2) for i in range(n_seq)])
    grad_input, finished = call(
        finish_kernel,
        "finish",
        3,
        steps,
        [
            (near,) + wide_block,
            (sent,) + wide_block,
            (grad_mid,) + wide_block,
            (block_input,) + wide_block,
            (gain_first,) + whole,
        ],
        [(tok,) + wide_block],
        after=[parted],
    )

    grad_expert_gate, grad_expert_up, owned = kept_in(2, [])
    last = last + (finished[0, 0] + owned[0, 0]).astype(bf16)
    last = exchange(plane_blocks(last), PLANE)
    kept_down, _ = to_owner(down_part, [grad_expert_gate])
    cols = last[:, :, :, : 3 * wide].reshape(n_in, n_seq, n_out, rows_here, 3 * wide)
    cols = jnp.sum(cols.astype(f32), 0).astype(bf16).transpose(1, 2, 0, 3)
    rest = jnp.sum(last[:, :, :, 3 * wide : 3 * wide + 2 * n_small].astype(f32), 0)
    rest = rest[:, :, :n_small] + rest[:, :, n_small:]
    last = jnp.concatenate(
        [cols.reshape(n_out, rows_here, -1), out_grad, two_parts(rest, 2)], 2
    )
    last = jnp.pad(last, ((0, 0), (0, 0), (0, -last.shape[2] % 128)))
    loss_share = 1.0 / (2.0 * features * valid_count)
    *last, _, grad_const_vectors, mean_loss, gain_first_row, gain_mid_row, _ = call(
        functools.partial(total_kernel, n_small),
        "total",
        2,
        (1,),
        [(exchange(last, OUTER),) + whole, (loss_share.reshape(1, 1),) + whole],
        [
            (sds((rows_here, 3 * features), f32),) + whole,
            (sds((rows_here, features), f32),) + whole,
            (sds((rows_here, ROUTES), f32),) + whole,
            (sds((rows_here, 4), f32),) + whole,
            (sds((24, rows_here), f32),) + whole,
            (sds((2, rows_here), f32),) + whole,
            (sds((1, 1), f32),) + whole,
            (sds((1, rows_here), f32),) + whole,
            (sds((1, rows_here), f32),) + whole,
        ],
    )
    grad_expert_down, _ = kept_down(1, [mean_loss])
    grad_input_proj, grad_output_proj, grad_router, grad_const_mix = last
    return (
        full_output,
        mean_loss.reshape(()),
        grad_input,
        grad_input_proj,
        grad_output_proj,
        gain_first_row.reshape(-1),
        gain_mid_row.reshape(-1),
        grad_router,
        grad_const_mix,
        grad_const_vectors,
        grad_expert_gate,
        grad_expert_up,
        grad_expert_down,
    )


def solution(mesh):
    cut = Mesh(mesh.devices.reshape(-1, 2, 2, 2, mesh.shape["seq"] // 2), ALL)
    rows = P(ALL, None)
    line = P(ALL)
    cols = P(None, ALL)
    expert = P(SEQ, OUTER + ("d",), None)
    return jax.shard_map(
        body,
        mesh=cut,
        in_specs=(rows, rows, rows, line, line, rows, rows, rows, line, line, rows, rows, cols)
        + (expert,) * 3,
        out_specs=(rows, P(), rows, rows, rows, line, line, rows, rows, cols) + (expert,) * 3,
        check_vma=False,
    )
```
